32 devices in a mesh: tgt: 8 (over z, y), mem: 4 (over x, core).
Axes of the slice: x: 2, y: 2, z: 4, core: 2. Of those that a mesh axis runs over, the one named last changes fastest.
Arguments:
- target: bfloat16 [64, 189, 1472], P(('tgt', 'mem')), may hold values from -6 to 6
- memory: bfloat16 [64, 1024, 1472], P('tgt', 'mem'), may hold values from -6 to 6
- lengths: int32 [64], P('tgt'), may hold values from 200 to 1024, as said below
- gate_bias: float32 [64, 1024], P('tgt', 'mem'), may hold values from -3 to 0
- out_grad: bfloat16 [64, 189, 1472], P(('tgt', 'mem')), may hold values from -6 to 6
- gain_self: bfloat16 [1472], replicated, may hold values from 0.5 to 1.5
- gain_cross: bfloat16 [1472], replicated, may hold values from 0.5 to 1.5
- gain_ffn: bfloat16 [1472], replicated, may hold values from 0.5 to 1.5
- rel_table: float32 [32, 6], replicated, may hold values from -4 to 4
- self_q: bfloat16 [1472, 384], P('tgt'), may hold values from -0.0390625 to 0.0390625
- self_k: bfloat16 [1472, 384], P('tgt'), may hold values from -0.15625 to 0.15625
- self_v: bfloat16 [1472, 384], P('tgt'), may hold values from -0.15625 to 0.15625
- self_o: bfloat16 [384, 1472], P('tgt'), may hold values from -1.75 to 1.75
- cross_q: bfloat16 [1472, 384], P('tgt'), may hold values from -0.0390625 to 0.0390625
- cross_k: bfloat16 [1472, 384], P('tgt'), may hold values from -0.15625 to 0.15625
- cross_v: bfloat16 [1472, 384], P('tgt'), may hold values from -0.15625 to 0.15625
- cross_o: bfloat16 [384, 1472], P('tgt'), may hold values from -3.5 to 3.5
- ffn_gate: bfloat16 [1472, 3584], P('tgt'), may hold values from -0.15625 to 0.15625
- ffn_up: bfloat16 [1472, 3584], P('tgt'), may hold values from -0.15625 to 0.15625
- ffn_down: bfloat16 [3584, 1472], P('tgt'), may hold values from -0.09375 to 0.09375
Outputs:
- layer_out: bfloat16 [64, 189, 1472], P(('tgt', 'mem'))
- target_grad: bfloat16 [64, 189, 1472], P(('tgt', 'mem'))
- memory_grad: bfloat16 [64, 1024, 1472], P('tgt', 'mem')
- gain_self_grad: float32 [1472], replicated
- gain_cross_grad: float32 [1472], replicated
- gain_ffn_grad: float32 [1472], replicated
- rel_table_grad: float32 [32, 6], replicated
- self_q_grad: float32 [1472, 384], P('tgt')
- self_k_grad: float32 [1472, 384], P('tgt')
- self_v_grad: float32 [1472, 384], P('tgt')
- self_o_grad: float32 [384, 1472], P('tgt')
- cross_q_grad: float32 [1472, 384], P('tgt')
- cross_k_grad: float32 [1472, 384], P('tgt')
- cross_v_grad: float32 [1472, 384], P('tgt')
- cross_o_grad: float32 [384, 1472], P('tgt')
- ffn_gate_grad: float32 [1472, 3584], P('tgt')
- ffn_up_grad: float32 [1472, 3584], P('tgt')
- ffn_down_grad: float32 [3584, 1472], P('tgt')
The draws below stay inside these ranges and needn't reach their ends.
Inputs may be any that keep to these rules, and one draw needn't show every extreme that they name: `lengths`: each item's true encoder length; some item has exactly 1024.
All inputs are finite; a program needn't handle non-finite values.
Results may differ from the reference program's by a relative error of at most 0.025.
The reference program's roundings to bfloat16 on the way count: a program that leaves them out, or rounds other values in their place, can miss the bound.
Values may be sent and summed in bfloat16 or wider, within the bound.
A program may use at most 448 MiB of HBM per device.

```python
import jax
import jax.numpy as jnp
import numpy as np
from jax import lax

D = 1472
HEADS = 6
HEAD = 64
FF = 3584
BUCKETS = 32
MAX_DIST = 128
TGT_LEN = 189
MEM_LEN = 1024
MIN_LEN = 200
ITEMS = 64


def draw_lengths(key, part):
    first_key, second_key = jax.random.split(key)
    values = jax.random.randint(first_key, (ITEMS,), MIN_LEN, MEM_LEN + 1)
    longest = jax.random.randint(second_key, (), 0, ITEMS)
    return jnp.where(jnp.arange(ITEMS) == longest, MEM_LEN, values).astype(jnp.int32)


def block_levels(stream_key, extent, cuts, least, top_value):
    loudness, own = 1.0, jax.random.fold_in(stream_key, 6)
    for dim, blocks in cuts:
        steps = jnp.exp(jax.random.uniform(jax.random.fold_in(own, dim), (blocks,), jnp.float32, least / len(cuts), top_value / len(cuts)))
        loudness = loudness * jnp.repeat(steps, extent[dim] // blocks).reshape([-1 if axis == dim else 1 for axis in range(len(extent))])
    return loudness


def bell_draw(rng, dims, width, bound, pieces=(), held_as=jnp.bfloat16):
    loudness = block_levels(rng, dims, pieces, -0.22, 0.18) if pieces else 1.0
    values = jax.random.normal(rng, dims, jnp.float32) * width * loudness
    return jnp.minimum(jnp.maximum(values, -bound), bound).astype(held_as)


def setup_inputs(seed: int = 0) -> dict:
    seeds = jax.random.split(jax.random.key(seed), 21)
    return {
        "target": bell_draw(seeds[0], (ITEMS, TGT_LEN, D), 1.0, 6.0, ((0, 32),)),
        "memory": bell_draw(seeds[1], (ITEMS, MEM_LEN, D), 1.0, 6.0, ((0, 8), (1, 4))),
        "lengths": draw_lengths(jax.random.fold_in(seeds[20], 71), 0),
        "gate_bias": jnp.clip(-3.0 + 3.0 * jax.random.uniform(seeds[3], (ITEMS, MEM_LEN), jnp.float32) ** block_levels(seeds[3], (ITEMS, MEM_LEN), ((0, 8), (1, 4)), -0.2, 0.2), -3.0, 0.0),
        "out_grad": bell_draw(seeds[4], (ITEMS, TGT_LEN, D), 1.0, 6.0, ((0, 32),)),
        "gain_self": jnp.clip(1.0 + 0.1 * jax.random.normal(seeds[5], (D,), jnp.float32), 0.5, 1.5).astype(jnp.bfloat16),
        "gain_cross": jnp.clip(1.0 + 0.1 * jax.random.normal(seeds[6], (D,), jnp.float32), 0.5, 1.5).astype(jnp.bfloat16),
        "gain_ffn": jnp.clip(1.0 + 0.1 * jax.random.normal(seeds[7], (D,), jnp.float32), 0.5, 1.5).astype(jnp.bfloat16),
        "rel_table": bell_draw(seeds[8], (BUCKETS, HEADS), 1.0, 4.0, (), jnp.float32),
        "self_q": bell_draw(seeds[9], (D, HEADS * HEAD), (D * HEAD // 4) ** -0.5, 0.0390625, ((0, 8),)),
        "self_k": bell_draw(seeds[10], (D, HEADS * HEAD), D ** -0.5, 0.15625, ((0, 8),)),
        "self_v": bell_draw(seeds[11], (D, HEADS * HEAD), D ** -0.5, 0.15625, ((0, 8),)),
        "self_o": bell_draw(seeds[12], (HEADS * HEAD, D), (max(HEADS * HEAD // 32, 1)) ** -0.5, 1.75, ((0, 8),)),
        "cross_q": bell_draw(seeds[13], (D, HEADS * HEAD), (D * HEAD // 4) ** -0.5, 0.0390625, ((0, 8),)),
        "cross_k": bell_draw(seeds[14], (D, HEADS * HEAD), D ** -0.5, 0.15625, ((0, 8),)),
        "cross_v": bell_draw(seeds[15], (D, HEADS * HEAD), D ** -0.5, 0.15625, ((0, 8),)),
        "cross_o": bell_draw(seeds[16], (HEADS * HEAD, D), (max(HEADS * HEAD // 128, 1)) ** -0.5, 3.5, ((0, 8),)),
        "ffn_gate": bell_draw(seeds[17], (D, FF), D ** -0.5, 0.15625, ((0, 8),)),
        "ffn_up": bell_draw(seeds[18], (D, FF), D ** -0.5, 0.15625, ((0, 8),)),
        "ffn_down": bell_draw(seeds[19], (FF, D), FF ** -0.5, 0.09375, ((0, 8),)),
    }


EPS = 1e-06
NEG = -1e+30
HIGH = lax.Precision.HIGHEST

@jax.custom_vjp
def low(v):
    return lax.optimization_barrier(v.astype(jnp.bfloat16)).astype(jnp.float32)

@jax.custom_vjp
def low_back(v):
    return v

def low_keep(v):
    return (low(v), None)

def low_pass(kept, grad):
    return (grad,)

def back_keep(v):
    return (v, None)

def back_low(kept, grad):
    return (low(grad),)
low.defvjp(low_keep, low_pass)
low_back.defvjp(back_keep, back_low)

def lower_both(values):
    return low(low_back(values))

def bucket_onehot():
    places = np.arange(TGT_LEN)
    distance = np.maximum(places[:, None] - places[None, :], 0)
    exact_max = BUCKETS // 2
    scaled = np.log(np.maximum(distance, 1) / exact_max) / np.log(MAX_DIST / exact_max) * (BUCKETS - exact_max)
    far_bucket = np.minimum(exact_max + np.floor(np.maximum(scaled, 0.0)).astype(np.int64), BUCKETS - 1)
    bucket = np.where(distance < exact_max, distance, far_bucket)
    return (bucket.reshape(-1)[:, None] == np.arange(BUCKETS)[None, :]).astype(np.float32)

def rms_norm(inputs, gain_vec):
    scaled = lax.rsqrt(lax.optimization_barrier(jnp.mean(inputs * inputs, axis=-1, keepdims=True)) + EPS)
    return inputs * scaled * gain_vec

def project(inputs, weight):
    return jnp.einsum('nte,ef->ntf', inputs, weight, precision=HIGH)

def layer_forward(target, memory, lengths, gate_bias, params):
    gain_self, gain_cross, gain_ffn, rel_table, self_q, self_k, self_v, self_o, cross_q, cross_k, cross_v, cross_o, ffn_gate, ffn_up, ffn_down = params
    items_now = target.shape[0]
    normed = low(rms_norm(target, gain_self))
    queries = lower_both(project(normed, self_q)).reshape(items_now, TGT_LEN, HEADS, HEAD)
    keys_self = lower_both(project(normed, self_k)).reshape(items_now, TGT_LEN, HEADS, HEAD)
    values_self = lower_both(project(normed, self_v)).reshape(items_now, TGT_LEN, HEADS, HEAD)
    onehot = jnp.asarray(bucket_onehot())
    rel_bias = jnp.dot(onehot, rel_table, precision=HIGH).reshape(TGT_LEN, TGT_LEN, HEADS).transpose(2, 0, 1)
    causal = jnp.arange(TGT_LEN)[:, None] >= jnp.arange(TGT_LEN)[None, :]
    scores = low_back(jnp.einsum('nihc,njhc->nhij', queries, keys_self, precision=HIGH)) + rel_bias[None]
    scores = jnp.where(causal[None, None], scores, NEG)
    self_probs = low(jax.nn.softmax(scores, axis=-1))
    attended = lower_both(jnp.einsum('nhij,njhc->nihc', self_probs, values_self, precision=HIGH).reshape(items_now, TGT_LEN, HEADS * HEAD))
    after_self = target + low_back(project(attended, self_o))
    normed_cross = low(rms_norm(after_self, gain_cross))
    cross_queries = lower_both(project(normed_cross, cross_q)).reshape(items_now, TGT_LEN, HEADS, HEAD)
    mem_keys = lower_both(project(memory, cross_k)).reshape(items_now, MEM_LEN, HEADS, HEAD)
    mem_values = lower_both(project(memory, cross_v)).reshape(items_now, MEM_LEN, HEADS, HEAD)
    valid_pos = jnp.arange(MEM_LEN)[None, :] < lengths[:, None]
    cross_scores = low_back(jnp.einsum('nihc,njhc->nhij', cross_queries, mem_keys, precision=HIGH)) + gate_bias[:, None, None, :]
    cross_scores = jnp.where(valid_pos[:, None, None, :], cross_scores, NEG)
    cross_probs = low(jax.nn.softmax(cross_scores, axis=-1))
    cross_att = lower_both(jnp.einsum('nhij,njhc->nihc', cross_probs, mem_values, precision=HIGH).reshape(items_now, TGT_LEN, HEADS * HEAD))
    after_cross = after_self + low_back(project(cross_att, cross_o))
    normed_ffn = low(rms_norm(after_cross, gain_ffn))
    gate_pre = low_back(project(normed_ffn, ffn_gate))
    up_pre = low_back(project(normed_ffn, ffn_up))
    hidden = lower_both(jax.nn.gelu(gate_pre, approximate=True) * up_pre)
    return after_cross + low_back(project(hidden, ffn_down))

def reference(target, memory, lengths, gate_bias, out_grad, gain_self, gain_cross, gain_ffn, rel_table, self_q, self_k, self_v, self_o, cross_q, cross_k, cross_v, cross_o, ffn_gate, ffn_up, ffn_down):
    params = tuple((weight.astype(jnp.float32) for weight in (gain_self, gain_cross, gain_ffn, rel_table, self_q, self_k, self_v, self_o, cross_q, cross_k, cross_v, cross_o, ffn_gate, ffn_up, ffn_down)))
    group_count = ITEMS // 4

    def regroup(array):
        return array.reshape((group_count, 4) + array.shape[1:])
    blocks = (regroup(target.astype(jnp.float32)), regroup(memory.astype(jnp.float32)), regroup(lengths), regroup(gate_bias), regroup(out_grad.astype(jnp.float32)))

    def visit_block(totals, block):
        target_blk, memory_blk, length_blk, bias_blk, upstream_blk = block

        def forward(target_in, memory_in, weights):
            return layer_forward(target_in, memory_in, length_blk, bias_blk, weights)
        output, pullback = jax.vjp(forward, target_blk, memory_blk, params)
        target_back, memory_back, param_back = pullback(upstream_blk)
        totals = jax.tree.map(jnp.add, totals, param_back)
        return (totals, (output.astype(jnp.bfloat16), target_back.astype(jnp.bfloat16), memory_back.astype(jnp.bfloat16)))
    initial = tuple((jnp.zeros_like(weight) for weight in params))
    totals, (outputs, target_backs, memory_backs) = lax.scan(visit_block, initial, blocks)
    layer_out = outputs.reshape(ITEMS, TGT_LEN, D)
    target_grad = target_backs.reshape(ITEMS, TGT_LEN, D)
    memory_grad = memory_backs.reshape(ITEMS, MEM_LEN, D)
    return (layer_out, target_grad, memory_grad, totals[0], totals[1], totals[2], totals[3], totals[4], totals[5], totals[6], totals[7], totals[8], totals[9], totals[10], totals[11], totals[12], totals[13], totals[14])
```

```python
import functools

import jax
import jax.numpy as jnp
import numpy as np
from jax import lax
from jax.experimental import pallas as pl
from jax.experimental.pallas import tpu as pltpu
from jax.sharding import PartitionSpec as P

HEADS = 6
HEAD = 64
BUCKETS = 32
MAX_DIST = 128
ROWS = 192
SPAN = 256
STATS = 128

EPS = 1e-06
NEG = -1e30
HIGH = lax.Precision.HIGHEST
BF = jnp.bfloat16
F32 = jnp.float32
MESH = pl.DeviceIdType.MESH
NT = (((1,), (1,)), ((), ()))
TN = (((0,), (0,)), ((), ()))
VMEM_SPEC = pl.BlockSpec(memory_space=pltpu.VMEM)
ANY_SPEC = pl.BlockSpec(memory_space=pl.ANY)
VMEM_CAP = 56 * 1024 * 1024


def distance_onehot():
    distance = (SPAN - np.arange(SPAN)) % SPAN
    exact_max = BUCKETS // 2
    scaled = (
        np.log(np.maximum(distance, 1) / exact_max)
        / np.log(MAX_DIST / exact_max)
        * (BUCKETS - exact_max)
    )
    far = np.minimum(
        exact_max + np.floor(np.maximum(scaled, 0.0)).astype(np.int64), BUCKETS - 1
    )
    bucket = np.where(distance < exact_max, distance, far)
    return (np.arange(BUCKETS)[:, None] == bucket[None, :]).astype(np.float32)


def dot(left, right):
    return jnp.dot(left, right, preferred_element_type=F32)


def dot_nt(left, right):
    return lax.dot_general(left, right, NT, preferred_element_type=F32)


def dot_tn(left, right):
    return lax.dot_general(left, right, TN, preferred_element_type=F32)


def rms_scale(inputs):
    return lax.rsqrt(jnp.mean(inputs * inputs, axis=-1, keepdims=True) + EPS)


def rms_back(inputs, gain, upstream):
    scale = rms_scale(inputs)
    gu = gain * upstream
    inner = jnp.mean(inputs * gu, axis=-1, keepdims=True)
    dx = scale * gu - inputs * (scale * scale * scale * inner)
    return dx, jnp.sum(upstream * inputs * scale, axis=0)


def half_masks():
    lane = lax.broadcasted_iota(jnp.int32, (1, 2 * HEAD), 1)
    low = (lane < HEAD).astype(BF)
    return low, 1 - low


def pair(index):
    return slice(index * 2 * HEAD, (index + 1) * 2 * HEAD)


def head_bias(base_ref, head):
    row = jnp.broadcast_to(base_ref[head : head + 1, :], (ROWS, SPAN))
    return pltpu.roll(row, 0, 1, stride=1, stride_axis=0)


def causal_mask():
    rows = lax.broadcasted_iota(jnp.int32, (ROWS, SPAN), 0)
    cols = lax.broadcasted_iota(jnp.int32, (ROWS, SPAN), 1)
    return cols <= rows


def self_fwd_kernel(items, qkv_ref, base_ref, att_ref, k_pad, v_pad):
    inner = HEADS * HEAD
    k_pad[...] = jnp.zeros_like(k_pad)
    v_pad[...] = jnp.zeros_like(v_pad)
    for item in range(items):
        k_pad[item, :ROWS, :] = qkv_ref[item, :, inner : 2 * inner]
        v_pad[item, :ROWS, :] = qkv_ref[item, :, 2 * inner :]
    causal = causal_mask()
    masks = half_masks()
    for index in range(HEADS // 2):
        sums = [None] * items
        for half in range(2):
            bias = head_bias(base_ref, 2 * index + half)
            for item in range(items):
                query = qkv_ref[item, :, pair(index)] * masks[half]
                scores = dot_nt(query, k_pad[item, :, pair(index)]) + bias
                scores = jnp.where(causal, scores, NEG)
                top = jnp.max(scores, axis=-1, keepdims=True)
                probs = jnp.exp(scores - top)
                probs = probs * (1.0 / jnp.sum(probs, axis=-1, keepdims=True))
                part = dot(probs.astype(BF), v_pad[item, :, pair(index)] * masks[half])
                sums[item] = part if half == 0 else sums[item] + part
        for item in range(items):
            att_ref[item, :, pair(index)] = sums[item].astype(BF)


def self_fwd(qkv, base):
    items = qkv.shape[0]
    inner = HEADS * HEAD
    return pl.pallas_call(
        functools.partial(self_fwd_kernel, items),
        out_shape=jax.ShapeDtypeStruct((items, ROWS, inner), BF),
        in_specs=[VMEM_SPEC] * 2,
        out_specs=VMEM_SPEC,
        scratch_shapes=[pltpu.VMEM((items, SPAN, inner), BF)] * 2,
        compiler_params=pltpu.CompilerParams(vmem_limit_bytes=VMEM_CAP),
        cost_estimate=pl.CostEstimate(
            flops=items * HEADS * ROWS * SPAN * 128 * 4,
            bytes_accessed=items * ROWS * inner * 8,
            transcendentals=items * HEADS * ROWS * SPAN,
        ),
        name="self_fwd",
    )(qkv, base)


def diagonal_sums(values):
    total = values[:8]
    for start in range(8, ROWS, 8):
        total = total + pltpu.roll(values[start : start + 8], SPAN - start, 1)
    row = lax.broadcasted_iota(jnp.int32, (8, SPAN), 0)
    for bit in (1, 2, 4):
        total = jnp.where((row & bit) > 0, pltpu.roll(total, SPAN - bit, 1), total)
    return jnp.sum(total, axis=0, keepdims=True)


def self_bwd_kernel(items, qkv_ref, datt_ref, base_ref, dqkv_ref, diag_ref, k_pad, v_pad):
    inner = HEADS * HEAD
    k_pad[...] = jnp.zeros_like(k_pad)
    v_pad[...] = jnp.zeros_like(v_pad)
    diag_ref[...] = jnp.zeros_like(diag_ref)
    for item in range(items):
        k_pad[item, :ROWS, :] = qkv_ref[item, :, inner : 2 * inner]
        v_pad[item, :ROWS, :] = qkv_ref[item, :, 2 * inner :]
    causal = causal_mask()
    masks = half_masks()
    for index in range(HEADS // 2):
        dq = [None] * items
        dk = [None] * items
        dv = [None] * items
        for half in range(2):
            head = 2 * index + half
            bias = head_bias(base_ref, head)
            ds_sum = None
            for item in range(items):
                query = qkv_ref[item, :, pair(index)] * masks[half]
                upstream = datt_ref[item, :, pair(index)] * masks[half]
                keys = k_pad[item, :, pair(index)]
                scores = dot_nt(query, keys) + bias
                scores = jnp.where(causal, scores, NEG)
                top = jnp.max(scores, axis=-1, keepdims=True)
                probs = jnp.exp(scores - top)
                probs = probs * (1.0 / jnp.sum(probs, axis=-1, keepdims=True))
                dprobs = dot_nt(upstream, v_pad[item, :, pair(index)])
                delta = jnp.sum(probs * dprobs, axis=-1, keepdims=True)
                ds = probs * (dprobs - delta)
                ds_sum = ds if item == 0 else ds_sum + ds
                ds_low = ds.astype(BF)
                q_part = dot(ds_low, keys * masks[half])
                k_part = dot_tn(ds_low, query)[:ROWS]
                v_part = dot_tn(probs.astype(BF), upstream)[:ROWS]
                dq[item] = q_part if half == 0 else dq[item] + q_part
                dk[item] = k_part if half == 0 else dk[item] + k_part
                dv[item] = v_part if half == 0 else dv[item] + v_part
            diag_ref[head : head + 1, :] = diagonal_sums(ds_sum)
        for item in range(items):
            dqkv_ref[item, :, pair(index)] = dq[item].astype(BF)
            dqkv_ref[item, :, pair(index + 3)] = dk[item].astype(BF)
            dqkv_ref[item, :, pair(index + 6)] = dv[item].astype(BF)


def self_bwd(qkv, datt, base):
    items = qkv.shape[0]
    inner = HEADS * HEAD
    return pl.pallas_call(
        functools.partial(self_bwd_kernel, items),
        out_shape=(
            jax.ShapeDtypeStruct((items, ROWS, 3 * inner), BF),
            jax.ShapeDtypeStruct((8, SPAN), F32),
        ),
        in_specs=[VMEM_SPEC] * 3,
        out_specs=(VMEM_SPEC, VMEM_SPEC),
        scratch_shapes=[pltpu.VMEM((items, SPAN, inner), BF)] * 2,
        compiler_params=pltpu.CompilerParams(vmem_limit_bytes=VMEM_CAP),
        cost_estimate=pl.CostEstimate(
            flops=items * HEADS * ROWS * SPAN * 128 * 10,
            bytes_accessed=items * ROWS * inner * 14,
            transcendentals=items * HEADS * ROWS * SPAN,
        ),
        name="self_bwd",
    )(qkv, datt, base)


def greet(axis, offsets):
    me = lax.axis_index(axis)
    barrier = pltpu.get_barrier_semaphore()
    for offset in offsets:
        pl.semaphore_signal(
            barrier, inc=1, device_id={axis: jnp.bitwise_xor(me, offset)}, device_id_type=MESH
        )
    pl.semaphore_wait(barrier, len(offsets))


def send(src, dst, send_sem, recv_sem, offset):
    me = lax.axis_index("mem")
    return pltpu.make_async_remote_copy(
        src_ref=src,
        dst_ref=dst,
        send_sem=send_sem,
        recv_sem=recv_sem,
        device_id={"mem": jnp.bitwise_xor(me, offset)},
        device_id_type=MESH,
    )


def column(stats, index):
    return stats[:, index : index + 1]


def spread(stats, index, masks):
    return jnp.where(masks, column(stats, 2 * index), column(stats, 2 * index + 1))


def cross_fwd_kernel(
    items, q_ref, k_ref, v_ref, bias_ref, all_ref, att_ref, lse_ref,
    out_o, out_s, in_o, in_s, q_send, q_recv, o_send, o_recv, s_send, s_recv,
):
    me = lax.axis_index("mem")
    greet("mem", (1, 2, 3))
    q_to_core = send(q_ref, all_ref.at[1], q_send.at[0], q_recv.at[0], 1)
    q_to_far = send(q_ref, all_ref.at[2], q_send.at[1], q_recv.at[1], 2)
    q_relay = send(all_ref.at[2], all_ref.at[3], q_send.at[2], q_recv.at[2], 1)
    q_to_far.start()
    q_to_core.start()
    all_ref[0] = q_ref[...]
    low, high = half_masks()
    lane = lax.broadcasted_iota(jnp.int32, (1, STATS), 1)
    is_low = lax.broadcasted_iota(jnp.int32, (1, 2 * HEAD), 1) < HEAD
    copies = []
    for slot in (0, 2, 3, 1):
        if slot == 2:
            q_to_far.wait_recv()
            q_relay.start()
        if slot == 3:
            q_relay.wait_recv()
        if slot == 1:
            q_to_core.wait_recv()
        owner = jnp.bitwise_xor(me, slot)
        for item in range(items):
            place = owner * items + item
            bias = bias_ref[place]
            stats = jnp.zeros((ROWS, STATS), F32)
            for index in range(HEADS // 2):
                both = all_ref[slot, item, :, pair(index)]
                keys = k_ref[place, :, pair(index)]
                values = v_ref[place, :, pair(index)]
                total = None
                scales = []
                for half, mask in ((0, low), (1, high)):
                    scores = dot_nt(both * mask, keys) + bias
                    top = jnp.max(scores, axis=-1, keepdims=True)
                    probs = jnp.exp(scores - top)
                    amount = jnp.sum(probs, axis=-1, keepdims=True)
                    part = dot(probs.astype(BF), values * mask)
                    total = part if half == 0 else total + part
                    scales.append(1.0 / amount)
                    stats = jnp.where(
                        lane == 2 * index + half, top + jnp.log(amount), stats
                    )
                total = total * jnp.where(is_low, scales[0], scales[1])
                out_o[slot, item, :, pair(index)] = total.astype(BF)
            out_s[slot, item] = stats
        if slot:
            copies.append(send(out_o.at[slot], in_o.at[slot], o_send.at[slot], o_recv.at[slot], slot))
            copies.append(send(out_s.at[slot], in_s.at[slot], s_send.at[slot], s_recv.at[slot], slot))
            copies[-2].start()
            copies[-1].start()
    q_to_core.wait_send()
    q_to_far.wait_send()
    q_relay.wait_send()
    for copy in copies:
        copy.wait()
    for item in range(items):
        stats = [out_s[0, item]] + [in_s[slot, item] for slot in (1, 2, 3)]
        top = jnp.maximum(jnp.maximum(stats[0], stats[1]), jnp.maximum(stats[2], stats[3]))
        shares = [jnp.exp(part - top) for part in stats]
        amount = shares[0] + shares[1] + shares[2] + shares[3]
        lse_ref[item] = top + jnp.log(amount)
        scale = 1.0 / amount
        shares = [part * scale for part in shares]
        for index in range(HEADS // 2):
            total = out_o[0, item, :, pair(index)].astype(F32) * spread(shares[0], index, is_low)
            for slot in (1, 2, 3):
                total += in_o[slot, item, :, pair(index)].astype(F32) * spread(
                    shares[slot], index, is_low
                )
            att_ref[item, :, pair(index)] = total.astype(BF)


def cross_fwd(queries, keys, values, bias):
    items = queries.shape[0]
    inner = HEADS * HEAD
    block = (4, items, ROWS, inner)
    stat_block = (4, items, ROWS, STATS)
    flops = 4 * items * HEADS * ROWS * SPAN * 128 * 4
    return pl.pallas_call(
        functools.partial(cross_fwd_kernel, items),
        out_shape=(
            jax.ShapeDtypeStruct(block, BF),
            jax.ShapeDtypeStruct((items, ROWS, inner), BF),
            jax.ShapeDtypeStruct((items, ROWS, STATS), F32),
        ),
        in_specs=[VMEM_SPEC] * 4,
        out_specs=(VMEM_SPEC,) * 3,
        scratch_shapes=[
            pltpu.VMEM(block, BF),
            pltpu.VMEM(stat_block, F32),
            pltpu.VMEM(block, BF),
            pltpu.VMEM(stat_block, F32),
            pltpu.SemaphoreType.DMA((3,)),
            pltpu.SemaphoreType.DMA((3,)),
            pltpu.SemaphoreType.DMA((4,)),
            pltpu.SemaphoreType.DMA((4,)),
            pltpu.SemaphoreType.DMA((4,)),
            pltpu.SemaphoreType.DMA((4,)),
        ],
        compiler_params=pltpu.CompilerParams(
            collective_id=1, has_side_effects=True, vmem_limit_bytes=VMEM_CAP
        ),
        cost_estimate=pl.CostEstimate(
            flops=flops, bytes_accessed=8 * 1024 * 1024, transcendentals=flops // 512
        ),
        name="cross_fwd",
    )(queries, keys, values, bias)


def cross_bwd_kernel(
    items, all_ref, back_ref, stat_ref, k_ref, v_ref, bias_ref, dk_ref, dv_ref, dq_ref,
    all_b, all_s, out_q, in_q, b_send, b_recv, s_send, s_recv, q_send, q_recv,
):
    me = lax.axis_index("mem")
    greet("mem", (1, 2, 3))
    moves = []
    for offset, slot, source in ((2, 2, None), (1, 1, None), (1, 3, 2)):
        number = len(moves)
        moves.append(
            (
                send(back_ref if source is None else all_b.at[source], all_b.at[slot],
                     b_send.at[number], b_recv.at[number], offset),
                send(stat_ref if source is None else all_s.at[source], all_s.at[slot],
                     s_send.at[number], s_recv.at[number], offset),
            )
        )
    for move in moves[:2]:
        for copy in move:
            copy.start()
    low, high = half_masks()
    copies = []
    for slot in (0, 2, 3, 1):
        if slot == 2:
            for copy in moves[0]:
                copy.wait_recv()
            for copy in moves[2]:
                copy.start()
        if slot == 3:
            for copy in moves[2]:
                copy.wait_recv()
        if slot == 1:
            for copy in moves[1]:
                copy.wait_recv()
        owner = jnp.bitwise_xor(me, slot)
        for item in range(items):
            place = owner * items + item
            bias = bias_ref[place]
            stats = stat_ref[item] if slot == 0 else all_s[slot, item]
            for index in range(HEADS // 2):
                both = all_ref[slot, item, :, pair(index)]
                if slot == 0:
                    upstream = back_ref[item, :, pair(index)]
                else:
                    upstream = all_b[slot, item, :, pair(index)]
                keys = k_ref[place, :, pair(index)]
                values = v_ref[place, :, pair(index)]
                dq = dk = dv = None
                for half, mask in ((0, low), (1, high)):
                    head = 2 * index + half
                    query = both * mask
                    back = upstream * mask
                    scores = dot_nt(query, keys) + bias
                    probs = jnp.exp(scores - column(stats, head))
                    dprobs = dot_nt(back, values)
                    ds = (probs * (dprobs - column(stats, 8 + head))).astype(BF)
                    q_part = dot(ds, keys * mask)
                    k_part = dot_tn(ds, query)
                    v_part = dot_tn(probs.astype(BF), back)
                    dq = q_part if half == 0 else dq + q_part
                    dk = k_part if half == 0 else dk + k_part
                    dv = v_part if half == 0 else dv + v_part
                out_q[slot, item, :, pair(index)] = dq.astype(BF)
                dk_ref[place, :, pair(index)] = dk.astype(BF)
                dv_ref[place, :, pair(index)] = dv.astype(BF)
        if slot:
            copies.append(send(out_q.at[slot], in_q.at[slot], q_send.at[slot], q_recv.at[slot], slot))
            copies[-1].start()
    for move in moves:
        for copy in move:
            copy.wait_send()
    for copy in copies:
        copy.wait()
    for item in range(items):
        for index in range(HEADS // 2):
            total = out_q[0, item, :, pair(index)].astype(F32)
            for slot in (1, 2, 3):
                total += in_q[slot, item, :, pair(index)].astype(F32)
            dq_ref[item, :, pair(index)] = total.astype(BF)


def cross_bwd(all_queries, back, stats, keys, values, bias):
    items = back.shape[0]
    inner = HEADS * HEAD
    block = (4, items, ROWS, inner)
    flops = 4 * items * HEADS * ROWS * SPAN * 128 * 10
    return pl.pallas_call(
        functools.partial(cross_bwd_kernel, items),
        out_shape=(
            jax.ShapeDtypeStruct(keys.shape, BF),
            jax.ShapeDtypeStruct(keys.shape, BF),
            jax.ShapeDtypeStruct((items, ROWS, inner), BF),
        ),
        in_specs=[VMEM_SPEC] * 6,
        out_specs=(VMEM_SPEC,) * 3,
        scratch_shapes=[
            pltpu.VMEM(block, BF),
            pltpu.VMEM((4, items, ROWS, STATS), F32),
            pltpu.VMEM(block, BF),
            pltpu.VMEM(block, BF),
            pltpu.SemaphoreType.DMA((3,)),
            pltpu.SemaphoreType.DMA((3,)),
            pltpu.SemaphoreType.DMA((3,)),
            pltpu.SemaphoreType.DMA((3,)),
            pltpu.SemaphoreType.DMA((4,)),
            pltpu.SemaphoreType.DMA((4,)),
        ],
        compiler_params=pltpu.CompilerParams(
            collective_id=2, has_side_effects=True, vmem_limit_bytes=VMEM_CAP
        ),
        cost_estimate=pl.CostEstimate(
            flops=flops, bytes_accessed=12 * 1024 * 1024, transcendentals=flops // 1280
        ),
        name="cross_bwd",
    )(all_queries, back, stats, keys, values, bias)


def over_mem(value, offset):
    return lax.ppermute(value, "mem", [(i, i ^ offset) for i in range(4)])


def gather_mem(value):
    far = over_mem(value, 2)
    near = over_mem(value, 1)
    return value, near, far, over_mem(far, 1)


def owner_sum(own, near, far, far_near):
    far = (far + over_mem(far_near.astype(BF), 1).astype(F32)).astype(BF)
    total = own + over_mem(near.astype(BF), 1).astype(F32)
    return total + over_mem(far, 2).astype(F32)


def gather_tgt(shard):
    return lax.all_gather(shard, "tgt", axis=0, tiled=True)


def scatter_tgt(partial):
    return lax.psum_scatter(partial, "tgt", scatter_dimension=0, tiled=True)


def on_device(
    target, memory, lengths, gate_bias, out_grad, gain_self, gain_cross, gain_ffn, rel_table,
    self_q, self_k, self_v, self_o, cross_q, cross_k, cross_v, cross_o, ffn_gate, ffn_up, ffn_down,
):
    groups = lax.axis_size("mem")
    tgts = lax.axis_size("tgt")
    mem_index = lax.axis_index("mem")
    items, seq, model = target.shape
    all_items, positions_dev, _ = memory.shape
    inner = HEADS * HEAD
    tokens = items * ROWS
    shard_in = ffn_gate.shape[0]
    hidden_shard = ffn_down.shape[0]
    piece = hidden_shard // groups
    quarter = tgts * piece

    def padded(value):
        return jnp.pad(value, ((0, 0), (0, ROWS - seq), (0, 0))).reshape(tokens, model)

    def trimmed(value):
        return value.reshape(items, ROWS, model)[:, :seq]

    def my_columns(weight):
        parts = weight.reshape(shard_in, tgts, groups, piece)
        return lax.dynamic_index_in_dim(parts, mem_index, 2, keepdims=False).reshape(
            shard_in, quarter
        )

    def whole_columns(parts):
        return (
            parts.reshape(groups, shard_in, tgts, piece)
            .transpose(1, 2, 0, 3)
            .reshape(shard_in, tgts * hidden_shard)
            .astype(F32)
        )

    norm_self = gain_self.astype(F32)
    norm_cross = gain_cross.astype(F32)
    norm_ffn = gain_ffn.astype(F32)
    onehot = jnp.asarray(distance_onehot())
    base = jnp.pad(
        lax.dot_general(rel_table, onehot, TN, precision=HIGH), ((0, 2), (0, 0))
    )
    positions = mem_index * positions_dev + jnp.arange(positions_dev)
    bias = jnp.where(positions[None, :] < lengths[:, None], gate_bias, NEG)[:, None, :]

    attn = gather_tgt(
        jnp.concatenate([self_q, self_k, self_v, cross_q, cross_k, cross_v], axis=1)
    )
    self_w = attn[:, : 3 * inner]
    cross_q_w = attn[:, 3 * inner : 4 * inner]
    cross_kv_w = attn[:, 4 * inner :]
    self_o_w = gather_tgt(self_o)
    cross_o_w = gather_tgt(cross_o)
    gate_up = gather_tgt(jnp.concatenate([my_columns(ffn_gate), my_columns(ffn_up)], axis=1))
    down = gather_tgt(
        lax.dynamic_slice_in_dim(ffn_down, mem_index * piece, piece, axis=0)
    )

    inputs = padded(target).astype(F32)
    upstream_low = padded(out_grad)
    upstreams = gather_mem(upstream_low)
    mem_flat = memory.reshape(all_items * positions_dev, model)

    h1 = (inputs * rms_scale(inputs) * norm_self).astype(BF)
    qkv = dot(h1, self_w).astype(BF).reshape(items, ROWS, 3 * inner)
    att = self_fwd(qkv, base).reshape(tokens, inner)
    y1 = inputs + dot(att, self_o_w)
    h2 = (y1 * rms_scale(y1) * norm_cross).astype(BF)
    cq = dot(h2, cross_q_w).astype(BF).reshape(items, ROWS, inner)
    ckv = dot(mem_flat, cross_kv_w).astype(BF)
    ck = ckv[:, :inner].reshape(all_items, positions_dev, inner)
    cv = ckv[:, inner:].reshape(all_items, positions_dev, inner)
    all_queries, catt, lse = cross_fwd(cq, ck, cv, bias)
    catt = catt.reshape(tokens, inner)
    y2 = y1 + dot(catt, cross_o_w)
    h3 = (y2 * rms_scale(y2) * norm_ffn).astype(BF)
    h3s = gather_mem(h3)

    near_far = []
    for part in (0, 1):
        h3_two = jnp.concatenate(h3s[2 * part : 2 * part + 2], axis=0)
        up_two = jnp.concatenate(upstreams[2 * part : 2 * part + 2], axis=0)
        both = dot(h3_two, gate_up)
        gate_pre, up_pre = both[:, :quarter], both[:, quarter:]

        def gated(gate_in, up_in):
            return jax.nn.gelu(gate_in, approximate=True) * up_in

        gated_out, pull = jax.vjp(gated, gate_pre, up_pre)
        hidden = gated_out.astype(BF)
        hidden_back = dot_nt(up_two, down).astype(BF)
        gate_back, up_back = pull(hidden_back.astype(F32))
        two_back = jnp.concatenate([gate_back.astype(BF), up_back.astype(BF)], axis=1)
        h3_back = dot_nt(two_back, gate_up)
        out_part = dot(hidden, down)
        near_far.append((h3_two, up_two, hidden, two_back, h3_back, out_part))
    near, far = near_far
    h3_back = owner_sum(near[4][:tokens], near[4][tokens:], far[4][:tokens], far[4][tokens:])
    out_sum = owner_sum(near[5][:tokens], near[5][tokens:], far[5][:tokens], far[5][tokens:])
    layer_out = trimmed((y2 + out_sum).astype(BF))

    grad_gate_up = (dot_tn(near[0], near[3]) + dot_tn(far[0], far[3])).astype(BF)
    grad_down = (dot_tn(near[2], near[1]) + dot_tn(far[2], far[1])).astype(BF)
    grad_gate_up = scatter_tgt(grad_gate_up)
    grad_down = scatter_tgt(grad_down)
    grad_gate_up = lax.all_gather(grad_gate_up, "mem", axis=0)
    grad_down = lax.all_gather(grad_down, "mem", axis=0, tiled=True).astype(F32)
    grad_gate = whole_columns(grad_gate_up[:, :, :quarter])
    grad_up = whole_columns(grad_gate_up[:, :, quarter:])

    dx, grad_norm_ffn = rms_back(y2, norm_ffn, h3_back)
    dy2 = upstream_low.astype(F32) + dx
    e2 = dy2.astype(BF)
    grad_cross_o = dot_tn(catt, e2)
    dcatt = dot_nt(e2, cross_o_w).astype(BF)
    delta = jnp.sum(
        (dcatt.astype(F32) * catt.astype(F32)).reshape(tokens, HEADS, HEAD), axis=-1
    ).reshape(items, ROWS, HEADS)
    stats = jnp.concatenate(
        [lse[:, :, :8], delta, jnp.zeros((items, ROWS, STATS - 8 - HEADS), F32)], axis=-1
    )
    dck, dcv, dcq = cross_bwd(
        all_queries, dcatt.reshape(items, ROWS, inner), stats, ck, cv, bias
    )
    dckv = jnp.concatenate([dck, dcv], axis=-1).reshape(all_items * positions_dev, 2 * inner)
    dcq = dcq.reshape(tokens, inner)
    grad_cross_kv = dot_tn(mem_flat, dckv)
    memory_grad = dot_nt(dckv, cross_kv_w).astype(BF).reshape(memory.shape)
    grad_cross_q = dot_tn(h2, dcq)
    dx, grad_norm_cross = rms_back(y1, norm_cross, dot_nt(dcq, cross_q_w))
    dy1 = dy2 + dx
    e1 = dy1.astype(BF)
    grad_self_o = dot_tn(att, e1)
    datt = dot_nt(e1, self_o_w).astype(BF).reshape(items, ROWS, inner)
    dqkv, diag = self_bwd(qkv, datt, base)
    dqkv = dqkv.reshape(tokens, 3 * inner)
    grad_self = dot_tn(h1, dqkv)
    dx, grad_norm_self = rms_back(inputs, norm_self, dot_nt(dqkv, self_w))
    target_grad = trimmed((dy1 + dx).astype(BF))
    table = lax.dot_general(
        onehot, diag[:HEADS], NT, precision=HIGH
    )

    wide = jnp.concatenate([grad_self, grad_cross_q, grad_cross_kv], axis=1).astype(BF)
    wide = scatter_tgt(wide)
    wide = lax.psum(wide.astype(F32), "mem")
    outs = scatter_tgt(
        jnp.concatenate([grad_self_o.astype(BF).reshape(tgts, -1, model),
                         grad_cross_o.astype(BF).reshape(tgts, -1, model)], axis=1)
        .reshape(-1, model)
    )
    outs = lax.psum(outs.astype(F32), "mem")
    rows = outs.shape[0] // 2
    small = lax.psum((grad_norm_self, grad_norm_cross, grad_norm_ffn, table), ("tgt", "mem"))
    columns = [wide[:, i * inner : (i + 1) * inner] for i in range(6)]
    return (
        layer_out,
        target_grad,
        memory_grad,
        *small,
        columns[0],
        columns[1],
        columns[2],
        outs[:rows],
        columns[3],
        columns[4],
        columns[5],
        outs[rows:],
        grad_gate,
        grad_up,
        grad_down,
    )


def solution(mesh):
    owned = P(("tgt", "mem"), None, None)
    held = P("tgt", "mem", None)
    rows = P("tgt", None)
    return jax.shard_map(
        on_device,
        mesh=mesh,
        in_specs=(owned, held, P("tgt"), P("tgt", "mem"), owned, P(), P(), P(), P()) + (rows,) * 11,
        out_specs=(owned, owned, held, P(), P(), P(), P()) + (rows,) * 11,
        check_vma=False,
    )
```

```python
import functools

import jax
import jax.numpy as jnp
import numpy as np
from jax import lax
from jax.experimental import pallas as pl
from jax.experimental.pallas import tpu as pltpu
from jax.sharding import PartitionSpec as P

HEADS = 6
HEAD = 64
BUCKETS = 32
MAX_DIST = 128
ROWS = 192
SPAN = 256
STATS = 128

EPS = 1e-06
NEG = -1e30
HIGH = lax.Precision.HIGHEST
BF = jnp.bfloat16
F32 = jnp.float32
MESH = pl.DeviceIdType.MESH
NT = (((1,), (1,)), ((), ()))
TN = (((0,), (0,)), ((), ()))
VMEM_SPEC = pl.BlockSpec(memory_space=pltpu.VMEM)
ANY_SPEC = pl.BlockSpec(memory_space=pl.ANY)
VMEM_CAP = 56 * 1024 * 1024
FFN_CAP = 62 * 1024 * 1024


def distance_onehot():
    distance = (SPAN - np.arange(SPAN)) % SPAN
    exact_max = BUCKETS // 2
    scaled = (
        np.log(np.maximum(distance, 1) / exact_max)
        / np.log(MAX_DIST / exact_max)
        * (BUCKETS - exact_max)
    )
    far = np.minimum(
        exact_max + np.floor(np.maximum(scaled, 0.0)).astype(np.int64), BUCKETS - 1
    )
    bucket = np.where(distance < exact_max, distance, far)
    return (np.arange(BUCKETS)[:, None] == bucket[None, :]).astype(np.float32)


def dot(left, right):
    return jnp.dot(left, right, preferred_element_type=F32)


def dot_nt(left, right):
    return lax.dot_general(left, right, NT, preferred_element_type=F32)


def dot_tn(left, right):
    return lax.dot_general(left, right, TN, preferred_element_type=F32)


def rms_scale(inputs):
    return lax.rsqrt(jnp.mean(inputs * inputs, axis=-1, keepdims=True) + EPS)


def rms_back(inputs, gain, upstream):
    scale = rms_scale(inputs)
    gu = gain * upstream
    inner = jnp.mean(inputs * gu, axis=-1, keepdims=True)
    dx = scale * gu - inputs * (scale * scale * scale * inner)
    return dx, jnp.sum(upstream * inputs * scale, axis=0)


def half_masks():
    lane = lax.broadcasted_iota(jnp.int32, (1, 2 * HEAD), 1)
    low = (lane < HEAD).astype(BF)
    return low, 1 - low


def pair(index):
    return slice(index * 2 * HEAD, (index + 1) * 2 * HEAD)


def head_bias(base_ref, head):
    row = jnp.broadcast_to(base_ref[head : head + 1, :], (ROWS, SPAN))
    return pltpu.roll(row, 0, 1, stride=1, stride_axis=0)


def causal_mask():
    rows = lax.broadcasted_iota(jnp.int32, (ROWS, SPAN), 0)
    cols = lax.broadcasted_iota(jnp.int32, (ROWS, SPAN), 1)
    return cols <= rows


def self_fwd_kernel(items, qkv_ref, base_ref, att_ref, k_pad, v_pad):
    inner = HEADS * HEAD
    k_pad[...] = jnp.zeros_like(k_pad)
    v_pad[...] = jnp.zeros_like(v_pad)
    for item in range(items):
        k_pad[item, :ROWS, :] = qkv_ref[item, :, inner : 2 * inner]
        v_pad[item, :ROWS, :] = qkv_ref[item, :, 2 * inner :]
    causal = causal_mask()
    masks = half_masks()
    for index in range(HEADS // 2):
        sums = [None] * items
        for half in range(2):
            bias = head_bias(base_ref, 2 * index + half)
            for item in range(items):
                query = qkv_ref[item, :, pair(index)] * masks[half]
                scores = dot_nt(query, k_pad[item, :, pair(index)]) + bias
                scores = jnp.where(causal, scores, NEG)
                top = jnp.max(scores, axis=-1, keepdims=True)
                probs = jnp.exp(scores - top)
                probs = probs * (1.0 / jnp.sum(probs, axis=-1, keepdims=True))
                part = dot(probs.astype(BF), v_pad[item, :, pair(index)] * masks[half])
                sums[item] = part if half == 0 else sums[item] + part
        for item in range(items):
            att_ref[item, :, pair(index)] = sums[item].astype(BF)


def self_fwd(qkv, base):
    items = qkv.shape[0]
    inner = HEADS * HEAD
    return pl.pallas_call(
        functools.partial(self_fwd_kernel, items),
        out_shape=jax.ShapeDtypeStruct((items, ROWS, inner), BF),
        in_specs=[VMEM_SPEC] * 2,
        out_specs=VMEM_SPEC,
        scratch_shapes=[pltpu.VMEM((items, SPAN, inner), BF)] * 2,
        compiler_params=pltpu.CompilerParams(vmem_limit_bytes=VMEM_CAP),
        cost_estimate=pl.CostEstimate(
            flops=items * HEADS * ROWS * SPAN * 128 * 4,
            bytes_accessed=items * ROWS * inner * 8,
            transcendentals=items * HEADS * ROWS * SPAN,
        ),
        name="self_fwd",
    )(qkv, base)


def diagonal_sums(values):
    total = values[:8]
    for start in range(8, ROWS, 8):
        total = total + pltpu.roll(values[start : start + 8], SPAN - start, 1)
    row = lax.broadcasted_iota(jnp.int32, (8, SPAN), 0)
    for bit in (1, 2, 4):
        total = jnp.where((row & bit) > 0, pltpu.roll(total, SPAN - bit, 1), total)
    return jnp.sum(total, axis=0, keepdims=True)


def self_bwd_kernel(items, qkv_ref, datt_ref, base_ref, dqkv_ref, diag_ref, k_pad, v_pad):
    inner = HEADS * HEAD
    k_pad[...] = jnp.zeros_like(k_pad)
    v_pad[...] = jnp.zeros_like(v_pad)
    diag_ref[...] = jnp.zeros_like(diag_ref)
    for item in range(items):
        k_pad[item, :ROWS, :] = qkv_ref[item, :, inner : 2 * inner]
        v_pad[item, :ROWS, :] = qkv_ref[item, :, 2 * inner :]
    causal = causal_mask()
    masks = half_masks()
    for index in range(HEADS // 2):
        dq = [None] * items
        dk = [None] * items
        dv = [None] * items
        for half in range(2):
            head = 2 * index + half
            bias = head_bias(base_ref, head)
            ds_sum = None
            for item in range(items):
                query = qkv_ref[item, :, pair(index)] * masks[half]
                upstream = datt_ref[item, :, pair(index)] * masks[half]
                keys = k_pad[item, :, pair(index)]
                scores = dot_nt(query, keys) + bias
                scores = jnp.where(causal, scores, NEG)
                top = jnp.max(scores, axis=-1, keepdims=True)
                probs = jnp.exp(scores - top)
                probs = probs * (1.0 / jnp.sum(probs, axis=-1, keepdims=True))
                dprobs = dot_nt(upstream, v_pad[item, :, pair(index)])
                delta = jnp.sum(probs * dprobs, axis=-1, keepdims=True)
                ds = probs * (dprobs - delta)
                ds_sum = ds if item == 0 else ds_sum + ds
                ds_low = ds.astype(BF)
                q_part = dot(ds_low, keys * masks[half])
                k_part = dot_tn(ds_low, query)[:ROWS]
                v_part = dot_tn(probs.astype(BF), upstream)[:ROWS]
                dq[item] = q_part if half == 0 else dq[item] + q_part
                dk[item] = k_part if half == 0 else dk[item] + k_part
                dv[item] = v_part if half == 0 else dv[item] + v_part
            diag_ref[head : head + 1, :] = diagonal_sums(ds_sum)
        for item in range(items):
            dqkv_ref[item, :, pair(index)] = dq[item].astype(BF)
            dqkv_ref[item, :, pair(index + 3)] = dk[item].astype(BF)
            dqkv_ref[item, :, pair(index + 6)] = dv[item].astype(BF)


def self_bwd(qkv, datt, base):
    items = qkv.shape[0]
    inner = HEADS * HEAD
    return pl.pallas_call(
        functools.partial(self_bwd_kernel, items),
        out_shape=(
            jax.ShapeDtypeStruct((items, ROWS, 3 * inner), BF),
            jax.ShapeDtypeStruct((8, SPAN), F32),
        ),
        in_specs=[VMEM_SPEC] * 3,
        out_specs=(VMEM_SPEC, VMEM_SPEC),
        scratch_shapes=[pltpu.VMEM((items, SPAN, inner), BF)] * 2,
        compiler_params=pltpu.CompilerParams(vmem_limit_bytes=VMEM_CAP),
        cost_estimate=pl.CostEstimate(
            flops=items * HEADS * ROWS * SPAN * 128 * 10,
            bytes_accessed=items * ROWS * inner * 14,
            transcendentals=items * HEADS * ROWS * SPAN,
        ),
        name="self_bwd",
    )(qkv, datt, base)


def greet(axis, offsets):
    me = lax.axis_index(axis)
    barrier = pltpu.get_barrier_semaphore()
    for offset in offsets:
        pl.semaphore_signal(
            barrier, inc=1, device_id={axis: jnp.bitwise_xor(me, offset)}, device_id_type=MESH
        )
    pl.semaphore_wait(barrier, len(offsets))


def send(src, dst, send_sem, recv_sem, offset):
    me = lax.axis_index("mem")
    return pltpu.make_async_remote_copy(
        src_ref=src,
        dst_ref=dst,
        send_sem=send_sem,
        recv_sem=recv_sem,
        device_id={"mem": jnp.bitwise_xor(me, offset)},
        device_id_type=MESH,
    )


def column(stats, index):
    return stats[:, index : index + 1]


def spread(stats, index, masks):
    return jnp.where(masks, column(stats, 2 * index), column(stats, 2 * index + 1))


def cross_fwd_kernel(
    items, q_ref, k_ref, v_ref, bias_ref, all_ref, att_ref, lse_ref,
    out_o, out_s, in_o, in_s, q_send, q_recv, o_send, o_recv, s_send, s_recv,
):
    me = lax.axis_index("mem")
    greet("mem", (1, 2, 3))
    q_to_core = send(q_ref, all_ref.at[1], q_send.at[0], q_recv.at[0], 1)
    q_to_far = send(q_ref, all_ref.at[2], q_send.at[1], q_recv.at[1], 2)
    q_relay = send(all_ref.at[2], all_ref.at[3], q_send.at[2], q_recv.at[2], 1)
    q_to_far.start()
    q_to_core.start()
    all_ref[0] = q_ref[...]
    low, high = half_masks()
    lane = lax.broadcasted_iota(jnp.int32, (1, STATS), 1)
    is_low = lax.broadcasted_iota(jnp.int32, (1, 2 * HEAD), 1) < HEAD
    copies = []
    for slot in (0, 2, 3, 1):
        if slot == 2:
            q_to_far.wait_recv()
            q_relay.start()
        if slot == 3:
            q_relay.wait_recv()
        if slot == 1:
            q_to_core.wait_recv()
        owner = jnp.bitwise_xor(me, slot)
        for item in range(items):
            place = owner * items + item
            bias = bias_ref[place]
            stats = jnp.zeros((ROWS, STATS), F32)
            for index in range(HEADS // 2):
                both = all_ref[slot, item, :, pair(index)]
                keys = k_ref[place, :, pair(index)]
                values = v_ref[place, :, pair(index)]
                total = None
                scales = []
                for half, mask in ((0, low), (1, high)):
                    scores = dot_nt(both * mask, keys) + bias
                    top = jnp.max(scores, axis=-1, keepdims=True)
                    probs = jnp.exp(scores - top)
                    amount = jnp.sum(probs, axis=-1, keepdims=True)
                    part = dot(probs.astype(BF), values * mask)
                    total = part if half == 0 else total + part
                    scales.append(1.0 / amount)
                    stats = jnp.where(
                        lane == 2 * index + half, top + jnp.log(amount), stats
                    )
                total = total * jnp.where(is_low, scales[0], scales[1])
                out_o[slot, item, :, pair(index)] = total.astype(BF)
            out_s[slot, item] = stats
        if slot:
            copies.append(send(out_o.at[slot], in_o.at[slot], o_send.at[slot], o_recv.at[slot], slot))
            copies.append(send(out_s.at[slot], in_s.at[slot], s_send.at[slot], s_recv.at[slot], slot))
            copies[-2].start()
            copies[-1].start()
    q_to_core.wait_send()
    q_to_far.wait_send()
    q_relay.wait_send()
    for copy in copies:
        copy.wait()
    for item in range(items):
        stats = [out_s[0, item]] + [in_s[slot, item] for slot in (1, 2, 3)]
        top = jnp.maximum(jnp.maximum(stats[0], stats[1]), jnp.maximum(stats[2], stats[3]))
        shares = [jnp.exp(part - top) for part in stats]
        amount = shares[0] + shares[1] + shares[2] + shares[3]
        lse_ref[item] = top + jnp.log(amount)
        scale = 1.0 / amount
        shares = [part * scale for part in shares]
        for index in range(HEADS // 2):
            total = out_o[0, item, :, pair(index)].astype(F32) * spread(shares[0], index, is_low)
            for slot in (1, 2, 3):
                total += in_o[slot, item, :, pair(index)].astype(F32) * spread(
                    shares[slot], index, is_low
                )
            att_ref[item, :, pair(index)] = total.astype(BF)


def cross_fwd(queries, keys, values, bias):
    items = queries.shape[0]
    inner = HEADS * HEAD
    block = (4, items, ROWS, inner)
    stat_block = (4, items, ROWS, STATS)
    flops = 4 * items * HEADS * ROWS * SPAN * 128 * 4
    return pl.pallas_call(
        functools.partial(cross_fwd_kernel, items),
        out_shape=(
            jax.ShapeDtypeStruct(block, BF),
            jax.ShapeDtypeStruct((items, ROWS, inner), BF),
            jax.ShapeDtypeStruct((items, ROWS, STATS), F32),
        ),
        in_specs=[VMEM_SPEC] * 4,
        out_specs=(VMEM_SPEC,) * 3,
        scratch_shapes=[
            pltpu.VMEM(block, BF),
            pltpu.VMEM(stat_block, F32),
            pltpu.VMEM(block, BF),
            pltpu.VMEM(stat_block, F32),
            pltpu.SemaphoreType.DMA((3,)),
            pltpu.SemaphoreType.DMA((3,)),
            pltpu.SemaphoreType.DMA((4,)),
            pltpu.SemaphoreType.DMA((4,)),
            pltpu.SemaphoreType.DMA((4,)),
            pltpu.SemaphoreType.DMA((4,)),
        ],
        compiler_params=pltpu.CompilerParams(
            collective_id=1, has_side_effects=True, vmem_limit_bytes=VMEM_CAP
        ),
        cost_estimate=pl.CostEstimate(
            flops=flops, bytes_accessed=8 * 1024 * 1024, transcendentals=flops // 512
        ),
        name="cross_fwd",
    )(queries, keys, values, bias)


def cross_bwd_kernel(
    items, all_ref, back_ref, stat_ref, k_ref, v_ref, bias_ref, dk_ref, dv_ref, dq_ref,
    all_b, all_s, out_q, in_q, b_send, b_recv, s_send, s_recv, q_send, q_recv,
):
    me = lax.axis_index("mem")
    greet("mem", (1, 2, 3))
    moves = []
    for offset, slot, source in ((2, 2, None), (1, 1, None), (1, 3, 2)):
        number = len(moves)
        moves.append(
            (
                send(back_ref if source is None else all_b.at[source], all_b.at[slot],
                     b_send.at[number], b_recv.at[number], offset),
                send(stat_ref if source is None else all_s.at[source], all_s.at[slot],
                     s_send.at[number], s_recv.at[number], offset),
            )
        )
    for move in moves[:2]:
        for copy in move:
            copy.start()
    low, high = half_masks()
    copies = []
    for slot in (0, 2, 3, 1):
        if slot == 2:
            for copy in moves[0]:
                copy.wait_recv()
            for copy in moves[2]:
                copy.start()
        if slot == 3:
            for copy in moves[2]:
                copy.wait_recv()
        if slot == 1:
            for copy in moves[1]:
                copy.wait_recv()
        owner = jnp.bitwise_xor(me, slot)
        for item in range(items):
            place = owner * items + item
            bias = bias_ref[place]
            stats = stat_ref[item] if slot == 0 else all_s[slot, item]
            for index in range(HEADS // 2):
                both = all_ref[slot, item, :, pair(index)]
                if slot == 0:
                    upstream = back_ref[item, :, pair(index)]
                else:
                    upstream = all_b[slot, item, :, pair(index)]
                keys = k_ref[place, :, pair(index)]
                values = v_ref[place, :, pair(index)]
                dq = dk = dv = None
                for half, mask in ((0, low), (1, high)):
                    head = 2 * index + half
                    query = both * mask
                    back = upstream * mask
                    scores = dot_nt(query, keys) + bias
                    probs = jnp.exp(scores - column(stats, head))
                    dprobs = dot_nt(back, values)
                    ds = (probs * (dprobs - column(stats, 8 + head))).astype(BF)
                    q_part = dot(ds, keys * mask)
                    k_part = dot_tn(ds, query)
                    v_part = dot_tn(probs.astype(BF), back)
                    dq = q_part if half == 0 else dq + q_part
                    dk = k_part if half == 0 else dk + k_part
                    dv = v_part if half == 0 else dv + v_part
                out_q[slot, item, :, pair(index)] = dq.astype(BF)
                dk_ref[place, :, pair(index)] = dk.astype(BF)
                dv_ref[place, :, pair(index)] = dv.astype(BF)
        if slot:
            copies.append(send(out_q.at[slot], in_q.at[slot], q_send.at[slot], q_recv.at[slot], slot))
            copies[-1].start()
    for move in moves:
        for copy in move:
            copy.wait_send()
    for copy in copies:
        copy.wait()
    for item in range(items):
        for index in range(HEADS // 2):
            total = out_q[0, item, :, pair(index)].astype(F32)
            for slot in (1, 2, 3):
                total += in_q[slot, item, :, pair(index)].astype(F32)
            dq_ref[item, :, pair(index)] = total.astype(BF)


def cross_bwd(all_queries, back, stats, keys, values, bias):
    items = back.shape[0]
    inner = HEADS * HEAD
    block = (4, items, ROWS, inner)
    flops = 4 * items * HEADS * ROWS * SPAN * 128 * 10
    return pl.pallas_call(
        functools.partial(cross_bwd_kernel, items),
        out_shape=(
            jax.ShapeDtypeStruct(keys.shape, BF),
            jax.ShapeDtypeStruct(keys.shape, BF),
            jax.ShapeDtypeStruct((items, ROWS, inner), BF),
        ),
        in_specs=[VMEM_SPEC] * 6,
        out_specs=(VMEM_SPEC,) * 3,
        scratch_shapes=[
            pltpu.VMEM(block, BF),
            pltpu.VMEM((4, items, ROWS, STATS), F32),
            pltpu.VMEM(block, BF),
            pltpu.VMEM(block, BF),
            pltpu.SemaphoreType.DMA((3,)),
            pltpu.SemaphoreType.DMA((3,)),
            pltpu.SemaphoreType.DMA((3,)),
            pltpu.SemaphoreType.DMA((3,)),
            pltpu.SemaphoreType.DMA((4,)),
            pltpu.SemaphoreType.DMA((4,)),
        ],
        compiler_params=pltpu.CompilerParams(
            collective_id=2, has_side_effects=True, vmem_limit_bytes=VMEM_CAP
        ),
        cost_estimate=pl.CostEstimate(
            flops=flops, bytes_accessed=12 * 1024 * 1024, transcendentals=flops // 1280
        ),
        name="cross_bwd",
    )(all_queries, back, stats, keys, values, bias)


CUBIC = 0.044715
ROOT = float(np.sqrt(2.0 / np.pi))


def strips(width, step):
    return [(start, min(step, width - start)) for start in range(0, width, step)]


def ffn_kernel(
    h_ref, up0_ref, up1_ref, up2_ref, up3_ref, gate_up_ref, down_ref,
    h_back_ref, near_ref, far_ref, grad_gu_ref, grad_down_ref,
    h_all, u_all, hidden, two_back, h_part, y_part, h_in, y_in,
    h_send, h_recv, d_send, d_recv, y_send, y_recv,
):
    tokens, model = h_ref.shape
    units = down_ref.shape[0]
    greet("mem", (1, 2))
    h_to_core = send(h_ref, h_all.at[1], h_send.at[0], h_recv.at[0], 1)
    h_to_far = send(h_ref, h_all.at[2], h_send.at[1], h_recv.at[1], 2)
    h_relay = send(h_all.at[2], h_all.at[3], h_send.at[2], h_recv.at[2], 1)
    d_near = send(h_part.at[1], h_in.at[0], d_send.at[0], d_recv.at[0], 1)
    d_pass = send(h_part.at[3], h_in.at[1], d_send.at[1], d_recv.at[1], 1)
    d_far = send(h_part.at[2], h_in.at[2], d_send.at[2], d_recv.at[2], 2)
    y_near = send(y_part.at[1], y_in.at[0], y_send.at[0], y_recv.at[0], 1)
    y_pass = send(y_part.at[3], y_in.at[1], y_send.at[1], y_recv.at[1], 1)
    h_to_far.start()
    h_to_core.start()
    h_all[0] = h_ref[...]
    u_all[0] = up0_ref[...]
    u_all[1] = up1_ref[...]
    u_all[2] = up2_ref[...]
    u_all[3] = up3_ref[...]

    def token_block(slot, carry):
        @pl.when(slot == 1)
        def _():
            h_to_core.wait_recv()

        @pl.when(slot == 2)
        def _():
            d_near.start()
            y_near.start()
            h_to_far.wait_recv()
            h_relay.start()

        @pl.when(slot == 3)
        def _():
            h_relay.wait_recv()

        def units_block(block, inside):
            pairs = pl.ds(pl.multiple_of(block * 256, 256), 256)
            ones = pl.ds(pl.multiple_of(block * 128, 128), 128)
            both = dot(h_all[slot], gate_up_ref[:, pairs])
            back = dot_nt(u_all[slot], down_ref[ones, :]).astype(BF).astype(F32)
            gate, up = both[:, :128], both[:, 128:]
            square = gate * gate
            bend = jnp.tanh(ROOT * gate * (1.0 + CUBIC * square))
            share = 0.5 * (1.0 + bend)
            active = gate * share
            slope = share + 0.5 * gate * (1.0 - bend * bend) * (
                ROOT * (1.0 + 3.0 * CUBIC * square)
            )
            hidden[slot, :, ones] = (active * up).astype(BF)
            two_back[slot, :, pairs] = jnp.concatenate(
                [(back * up * slope).astype(BF), (back * active).astype(BF)], axis=1
            )
            return inside

        lax.fori_loop(0, units // 128, units_block, 0)
        for start, width in strips(model, 256):
            part = slice(start, start + width)
            h_part[slot, :, part] = dot_nt(two_back[slot], gate_up_ref[part, :]).astype(BF)
            y_part[slot, :, part] = dot(hidden[slot], down_ref[:, part]).astype(BF)
        return carry

    lax.fori_loop(0, 4, token_block, 0)
    d_pass.start()
    y_pass.start()
    d_pass.wait_recv()
    h_part[2] = (h_part[2].astype(F32) + h_in[1].astype(F32)).astype(BF)
    d_far.start()
    count = 4 * tokens
    for start, width in strips(model, 256):
        part = slice(start, start + width)
        grad_gu_ref[part, :] = dot_tn(
            h_all[:, :, part].reshape(count, width), two_back[...].reshape(count, 2 * units)
        ).astype(BF)
    for start, width in strips(units, 256):
        part = slice(start, start + width)
        grad_down_ref[part, :] = dot_tn(
            hidden[:, :, part].reshape(count, width), u_all[...].reshape(count, model)
        ).astype(BF)
    y_pass.wait_recv()
    far_ref[...] = (y_part[2].astype(F32) + y_in[1].astype(F32)).astype(BF)
    y_near.wait_recv()
    near_ref[...] = (y_part[0].astype(F32) + y_in[0].astype(F32)).astype(BF)
    d_near.wait_recv()
    d_far.wait_recv()
    h_back_ref[...] = (
        h_part[0].astype(F32) + h_in[0].astype(F32) + h_in[2].astype(F32)
    )
    for copy in (h_to_core, h_to_far, h_relay, d_near, d_pass, d_far, y_near, y_pass):
        copy.wait_send()


def ffn(h3, upstreams, gate_up, down):
    tokens, model = h3.shape
    units = down.shape[0]
    every = (4, tokens, model)
    flops = 4 * tokens * model * units * 18
    return pl.pallas_call(
        ffn_kernel,
        out_shape=(
            jax.ShapeDtypeStruct((tokens, model), F32),
            jax.ShapeDtypeStruct((tokens, model), BF),
            jax.ShapeDtypeStruct((tokens, model), BF),
            jax.ShapeDtypeStruct((model, 2 * units), BF),
            jax.ShapeDtypeStruct((units, model), BF),
        ),
        in_specs=[VMEM_SPEC] * 7,
        out_specs=(VMEM_SPEC,) * 5,
        scratch_shapes=[
            pltpu.VMEM(every, BF),
            pltpu.VMEM(every, BF),
            pltpu.VMEM((4, tokens, units), BF),
            pltpu.VMEM((4, tokens, 2 * units), BF),
            pltpu.VMEM(every, BF),
            pltpu.VMEM(every, BF),
            pltpu.VMEM((3, tokens, model), BF),
            pltpu.VMEM((2, tokens, model), BF),
            pltpu.SemaphoreType.DMA((3,)),
            pltpu.SemaphoreType.DMA((3,)),
            pltpu.SemaphoreType.DMA((3,)),
            pltpu.SemaphoreType.DMA((3,)),
            pltpu.SemaphoreType.DMA((2,)),
            pltpu.SemaphoreType.DMA((2,)),
        ],
        compiler_params=pltpu.CompilerParams(
            collective_id=3, has_side_effects=True, vmem_limit_bytes=FFN_CAP
        ),
        cost_estimate=pl.CostEstimate(
            flops=flops, bytes_accessed=32 * 1024 * 1024, transcendentals=4 * tokens * units
        ),
        name="feed_forward",
    )(h3, *upstreams, gate_up, down)


def peer_copy(src, dst, send_sem, recv_sem, tgt=None, mem=None):
    where = {}
    if tgt is not None:
        where["tgt"] = tgt
    if mem is not None:
        where["mem"] = mem
    return pltpu.make_async_remote_copy(
        src_ref=src, dst_ref=dst, send_sem=send_sem, recv_sem=recv_sem,
        device_id=where, device_id_type=MESH,
    )


def greet_all(mem, tgt):
    barrier = pltpu.get_barrier_semaphore()
    for offset in (1, 2):
        pl.semaphore_signal(
            barrier, inc=1, device_id={"mem": jnp.bitwise_xor(mem, offset)}, device_id_type=MESH
        )
    for offset in (1, 2, 4, 6):
        pl.semaphore_signal(
            barrier, inc=1, device_id={"tgt": jnp.bitwise_xor(tgt, offset)}, device_id_type=MESH
        )
    pl.semaphore_wait(barrier, 6)


FIRST = (1, 2, 4, 6)
PASSED = (3, 5, 7)


def gather_kernel(
    self_q, self_k, self_v, cross_q, cross_k, cross_v, self_o, cross_o,
    qkv_out, kv_out, cq_out, so_out, co_out,
    t_send, t_recv, x_send, x_recv, c_send, c_recv, r_send, r_recv, own_sem,
):
    mem = lax.axis_index("mem")
    tgt = lax.axis_index("tgt")
    inner = HEADS * HEAD

    def part(out, index):
        return lambda place: out.at[place, :, index * inner : (index + 1) * inner]

    def whole(out):
        return lambda place: out.at[place]

    groups = (
        ((self_q, part(qkv_out, 0)), (self_k, part(qkv_out, 1))),
        ((self_v, part(qkv_out, 2)), (cross_q, part(cq_out, 0))),
        ((cross_k, part(kv_out, 0)), (cross_v, part(kv_out, 1))),
        ((self_o, whole(so_out)), (cross_o, whole(co_out))),
    )
    greet_all(mem, tgt)
    near = jnp.bitwise_xor(mem, 1)
    far = jnp.bitwise_xor(mem, 2)

    def over_tgt(member, number, step, offset):
        src, dst = member
        if step < 4:
            return peer_copy(
                src, dst(tgt), t_send.at[step, number], t_recv.at[step, number],
                tgt=jnp.bitwise_xor(tgt, offset),
            )
        place = jnp.bitwise_xor(tgt, offset - 1)
        return peer_copy(
            dst(place), dst(place), t_send.at[step, number], t_recv.at[step, number],
            tgt=jnp.bitwise_xor(tgt, 1),
        )

    def over_far(member, number, step, offset):
        dst = member[1](jnp.bitwise_xor(tgt, offset))
        return peer_copy(dst, dst, x_send.at[step, number], x_recv.at[step, number], mem=far)

    def over_near(member, number, step, offset):
        dst = member[1](jnp.bitwise_xor(tgt, offset))
        return peer_copy(dst, dst, c_send.at[step, number], c_recv.at[step, number], mem=near)

    def relay(member, number, step, offset):
        dst = member[1](jnp.bitwise_xor(tgt, offset))
        return peer_copy(dst, dst, r_send.at[step, number], r_recv.at[step, number], mem=near)

    steps = list(enumerate(FIRST + PASSED))
    for index, group in enumerate(groups):

        @pl.when(mem == index)
        def _(index=index, group=group):
            members = list(enumerate(group))
            for step, offset in steps[:4]:
                for number, member in members:
                    over_tgt(member, number, step, offset).start()
            own = []
            for place, (src, dst) in enumerate(member for all_of in groups for member in all_of):
                own.append(pltpu.make_async_copy(src, dst(tgt), own_sem.at[place]))
                own[-1].start()
            for step, offset in steps:
                for number, member in members:
                    over_tgt(member, number, step, offset).wait_recv()
                    if 0 < step < 4:
                        over_tgt(member, number, step + 3, offset + 1).start()
                    over_far(member, number, step, offset).start()
                    over_near(member, number, step, offset).start()
            far_members = list(enumerate(groups[index ^ 2]))
            near_members = list(enumerate(groups[index ^ 1]))
            last_members = list(enumerate(groups[index ^ 3]))
            for step, offset in steps:
                for number, member in far_members:
                    over_far(member, number, step, offset).wait_recv()
                    relay(member, number, step, offset).start()
            for step, offset in steps:
                for number, member in near_members:
                    over_near(member, number, step, offset).wait_recv()
                for number, member in last_members:
                    relay(member, number, step, offset).wait_recv()
                for number, member in members:
                    over_tgt(member, number, step, offset).wait_send()
                    over_far(member, number, step, offset).wait_send()
                    over_near(member, number, step, offset).wait_send()
                for number, member in far_members:
                    relay(member, number, step, offset).wait_send()
            for copy in own:
                copy.wait()


def gather_weights(weights):
    tgts = lax.axis_size("tgt")
    rows, inner = weights[0].shape
    o_rows, model = weights[-1].shape

    def out(columns, height=rows):
        return jax.ShapeDtypeStruct((tgts, height, columns), BF)

    shapes = (out(3 * inner), out(2 * inner), out(inner), out(model, o_rows), out(model, o_rows))
    sems = [pltpu.SemaphoreType.DMA((7, 2))] * 8
    return pl.pallas_call(
        gather_kernel,
        out_shape=shapes,
        in_specs=[ANY_SPEC] * 8,
        out_specs=(ANY_SPEC,) * 5,
        scratch_shapes=sems + [pltpu.SemaphoreType.DMA((8,))],
        compiler_params=pltpu.CompilerParams(collective_id=4, has_side_effects=True),
        cost_estimate=pl.CostEstimate(
            flops=0, bytes_accessed=150 * 1024 * 1024, transcendentals=0
        ),
        name="gather_weights",
    )(*weights)


TURNS = (7, 6, 5, 4, 3, 2, 1, 0)


def reduce_kernel(
    qkv_ref, kv_ref, cq_ref, so_ref, co_ref, small_ref,
    q_out, k_out, v_out, cq_out, ck_out, cv_out, so_out, co_out, small_out,
    small_in, s_send, s_recv,
    wide_in, tall_in, wide_x, tall_x, wide_y, tall_y, wide_z, tall_z, wide_e, tall_e,
    a_send, a_recv, b_send, b_recv, x_send, x_recv, y_send, y_recv, z_send, z_recv,
    e_send, e_recv,
):
    mem = lax.axis_index("mem")
    tgt = lax.axis_index("tgt")
    inner = HEADS * HEAD

    def part(ref, index):
        return lambda place: ref.at[place, :, index * inner : (index + 1) * inner]

    def whole(ref):
        return lambda place: ref.at[place]

    wide = (wide_in, wide_x, wide_y, wide_z, wide_e)
    tall = (tall_in, tall_x, tall_y, tall_z, tall_e)
    groups = (
        ((part(qkv_ref, 0), q_out, wide), (part(qkv_ref, 1), k_out, wide)),
        ((part(qkv_ref, 2), v_out, wide), (part(cq_ref, 0), cq_out, wide)),
        ((part(kv_ref, 0), ck_out, wide), (part(kv_ref, 1), cv_out, wide)),
        ((whole(so_ref), so_out, tall), (whole(co_ref), co_out, tall)),
    )
    greet_all(mem, tgt)
    near = jnp.bitwise_xor(mem, 1)
    far = jnp.bitwise_xor(mem, 2)

    def to_near(member, number, step, lane):
        place = jnp.bitwise_xor(tgt, TURNS[step])
        send_sems, recv_sems = ((a_send, a_recv), (b_send, b_recv))[lane]
        return peer_copy(
            member[0](place), member[2][0].at[lane, step, number],
            send_sems.at[step, number], recv_sems.at[step, number], mem=near,
        )

    def to_far(member, number, step):
        buffer = member[2][1]
        return peer_copy(
            buffer.at[0, step, number], buffer.at[1, step, number],
            x_send.at[step, number], x_recv.at[step, number], mem=far,
        )

    def to_side(member, number, turn):
        buffer = member[2][2]
        return peer_copy(
            buffer.at[0, turn, number], buffer.at[1, turn, number],
            y_send.at[turn, number], y_recv.at[turn, number], tgt=jnp.bitwise_xor(tgt, 1),
        )

    def to_owner(member, number, turn):
        buffer = member[2][3]
        return peer_copy(
            buffer.at[0, turn, number], buffer.at[1, turn, number],
            z_send.at[turn, number], z_recv.at[turn, number],
            tgt=jnp.bitwise_xor(tgt, TURNS[2 * turn + 1]),
        )

    def to_all(member, number, lane, peer):
        buffer = member[2][4]
        return peer_copy(
            buffer.at[2 if lane == 2 else 0, number],
            buffer.at[(1, 2, 3)[lane], number],
            e_send.at[lane, number], e_recv.at[lane, number], mem=peer,
        )

    partners = (
        {"mem": near}, {"mem": far}, {"tgt": jnp.bitwise_xor(tgt, 1)},
        {"tgt": jnp.bitwise_xor(tgt, 2)}, {"tgt": jnp.bitwise_xor(tgt, 4)},
    )
    small_moves = [
        peer_copy(small_in.at[0, step], small_in.at[1, step], s_send.at[step], s_recv.at[step], **to)
        for step, to in enumerate(partners)
    ]

    for index, group in enumerate(groups):

        @pl.when(mem == index)
        def _(index=index, group=group):
            mine = list(enumerate(group))
            near_group = list(enumerate(groups[index ^ 1]))
            far_group = list(enumerate(groups[index ^ 2]))
            last_group = list(enumerate(groups[index ^ 3]))
            steps = range(len(TURNS))
            for step in steps:
                for number, member in last_group:
                    to_near(member, number, step, 1).start()
                for number, member in near_group:
                    to_near(member, number, step, 0).start()
            for step in steps:
                place = jnp.bitwise_xor(tgt, TURNS[step])
                for number, member in far_group:
                    to_near(member, number, step, 1).wait_recv()
                    member[2][1][0, step, number] = (
                        member[0](place)[...].astype(F32)
                        + member[2][0][1, step, number].astype(F32)
                    ).astype(BF)
                    to_far(member, number, step).start()
            small_in[0, 0] = small_ref[...]
            for step, move in enumerate(small_moves):
                move.start()
                move.wait_recv()
                total = small_in[0, step] + small_in[1, step]
                if step + 1 < len(small_moves):
                    small_in[0, step + 1] = total
                else:
                    small_out[...] = total
            for step in steps:
                place = jnp.bitwise_xor(tgt, TURNS[step])
                turn = step // 2
                for number, member in mine:
                    to_near(member, number, step, 0).wait_recv()
                    to_far(member, number, step).wait_recv()
                    total = (
                        member[0](place)[...].astype(F32)
                        + member[2][0][0, step, number].astype(F32)
                        + member[2][1][1, step, number].astype(F32)
                    )
                    if step % 2 == 0:
                        member[2][2][0, turn, number] = total.astype(BF)
                        to_side(member, number, turn).start()
                        continue
                    to_side(member, number, turn).wait_recv()
                    total = total + member[2][2][1, turn, number].astype(F32)
                    if turn < 3:
                        member[2][3][0, turn, number] = total.astype(BF)
                        to_owner(member, number, turn).start()
                        continue
                    for other in range(3):
                        to_owner(member, number, other).wait_recv()
                        total = total + member[2][3][1, other, number].astype(F32)
                    member[2][4][0, number] = total.astype(BF)
                    to_all(member, number, 1, far).start()
                    to_all(member, number, 0, near).start()
                    member[1][...] = member[2][4][0, number]
            for number, member in far_group:
                to_all(member, number, 1, far).wait_recv()
                to_all(member, number, 2, near).start()
                member[1][...] = member[2][4][2, number]
            for number, member in near_group:
                to_all(member, number, 0, near).wait_recv()
                member[1][...] = member[2][4][1, number]
            for number, member in last_group:
                to_all(member, number, 2, near).wait_recv()
                member[1][...] = member[2][4][3, number]
            for move in small_moves:
                move.wait_send()
            for step in steps:
                for number, member in last_group:
                    to_near(member, number, step, 1).wait_send()
                for number, member in near_group:
                    to_near(member, number, step, 0).wait_send()
                for number, member in far_group:
                    to_far(member, number, step).wait_send()
            for number, member in mine:
                for turn in range(4):
                    to_side(member, number, turn).wait_send()
                for turn in range(3):
                    to_owner(member, number, turn).wait_send()
                to_all(member, number, 0, near).wait_send()
                to_all(member, number, 1, far).wait_send()
            for number, member in far_group:
                to_all(member, number, 2, near).wait_send()


def reduce_weights(d_qkv, d_kv, d_cq, d_so, d_co, small):
    rows, inner = d_cq.shape[1:]
    o_rows, model = d_so.shape[1:]
    wide, tall = (rows, inner), (o_rows, model)
    scratch = []
    for lead in ((2, 8, 2), (2, 8, 2), (2, 4, 2), (2, 3, 2), (4, 2)):
        scratch += [pltpu.VMEM(lead + wide, BF), pltpu.VMEM(lead + tall, BF)]
    sems = []
    for count in (8, 8, 8, 4, 3, 3):
        sems += [pltpu.SemaphoreType.DMA((count, 2))] * 2
    return pl.pallas_call(
        reduce_kernel,
        out_shape=tuple(jax.ShapeDtypeStruct(wide, BF) for _ in range(6))
        + tuple(jax.ShapeDtypeStruct(tall, BF) for _ in range(2))
        + (jax.ShapeDtypeStruct(small.shape, F32),),
        in_specs=[VMEM_SPEC] * 6,
        out_specs=(VMEM_SPEC,) * 9,
        scratch_shapes=[pltpu.VMEM((2, 5) + small.shape, F32)]
        + [pltpu.SemaphoreType.DMA((5,))] * 2
        + scratch
        + sems,
        compiler_params=pltpu.CompilerParams(
            collective_id=5, has_side_effects=True, vmem_limit_bytes=VMEM_CAP
        ),
        cost_estimate=pl.CostEstimate(
            flops=0, bytes_accessed=150 * 1024 * 1024, transcendentals=0
        ),
        name="reduce_weights",
    )(d_qkv, d_kv, d_cq, d_so, d_co, small)


def pick_kernel(tgts, groups, gate_ref, up_ref, out_ref):
    mem = lax.axis_index("mem")
    shard = gate_ref.shape[1] // tgts
    piece = shard // groups

    for group in range(groups):

        @pl.when(mem == group)
        def _(group=group):
            for number, ref in enumerate((gate_ref, up_ref)):
                parts = []
                for place in range(tgts):
                    start = place * shard + group * piece
                    parts.append(ref[:, start : start + piece].astype(F32))
                quarter = jnp.concatenate(parts, axis=1).astype(BF)
                for block in range(quarter.shape[1] // 128):
                    start = block * 256 + number * 128
                    out_ref[:, start : start + 128] = quarter[:, block * 128 : block * 128 + 128]


def pick_units(gate, up):
    groups, tgts = lax.axis_size("mem"), lax.axis_size("tgt")
    rows, units = gate.shape
    return pl.pallas_call(
        functools.partial(pick_kernel, tgts, groups),
        out_shape=jax.ShapeDtypeStruct((rows, 2 * units // groups), BF),
        in_specs=[VMEM_SPEC] * 2,
        out_specs=VMEM_SPEC,
        compiler_params=pltpu.CompilerParams(vmem_limit_bytes=VMEM_CAP),
        name="pick_units",
    )(gate, up)


def place_kernel(tgts, groups, parts_ref, gate_ref, up_ref):
    units = gate_ref.shape[1]
    piece = units // tgts // groups
    for number, ref in enumerate((gate_ref, up_ref)):
        quarters = []
        for group in range(groups):
            blocks = [
                parts_ref[group, :, start : start + 128]
                for start in range(number * 128, 2 * units // groups, 256)
            ]
            quarters.append(jnp.concatenate(blocks, axis=1).astype(F32))
        ref[...] = jnp.concatenate(
            [
                quarters[group][:, place * piece : (place + 1) * piece]
                for place in range(tgts)
                for group in range(groups)
            ],
            axis=1,
        )


def place_units(parts):
    groups, tgts = lax.axis_size("mem"), lax.axis_size("tgt")
    rows, columns = parts.shape[1:]
    shape = jax.ShapeDtypeStruct((rows, groups * columns // 2), F32)
    return pl.pallas_call(
        functools.partial(place_kernel, tgts, groups),
        out_shape=(shape, shape),
        in_specs=[VMEM_SPEC],
        out_specs=(VMEM_SPEC, VMEM_SPEC),
        compiler_params=pltpu.CompilerParams(vmem_limit_bytes=VMEM_CAP),
        name="place_units",
    )(parts)


def share_kernel(wide_ref, tall_ref, wide_out, tall_out, wide_send, wide_recv, tall_send, tall_recv, own):
    mem = lax.axis_index("mem")
    greet("mem", (1, 2))
    near = jnp.bitwise_xor(mem, 1)
    far = jnp.bitwise_xor(mem, 2)
    moves = []
    for src, out, sends, recvs in (
        (wide_ref, wide_out, wide_send, wide_recv),
        (tall_ref, tall_out, tall_send, tall_recv),
    ):
        to_far = peer_copy(src, out.at[mem], sends.at[0], recvs.at[0], mem=far)
        to_near = peer_copy(src, out.at[mem], sends.at[1], recvs.at[1], mem=near)
        relay = peer_copy(out.at[far], out.at[far], sends.at[2], recvs.at[2], mem=near)
        to_far.start()
        to_near.start()
        moves.append((to_far, to_near, relay))
    copies = [
        pltpu.make_async_copy(wide_ref, wide_out.at[mem], own.at[0]),
        pltpu.make_async_copy(tall_ref, tall_out.at[mem], own.at[1]),
    ]
    for copy in copies:
        copy.start()
    for to_far, _, relay in moves:
        to_far.wait_recv()
        relay.start()
    for to_far, to_near, relay in moves:
        to_near.wait_recv()
        relay.wait_recv()
        to_far.wait_send()
        to_near.wait_send()
        relay.wait_send()
    for copy in copies:
        copy.wait()


def share(wide, tall):
    groups = lax.axis_size("mem")
    return pl.pallas_call(
        share_kernel,
        out_shape=tuple(
            jax.ShapeDtypeStruct((groups,) + value.shape, BF) for value in (wide, tall)
        ),
        in_specs=[ANY_SPEC] * 2,
        out_specs=(ANY_SPEC,) * 2,
        scratch_shapes=[pltpu.SemaphoreType.DMA((3,))] * 4 + [pltpu.SemaphoreType.DMA((2,))],
        compiler_params=pltpu.CompilerParams(collective_id=6, has_side_effects=True),
        cost_estimate=pl.CostEstimate(
            flops=0, bytes_accessed=60 * 1024 * 1024, transcendentals=0
        ),
        name="share_sums",
    )(wide, tall)


def over_mem(value, offset):
    return lax.ppermute(value, "mem", [(i, i ^ offset) for i in range(4)])


def gather_mem(value):
    far = over_mem(value, 2)
    near = over_mem(value, 1)
    return value, near, far, over_mem(far, 1)


def gather_tgt(shard):
    return lax.all_gather(shard, "tgt", axis=0, tiled=True)


def scatter_tgt(partial):
    return lax.psum_scatter(partial, "tgt", scatter_dimension=0, tiled=True)


def attention_weights(weights):
    if lax.axis_size("tgt") == 8:
        return gather_weights(weights)
    parts = [lax.all_gather(weight, "tgt", axis=0) for weight in weights]
    return (
        jnp.concatenate(parts[:3], axis=-1),
        jnp.concatenate(parts[4:6], axis=-1),
        parts[3],
        parts[6],
        parts[7],
    )


def attention_sums(partials, small):
    if lax.axis_size("tgt") == 8:
        return reduce_weights(*partials, small)
    inner = HEADS * HEAD
    totals = [
        lax.psum_scatter(partial, "tgt", scatter_dimension=0, tiled=False) for partial in partials
    ]
    qkv, kv, cq, so, co = lax.psum(totals, "mem")
    return (
        qkv[:, :inner], qkv[:, inner : 2 * inner], qkv[:, 2 * inner :], cq,
        kv[:, :inner], kv[:, inner:], so, co, lax.psum(small, ("tgt", "mem")),
    )


def on_device(
    target, memory, lengths, gate_bias, out_grad, gain_self, gain_cross, gain_ffn, rel_table,
    self_q, self_k, self_v, self_o, cross_q, cross_k, cross_v, cross_o, ffn_gate, ffn_up, ffn_down,
):
    groups = lax.axis_size("mem")
    tgts = lax.axis_size("tgt")
    mem_index = lax.axis_index("mem")
    items, seq, model = target.shape
    all_items, positions_dev, _ = memory.shape
    inner = HEADS * HEAD
    tokens = items * ROWS
    shard_in = ffn_gate.shape[0]
    hidden_shard = ffn_down.shape[0]
    piece = hidden_shard // groups
    quarter = tgts * piece

    def padded(value):
        return jnp.pad(value, ((0, 0), (0, ROWS - seq), (0, 0))).reshape(tokens, model)

    def trimmed(value):
        return value.reshape(items, ROWS, model)[:, :seq]

    norm_self = gain_self.astype(F32)
    norm_cross = gain_cross.astype(F32)
    norm_ffn = gain_ffn.astype(F32)
    onehot = jnp.asarray(distance_onehot())
    base = jnp.pad(
        lax.dot_general(rel_table, onehot, TN, precision=HIGH), ((0, 2), (0, 0))
    )
    positions = mem_index * positions_dev + jnp.arange(positions_dev)
    bias = jnp.where(positions[None, :] < lengths[:, None], gate_bias, NEG)[:, None, :]

    self_w, cross_kv_w, cross_q_w, self_o_w, cross_o_w = (
        weight.reshape(-1, weight.shape[-1])
        for weight in attention_weights(
            (self_q, self_k, self_v, cross_q, cross_k, cross_v, self_o, cross_o)
        )
    )
    gate_up = gather_tgt(pick_units(ffn_gate, ffn_up))
    down = gather_tgt(
        lax.dynamic_slice_in_dim(ffn_down, mem_index * piece, piece, axis=0)
    )

    inputs = padded(target).astype(F32)
    upstream_low = padded(out_grad)
    late, self_w = lax.optimization_barrier((upstream_low, self_w))
    upstreams = gather_mem(late)
    mem_flat = memory.reshape(all_items * positions_dev, model)

    h1 = (inputs * rms_scale(inputs) * norm_self).astype(BF)
    qkv = dot(h1, self_w).astype(BF).reshape(items, ROWS, 3 * inner)
    att = self_fwd(qkv, base).reshape(tokens, inner)
    y1 = inputs + dot(att, self_o_w)
    h2 = (y1 * rms_scale(y1) * norm_cross).astype(BF)
    cq = dot(h2, cross_q_w).astype(BF).reshape(items, ROWS, inner)
    ckv = dot(mem_flat, cross_kv_w).astype(BF)
    ck = ckv[:, :inner].reshape(all_items, positions_dev, inner)
    cv = ckv[:, inner:].reshape(all_items, positions_dev, inner)
    all_queries, catt, lse = cross_fwd(cq, ck, cv, bias)
    catt = catt.reshape(tokens, inner)
    y2 = y1 + dot(catt, cross_o_w)
    h3 = (y2 * rms_scale(y2) * norm_ffn).astype(BF)

    h3_back, out_near, out_far, grad_gate_up, grad_down = ffn(h3, upstreams, gate_up, down)
    out_sum = over_mem(out_far, 2)
    grad_gate_up = scatter_tgt(grad_gate_up)
    grad_down = scatter_tgt(grad_down)
    dx, grad_norm_ffn = rms_back(y2, norm_ffn, h3_back)
    dy2 = upstream_low.astype(F32) + dx
    e2 = dy2.astype(BF)
    grad_cross_o = dot_tn(catt, e2)
    dcatt = dot_nt(e2, cross_o_w).astype(BF)
    delta = jnp.sum(
        (dcatt.astype(F32) * catt.astype(F32)).reshape(tokens, HEADS, HEAD), axis=-1
    ).reshape(items, ROWS, HEADS)
    stats = jnp.concatenate(
        [lse[:, :, :8], delta, jnp.zeros((items, ROWS, STATS - 8 - HEADS), F32)], axis=-1
    )
    dck, dcv, dcq = cross_bwd(
        all_queries, dcatt.reshape(items, ROWS, inner), stats, ck, cv, bias
    )
    y2_late, dcq = lax.optimization_barrier((y2, dcq))
    layer_out = trimmed(
        (y2_late + out_near.astype(F32) + out_sum.astype(F32)).astype(BF)
    )
    dckv = jnp.concatenate([dck, dcv], axis=-1).reshape(all_items * positions_dev, 2 * inner)
    dcq = dcq.reshape(tokens, inner)
    grad_cross_kv = dot_tn(mem_flat, dckv)
    memory_grad = dot_nt(dckv, cross_kv_w).astype(BF).reshape(memory.shape)
    grad_cross_q = dot_tn(h2, dcq)
    dx, grad_norm_cross = rms_back(y1, norm_cross, dot_nt(dcq, cross_q_w))
    dy1 = dy2 + dx
    e1 = dy1.astype(BF)
    grad_self_o = dot_tn(att, e1)
    datt = dot_nt(e1, self_o_w).astype(BF).reshape(items, ROWS, inner)
    dqkv, diag = self_bwd(qkv, datt, base)
    dqkv = dqkv.reshape(tokens, 3 * inner)
    grad_self = dot_tn(h1, dqkv)
    dx, grad_norm_self = rms_back(inputs, norm_self, dot_nt(dqkv, self_w))
    target_grad = trimmed((dy1 + dx).astype(BF))
    table = lax.dot_general(
        onehot, diag[:HEADS], NT, precision=HIGH
    )

    small = jnp.concatenate(
        [grad_norm_self, grad_norm_cross, grad_norm_ffn, table.reshape(-1)]
    )
    *sums, small = attention_sums(
        tuple(
            partial.astype(BF).reshape(tgts, -1, partial.shape[-1])
            for partial in (grad_self, grad_cross_kv, grad_cross_q, grad_self_o, grad_cross_o)
        ),
        jnp.pad(small, (0, -small.size % 1024)).reshape(-1, 128),
    )
    columns = [partial.astype(F32) for partial in sums]
    grad_gate_up, grad_down, small = lax.optimization_barrier((grad_gate_up, grad_down, small))
    grad_gate_up, grad_down = share(grad_gate_up, grad_down)
    grad_gate, grad_up = place_units(grad_gate_up)
    grad_down = grad_down.reshape(-1, model).astype(F32)
    small = small.reshape(-1)
    norms = [small[start : start + model] for start in range(0, 3 * model, model)]
    table = small[3 * model : 3 * model + table.size].reshape(table.shape)
    return (
        layer_out,
        target_grad,
        memory_grad,
        *norms,
        table,
        columns[0],
        columns[1],
        columns[2],
        columns[6],
        columns[3],
        columns[4],
        columns[5],
        columns[7],
        grad_gate,
        grad_up,
        grad_down,
    )


def solution(mesh):
    owned = P(("tgt", "mem"), None, None)
    held = P("tgt", "mem", None)
    rows = P("tgt", None)
    return jax.shard_map(
        on_device,
        mesh=mesh,
        in_specs=(owned, held, P("tgt"), P("tgt", "mem"), owned, P(), P(), P(), P()) + (rows,) * 11,
        out_specs=(owned, owned, held, P(), P(), P(), P()) + (rows,) * 11,
        check_vma=False,
    )
```

```python
import functools

import jax
import jax.numpy as jnp
import numpy as np
from jax import lax
from jax.experimental import pallas as pl
from jax.experimental.pallas import tpu as pltpu
from jax.sharding import PartitionSpec as P

HEADS = 6
HEAD = 64
BUCKETS = 32
MAX_DIST = 128
ROWS = 192
SPAN = 256
STATS = 128

EPS = 1e-06
NEG = -1e30
HIGH = lax.Precision.HIGHEST
BF = jnp.bfloat16
F32 = jnp.float32
MESH = pl.DeviceIdType.MESH
NT = (((1,), (1,)), ((), ()))
TN = (((0,), (0,)), ((), ()))
VMEM_SPEC = pl.BlockSpec(memory_space=pltpu.VMEM)
ANY_SPEC = pl.BlockSpec(memory_space=pl.ANY)
VMEM_CAP = 56 * 1024 * 1024
FFN_CAP = 62 * 1024 * 1024


def distance_onehot():
    distance = (SPAN - np.arange(SPAN)) % SPAN
    exact_max = BUCKETS // 2
    scaled = (
        np.log(np.maximum(distance, 1) / exact_max)
        / np.log(MAX_DIST / exact_max)
        * (BUCKETS - exact_max)
    )
    far = np.minimum(
        exact_max + np.floor(np.maximum(scaled, 0.0)).astype(np.int64), BUCKETS - 1
    )
    bucket = np.where(distance < exact_max, distance, far)
    return (np.arange(BUCKETS)[:, None] == bucket[None, :]).astype(np.float32)


def dot(left, right):
    return jnp.dot(left, right, preferred_element_type=F32)


def dot_nt(left, right):
    return lax.dot_general(left, right, NT, preferred_element_type=F32)


def dot_tn(left, right):
    return lax.dot_general(left, right, TN, preferred_element_type=F32)


def rms_scale(inputs):
    return lax.rsqrt(jnp.mean(inputs * inputs, axis=-1, keepdims=True) + EPS)


def rms_back(inputs, gain, upstream):
    scale = rms_scale(inputs)
    gu = gain * upstream
    inner = jnp.mean(inputs * gu, axis=-1, keepdims=True)
    dx = scale * gu - inputs * (scale * scale * scale * inner)
    return dx, jnp.sum(upstream * inputs * scale, axis=0)


def half_masks():
    lane = lax.broadcasted_iota(jnp.int32, (1, 2 * HEAD), 1)
    low = (lane < HEAD).astype(BF)
    return low, 1 - low


def pair(index):
    return slice(index * 2 * HEAD, (index + 1) * 2 * HEAD)


def head_bias(base_ref, head):
    row = jnp.broadcast_to(base_ref[head : head + 1, :], (ROWS, SPAN))
    return pltpu.roll(row, 0, 1, stride=1, stride_axis=0)


def causal_mask():
    rows = lax.broadcasted_iota(jnp.int32, (ROWS, SPAN), 0)
    cols = lax.broadcasted_iota(jnp.int32, (ROWS, SPAN), 1)
    return cols <= rows


def self_fwd_kernel(items, qkv_ref, base_ref, att_ref, k_pad, v_pad):
    inner = HEADS * HEAD
    k_pad[...] = jnp.zeros_like(k_pad)
    v_pad[...] = jnp.zeros_like(v_pad)
    for item in range(items):
        k_pad[item, :ROWS, :] = qkv_ref[item, :, inner : 2 * inner]
        v_pad[item, :ROWS, :] = qkv_ref[item, :, 2 * inner :]
    causal = causal_mask()
    masks = half_masks()
    for index in range(HEADS // 2):
        sums = [None] * items
        for half in range(2):
            bias = head_bias(base_ref, 2 * index + half)
            for item in range(items):
                query = qkv_ref[item, :, pair(index)] * masks[half]
                scores = dot_nt(query, k_pad[item, :, pair(index)]) + bias
                scores = jnp.where(causal, scores, NEG)
                top = jnp.max(scores, axis=-1, keepdims=True)
                probs = jnp.exp(scores - top)
                probs = probs * (1.0 / jnp.sum(probs, axis=-1, keepdims=True))
                part = dot(probs.astype(BF), v_pad[item, :, pair(index)] * masks[half])
                sums[item] = part if half == 0 else sums[item] + part
        for item in range(items):
            att_ref[item, :, pair(index)] = sums[item].astype(BF)


def self_fwd(qkv, base):
    items = qkv.shape[0]
    inner = HEADS * HEAD
    return pl.pallas_call(
        functools.partial(self_fwd_kernel, items),
        out_shape=jax.ShapeDtypeStruct((items, ROWS, inner), BF),
        in_specs=[VMEM_SPEC] * 2,
        out_specs=VMEM_SPEC,
        scratch_shapes=[pltpu.VMEM((items, SPAN, inner), BF)] * 2,
        compiler_params=pltpu.CompilerParams(vmem_limit_bytes=VMEM_CAP),
        cost_estimate=pl.CostEstimate(
            flops=items * HEADS * ROWS * SPAN * 128 * 4,
            bytes_accessed=items * ROWS * inner * 8,
            transcendentals=items * HEADS * ROWS * SPAN,
        ),
        name="self_fwd",
    )(qkv, base)


def diagonal_sums(values):
    total = values[:8]
    for start in range(8, ROWS, 8):
        total = total + pltpu.roll(values[start : start + 8], SPAN - start, 1)
    row = lax.broadcasted_iota(jnp.int32, (8, SPAN), 0)
    for bit in (1, 2, 4):
        total = jnp.where((row & bit) > 0, pltpu.roll(total, SPAN - bit, 1), total)
    return jnp.sum(total, axis=0, keepdims=True)


def self_bwd_kernel(items, qkv_ref, datt_ref, base_ref, dqkv_ref, diag_ref, k_pad, v_pad):
    inner = HEADS * HEAD
    k_pad[...] = jnp.zeros_like(k_pad)
    v_pad[...] = jnp.zeros_like(v_pad)
    diag_ref[...] = jnp.zeros_like(diag_ref)
    for item in range(items):
        k_pad[item, :ROWS, :] = qkv_ref[item, :, inner : 2 * inner]
        v_pad[item, :ROWS, :] = qkv_ref[item, :, 2 * inner :]
    causal = causal_mask()
    masks = half_masks()
    for index in range(HEADS // 2):
        dq = [None] * items
        dk = [None] * items
        dv = [None] * items
        for half in range(2):
            head = 2 * index + half
            bias = head_bias(base_ref, head)
            ds_sum = None
            for item in range(items):
                query = qkv_ref[item, :, pair(index)] * masks[half]
                upstream = datt_ref[item, :, pair(index)] * masks[half]
                keys = k_pad[item, :, pair(index)]
                scores = dot_nt(query, keys) + bias
                scores = jnp.where(causal, scores, NEG)
                top = jnp.max(scores, axis=-1, keepdims=True)
                probs = jnp.exp(scores - top)
                probs = probs * (1.0 / jnp.sum(probs, axis=-1, keepdims=True))
                dprobs = dot_nt(upstream, v_pad[item, :, pair(index)])
                delta = jnp.sum(probs * dprobs, axis=-1, keepdims=True)
                ds = probs * (dprobs - delta)
                ds_sum = ds if item == 0 else ds_sum + ds
                ds_low = ds.astype(BF)
                q_part = dot(ds_low, keys * masks[half])
                k_part = dot_tn(ds_low, query)[:ROWS]
                v_part = dot_tn(probs.astype(BF), upstream)[:ROWS]
                dq[item] = q_part if half == 0 else dq[item] + q_part
                dk[item] = k_part if half == 0 else dk[item] + k_part
                dv[item] = v_part if half == 0 else dv[item] + v_part
            diag_ref[head : head + 1, :] = diagonal_sums(ds_sum)
        for item in range(items):
            dqkv_ref[item, :, pair(index)] = dq[item].astype(BF)
            dqkv_ref[item, :, pair(index + 3)] = dk[item].astype(BF)
            dqkv_ref[item, :, pair(index + 6)] = dv[item].astype(BF)


def self_bwd(qkv, datt, base):
    items = qkv.shape[0]
    inner = HEADS * HEAD
    return pl.pallas_call(
        functools.partial(self_bwd_kernel, items),
        out_shape=(
            jax.ShapeDtypeStruct((items, ROWS, 3 * inner), BF),
            jax.ShapeDtypeStruct((8, SPAN), F32),
        ),
        in_specs=[VMEM_SPEC] * 3,
        out_specs=(VMEM_SPEC, VMEM_SPEC),
        scratch_shapes=[pltpu.VMEM((items, SPAN, inner), BF)] * 2,
        compiler_params=pltpu.CompilerParams(vmem_limit_bytes=VMEM_CAP),
        cost_estimate=pl.CostEstimate(
            flops=items * HEADS * ROWS * SPAN * 128 * 10,
            bytes_accessed=items * ROWS * inner * 14,
            transcendentals=items * HEADS * ROWS * SPAN,
        ),
        name="self_bwd",
    )(qkv, datt, base)


def greet(axis, offsets):
    me = lax.axis_index(axis)
    barrier = pltpu.get_barrier_semaphore()
    for offset in offsets:
        pl.semaphore_signal(
            barrier, inc=1, device_id={axis: jnp.bitwise_xor(me, offset)}, device_id_type=MESH
        )
    pl.semaphore_wait(barrier, len(offsets))


def send(src, dst, send_sem, recv_sem, offset):
    me = lax.axis_index("mem")
    return pltpu.make_async_remote_copy(
        src_ref=src,
        dst_ref=dst,
        send_sem=send_sem,
        recv_sem=recv_sem,
        device_id={"mem": jnp.bitwise_xor(me, offset)},
        device_id_type=MESH,
    )


def column(stats, index):
    return stats[:, index : index + 1]


def spread(stats, index, masks):
    return jnp.where(masks, column(stats, 2 * index), column(stats, 2 * index + 1))


def cross_fwd_kernel(
    items, q_ref, kv_ref, bias_ref, all_ref, att_ref, lse_ref,
    out_o, out_s, in_o, in_s, q_send, q_recv, o_send, o_recv, s_send, s_recv,
):
    me = lax.axis_index("mem")
    greet("mem", (1, 2, 3))
    q_to_core = send(q_ref, all_ref.at[1], q_send.at[0], q_recv.at[0], 1)
    q_to_far = send(q_ref, all_ref.at[2], q_send.at[1], q_recv.at[1], 2)
    q_relay = send(all_ref.at[2], all_ref.at[3], q_send.at[2], q_recv.at[2], 1)
    q_to_far.start()
    q_to_core.start()
    all_ref[0] = q_ref[...]
    low, high = half_masks()
    lane = lax.broadcasted_iota(jnp.int32, (1, STATS), 1)
    is_low = lax.broadcasted_iota(jnp.int32, (1, 2 * HEAD), 1) < HEAD
    copies = []
    for slot in (0, 2, 3, 1):
        if slot == 2:
            q_to_far.wait_recv()
            q_relay.start()
        if slot == 3:
            q_relay.wait_recv()
        if slot == 1:
            q_to_core.wait_recv()
        owner = jnp.bitwise_xor(me, slot)
        for item in range(items):
            place = owner * items + item
            bias = bias_ref[place]
            stats = jnp.zeros((ROWS, STATS), F32)
            for index in range(HEADS // 2):
                both = all_ref[slot, item, :, pair(index)]
                keys = kv_ref[place, :, pair(index)]
                values = kv_ref[place, :, pair(index + HEADS // 2)]
                total = None
                scales = []
                for half, mask in ((0, low), (1, high)):
                    scores = dot_nt(both * mask, keys) + bias
                    top = jnp.max(scores, axis=-1, keepdims=True)
                    probs = jnp.exp(scores - top)
                    amount = jnp.sum(probs, axis=-1, keepdims=True)
                    part = dot(probs.astype(BF), values * mask)
                    total = part if half == 0 else total + part
                    scales.append(1.0 / amount)
                    stats = jnp.where(
                        lane == 2 * index + half, top + jnp.log(amount), stats
                    )
                total = total * jnp.where(is_low, scales[0], scales[1])
                out_o[slot, item, :, pair(index)] = total.astype(BF)
            out_s[slot, item] = stats
        if slot:
            copies.append(send(out_o.at[slot], in_o.at[slot], o_send.at[slot], o_recv.at[slot], slot))
            copies.append(send(out_s.at[slot], in_s.at[slot], s_send.at[slot], s_recv.at[slot], slot))
            copies[-2].start()
            copies[-1].start()
    q_to_core.wait_send()
    q_to_far.wait_send()
    q_relay.wait_send()
    for copy in copies:
        copy.wait()
    for item in range(items):
        stats = [out_s[0, item]] + [in_s[slot, item] for slot in (1, 2, 3)]
        top = jnp.maximum(jnp.maximum(stats[0], stats[1]), jnp.maximum(stats[2], stats[3]))
        shares = [jnp.exp(part - top) for part in stats]
        amount = shares[0] + shares[1] + shares[2] + shares[3]
        lse_ref[item] = top + jnp.log(amount)
        scale = 1.0 / amount
        shares = [part * scale for part in shares]
        for index in range(HEADS // 2):
            total = out_o[0, item, :, pair(index)].astype(F32) * spread(shares[0], index, is_low)
            for slot in (1, 2, 3):
                total += in_o[slot, item, :, pair(index)].astype(F32) * spread(
                    shares[slot], index, is_low
                )
            att_ref[item, :, pair(index)] = total.astype(BF)


def cross_fwd(queries, keys_values, bias):
    items = queries.shape[0]
    inner = HEADS * HEAD
    block = (4, items, ROWS, inner)
    stat_block = (4, items, ROWS, STATS)
    flops = 4 * items * HEADS * ROWS * SPAN * 128 * 4
    return pl.pallas_call(
        functools.partial(cross_fwd_kernel, items),
        out_shape=(
            jax.ShapeDtypeStruct(block, BF),
            jax.ShapeDtypeStruct((items, ROWS, inner), BF),
            jax.ShapeDtypeStruct((items, ROWS, STATS), F32),
        ),
        in_specs=[VMEM_SPEC] * 3,
        out_specs=(VMEM_SPEC,) * 3,
        scratch_shapes=[
            pltpu.VMEM(block, BF),
            pltpu.VMEM(stat_block, F32),
            pltpu.VMEM(block, BF),
            pltpu.VMEM(stat_block, F32),
            pltpu.SemaphoreType.DMA((3,)),
            pltpu.SemaphoreType.DMA((3,)),
            pltpu.SemaphoreType.DMA((4,)),
            pltpu.SemaphoreType.DMA((4,)),
            pltpu.SemaphoreType.DMA((4,)),
            pltpu.SemaphoreType.DMA((4,)),
        ],
        compiler_params=pltpu.CompilerParams(
            collective_id=1, has_side_effects=True, vmem_limit_bytes=VMEM_CAP
        ),
        cost_estimate=pl.CostEstimate(
            flops=flops, bytes_accessed=8 * 1024 * 1024, transcendentals=flops // 512
        ),
        name="cross_fwd",
    )(queries, keys_values, bias)


def cross_bwd_kernel(
    items, all_ref, back_ref, stat_ref, kv_ref, bias_ref, dkv_ref, dq_ref,
    all_b, all_s, out_q, in_q, b_send, b_recv, s_send, s_recv, q_send, q_recv,
):
    me = lax.axis_index("mem")
    greet("mem", (1, 2, 3))
    moves = []
    for offset, slot, source in ((2, 2, None), (1, 1, None), (1, 3, 2)):
        number = len(moves)
        moves.append(
            (
                send(back_ref if source is None else all_b.at[source], all_b.at[slot],
                     b_send.at[number], b_recv.at[number], offset),
                send(stat_ref if source is None else all_s.at[source], all_s.at[slot],
                     s_send.at[number], s_recv.at[number], offset),
            )
        )
    for move in moves[:2]:
        for copy in move:
            copy.start()
    low, high = half_masks()
    copies = []
    for slot in (0, 2, 3, 1):
        if slot == 2:
            for copy in moves[0]:
                copy.wait_recv()
            for copy in moves[2]:
                copy.start()
        if slot == 3:
            for copy in moves[2]:
                copy.wait_recv()
        if slot == 1:
            for copy in moves[1]:
                copy.wait_recv()
        owner = jnp.bitwise_xor(me, slot)
        for item in range(items):
            place = owner * items + item
            bias = bias_ref[place]
            stats = stat_ref[item] if slot == 0 else all_s[slot, item]
            for index in range(HEADS // 2):
                both = all_ref[slot, item, :, pair(index)]
                if slot == 0:
                    upstream = back_ref[item, :, pair(index)]
                else:
                    upstream = all_b[slot, item, :, pair(index)]
                keys = kv_ref[place, :, pair(index)]
                values = kv_ref[place, :, pair(index + HEADS // 2)]
                dq = dk = dv = None
                for half, mask in ((0, low), (1, high)):
                    head = 2 * index + half
                    query = both * mask
                    back = upstream * mask
                    scores = dot_nt(query, keys) + bias
                    probs = jnp.exp(scores - column(stats, head))
                    dprobs = dot_nt(back, values)
                    ds = (probs * (dprobs - column(stats, 8 + head))).astype(BF)
                    q_part = dot(ds, keys * mask)
                    k_part = dot_tn(ds, query)
                    v_part = dot_tn(probs.astype(BF), back)
                    dq = q_part if half == 0 else dq + q_part
                    dk = k_part if half == 0 else dk + k_part
                    dv = v_part if half == 0 else dv + v_part
                out_q[slot, item, :, pair(index)] = dq.astype(BF)
                dkv_ref[place, :, pair(index)] = dk.astype(BF)
                dkv_ref[place, :, pair(index + HEADS // 2)] = dv.astype(BF)
        if slot:
            copies.append(send(out_q.at[slot], in_q.at[slot], q_send.at[slot], q_recv.at[slot], slot))
            copies[-1].start()
    for move in moves:
        for copy in move:
            copy.wait_send()
    for copy in copies:
        copy.wait()
    for item in range(items):
        for index in range(HEADS // 2):
            total = out_q[0, item, :, pair(index)].astype(F32)
            for slot in (1, 2, 3):
                total += in_q[slot, item, :, pair(index)].astype(F32)
            dq_ref[item, :, pair(index)] = total.astype(BF)


def cross_bwd(all_queries, back, stats, keys_values, bias):
    items = back.shape[0]
    inner = HEADS * HEAD
    block = (4, items, ROWS, inner)
    flops = 4 * items * HEADS * ROWS * SPAN * 128 * 10
    return pl.pallas_call(
        functools.partial(cross_bwd_kernel, items),
        out_shape=(
            jax.ShapeDtypeStruct(keys_values.shape, BF),
            jax.ShapeDtypeStruct((items, ROWS, inner), BF),
        ),
        in_specs=[VMEM_SPEC] * 5,
        out_specs=(VMEM_SPEC,) * 2,
        scratch_shapes=[
            pltpu.VMEM(block, BF),
            pltpu.VMEM((4, items, ROWS, STATS), F32),
            pltpu.VMEM(block, BF),
            pltpu.VMEM(block, BF),
            pltpu.SemaphoreType.DMA((3,)),
            pltpu.SemaphoreType.DMA((3,)),
            pltpu.SemaphoreType.DMA((3,)),
            pltpu.SemaphoreType.DMA((3,)),
            pltpu.SemaphoreType.DMA((4,)),
            pltpu.SemaphoreType.DMA((4,)),
        ],
        compiler_params=pltpu.CompilerParams(
            collective_id=2, has_side_effects=True, vmem_limit_bytes=VMEM_CAP
        ),
        cost_estimate=pl.CostEstimate(
            flops=flops, bytes_accessed=12 * 1024 * 1024, transcendentals=flops // 1280
        ),
        name="cross_bwd",
    )(all_queries, back, stats, keys_values, bias)


CUBIC = 0.044715
ROOT = float(np.sqrt(2.0 / np.pi))


def strips(width, step):
    return [(start, min(step, width - start)) for start in range(0, width, step)]


def ffn_kernel(
    items, h_ref, up0_ref, up1_ref, up2_ref, up3_ref, gate_up_hbm, down_hbm,
    h_back_ref, near_ref, far_ref, grad_gu_hbm, grad_down_hbm,
    gate_up_ref, down_ref, h_all, u_all, hidden, two_back, h_part, y_part, h_in, y_in, gu_strip, down_strip,
    h_send, h_recv, d_send, d_recv, y_send, y_recv, load_sem, up_sem, store_sem,
):
    tokens, model = h_ref.shape
    rows = tokens // items
    units = down_ref.shape[0]
    loads = [
        pltpu.make_async_copy(gate_up_hbm, gate_up_ref, load_sem.at[0]),
        pltpu.make_async_copy(down_hbm, down_ref, load_sem.at[1]),
        pltpu.make_async_copy(up0_ref, u_all.at[0], load_sem.at[2]),
        pltpu.make_async_copy(up1_ref, u_all.at[1], load_sem.at[3]),
    ]
    for copy in loads:
        copy.start()
    ups = []
    for item in range(items):
        mine = pl.ds(item * rows, rows)
        for place, ref in enumerate((up2_ref, up3_ref)):
            ups.append(
                pltpu.make_async_copy(
                    ref.at[mine], u_all.at[2 + item, pl.ds(place * rows, rows)],
                    up_sem.at[item, place],
                )
            )
            ups[-1].start()
    greet("mem", (1, 2))
    h_to_core = send(h_ref, h_all.at[1], h_send.at[0], h_recv.at[0], 1)
    h_to_far, h_relay, d_pass, d_far, y_pass = [], [], [], [], []
    first, second = pl.ds(0, rows), pl.ds(rows, rows)
    for item in range(items):
        block, at = 2 + item, 1 + item
        h_to_far.append(
            send(h_ref.at[pl.ds(item * rows, rows)], h_all.at[block, first],
                 h_send.at[at], h_recv.at[at], 2)
        )
        h_relay.append(
            send(h_all.at[block, first], h_all.at[block, second],
                 h_send.at[at + items], h_recv.at[at + items], 1)
        )
        d_pass.append(
            send(h_part.at[block, second], h_in.at[1, pl.ds(item * rows, rows)],
                 d_send.at[at], d_recv.at[at], 1)
        )
        y_pass.append(
            send(y_part.at[block, second], y_in.at[1, pl.ds(item * rows, rows)],
                 y_send.at[at], y_recv.at[at], 1)
        )
        d_far.append(
            send(h_part.at[block, first], h_in.at[2, pl.ds(item * rows, rows)],
                 d_send.at[at + items], d_recv.at[at + items], 2)
        )
    d_near = send(h_part.at[1], h_in.at[0], d_send.at[0], d_recv.at[0], 1)
    y_near = send(y_part.at[1], y_in.at[0], y_send.at[0], y_recv.at[0], 1)
    for copy in h_to_far:
        copy.start()
    h_to_core.start()
    h_all[0] = h_ref[...]
    for copy in loads:
        copy.wait()
    for copy in ups:
        copy.wait()

    def give_back(item):
        mine = pl.ds(item * rows, rows)
        d_pass[item].wait_recv()
        h_part[2 + item, first, :] = (
            h_part[2 + item, first, :].astype(F32) + h_in[1, mine, :].astype(F32)
        ).astype(BF)
        d_far[item].start()

    def token_block(slot, carry):
        @pl.when(slot == 1)
        def _():
            h_to_core.wait_recv()

        @pl.when(slot == 2)
        def _():
            d_near.start()
            y_near.start()

        for item in range(items):

            @pl.when(slot == 2 + item)
            def _(item=item):
                if item:
                    d_pass[item - 1].start()
                    y_pass[item - 1].start()
                h_relay[item].wait_recv()

        for item in range(items):

            @pl.when(slot == 1 + item)
            def _(item=item):
                h_to_far[item].wait_recv()
                h_relay[item].start()

        def units_block(block, inside):
            pairs = pl.ds(pl.multiple_of(block * 256, 256), 256)
            ones = pl.ds(pl.multiple_of(block * 128, 128), 128)
            both = dot(h_all[slot], gate_up_ref[:, pairs])
            back = dot_nt(u_all[slot], down_ref[ones, :]).astype(BF).astype(F32)
            gate, up = both[:, :128], both[:, 128:]
            square = gate * gate
            bend = jnp.tanh(ROOT * gate * (1.0 + CUBIC * square))
            share = 0.5 * (1.0 + bend)
            active = gate * share
            slope = share + 0.5 * gate * (1.0 - bend * bend) * (
                ROOT * (1.0 + 3.0 * CUBIC * square)
            )
            hidden[slot, :, ones] = (active * up).astype(BF)
            two_back[slot, :, pairs] = jnp.concatenate(
                [(back * up * slope).astype(BF), (back * active).astype(BF)], axis=1
            )
            return inside

        lax.fori_loop(0, units // 128, units_block, 0)
        for start, width in strips(model, 256):
            part = slice(start, start + width)
            h_part[slot, :, part] = dot_nt(two_back[slot], gate_up_ref[part, :]).astype(BF)
        for item in range(items - 1):

            @pl.when(slot == 3 + item)
            def _(item=item):
                give_back(item)

        for start, width in strips(model, 256):
            part = slice(start, start + width)
            y_part[slot, :, part] = dot(hidden[slot], down_ref[:, part]).astype(BF)
        return carry

    lax.fori_loop(0, 2 + items, token_block, 0)
    d_pass[-1].start()
    y_pass[-1].start()
    count = (2 + items) * tokens
    stores = []

    def store(value, strip, hbm, start, width):
        number = len(stores)
        if number >= 2:
            stores[number - 2].wait()
        strip[number % 2, :width, :] = value
        stores.append(
            pltpu.make_async_copy(
                strip.at[number % 2, pl.ds(0, width)],
                hbm.at[pl.ds(start, width)],
                store_sem.at[number],
            )
        )
        stores[-1].start()

    for start, width in strips(model, 256):
        part = slice(start, start + width)
        value = dot_tn(
            h_all[:, :, part].reshape(count, width), two_back[...].reshape(count, 2 * units)
        )
        store(value.astype(BF), gu_strip, grad_gu_hbm, start, width)
        if start == 0:
            give_back(items - 1)
    for start, width in strips(units, 256):
        part = slice(start, start + width)
        value = dot_tn(
            hidden[:, :, part].reshape(count, width), u_all[...].reshape(count, model)
        )
        store(value.astype(BF), down_strip, grad_down_hbm, start, width)
    for item in range(items):
        mine = pl.ds(item * rows, rows)
        y_pass[item].wait_recv()
        far_ref[mine, :] = (
            y_part[2 + item, first, :].astype(F32) + y_in[1, mine, :].astype(F32)
        ).astype(BF)
    y_near.wait_recv()
    near_ref[...] = (y_part[0].astype(F32) + y_in[0].astype(F32)).astype(BF)
    d_near.wait_recv()
    for copy in d_far:
        copy.wait_recv()
    h_back_ref[...] = (
        h_part[0].astype(F32) + h_in[0].astype(F32) + h_in[2].astype(F32)
    )
    for copy in stores[-2:]:
        copy.wait()
    for copy in (h_to_core, d_near, y_near, *h_to_far, *h_relay, *d_pass, *y_pass, *d_far):
        copy.wait_send()


def ffn(h3, upstreams, gate_up, down, items):
    tokens, model = h3.shape
    units = down.shape[0]
    every = (2 + items, tokens, model)
    flops = (2 + items) * tokens * model * units * 18
    grads = len(strips(model, 256)) + len(strips(units, 256))
    return pl.pallas_call(
        functools.partial(ffn_kernel, items),
        out_shape=(
            jax.ShapeDtypeStruct((tokens, model), F32),
            jax.ShapeDtypeStruct((tokens, model), BF),
            jax.ShapeDtypeStruct((tokens, model), BF),
            jax.ShapeDtypeStruct((model, 2 * units), BF),
            jax.ShapeDtypeStruct((units, model), BF),
        ),
        in_specs=[VMEM_SPEC] + [ANY_SPEC] * 6,
        out_specs=(VMEM_SPEC,) * 3 + (ANY_SPEC,) * 2,
        scratch_shapes=[
            pltpu.VMEM((model, 2 * units), BF),
            pltpu.VMEM((units, model), BF),
            pltpu.VMEM(every, BF),
            pltpu.VMEM(every, BF),
            pltpu.VMEM((2 + items, tokens, units), BF),
            pltpu.VMEM((2 + items, tokens, 2 * units), BF),
            pltpu.VMEM(every, BF),
            pltpu.VMEM(every, BF),
            pltpu.VMEM((3, tokens, model), BF),
            pltpu.VMEM((2, tokens, model), BF),
            pltpu.VMEM((2, 256, 2 * units), BF),
            pltpu.VMEM((2, 256, model), BF),
        ]
        + [pltpu.SemaphoreType.DMA((1 + 2 * items,))] * 4
        + [pltpu.SemaphoreType.DMA((1 + items,))] * 2
        + [
            pltpu.SemaphoreType.DMA((4,)),
            pltpu.SemaphoreType.DMA((items, 2)),
            pltpu.SemaphoreType.DMA((grads,)),
        ],
        compiler_params=pltpu.CompilerParams(
            collective_id=3, has_side_effects=True, vmem_limit_bytes=FFN_CAP
        ),
        cost_estimate=pl.CostEstimate(
            flops=flops, bytes_accessed=32 * 1024 * 1024, transcendentals=4 * tokens * units
        ),
        name="feed_forward",
    )(h3, *upstreams, gate_up, down)


def peer_copy(src, dst, send_sem, recv_sem, tgt=None, mem=None):
    where = {}
    if tgt is not None:
        where["tgt"] = tgt
    if mem is not None:
        where["mem"] = mem
    return pltpu.make_async_remote_copy(
        src_ref=src, dst_ref=dst, send_sem=send_sem, recv_sem=recv_sem,
        device_id=where, device_id_type=MESH,
    )


def greet_all(mem, tgt):
    barrier = pltpu.get_barrier_semaphore()
    for offset in (1, 2, 3):
        pl.semaphore_signal(
            barrier, inc=1, device_id={"mem": jnp.bitwise_xor(mem, offset)}, device_id_type=MESH
        )
    for offset in (1, 2, 4, 6):
        pl.semaphore_signal(
            barrier, inc=1, device_id={"tgt": jnp.bitwise_xor(tgt, offset)}, device_id_type=MESH
        )
    pl.semaphore_wait(barrier, 7)


FIRST = (1, 2, 4, 6)
PASSED = (3, 5, 7)


def gather_kernel(
    self_q, self_k, self_v, cross_q, cross_k, cross_v, self_o, cross_o,
    qkv_out, kv_out, cq_out, so_out, co_out,
    t_send, t_recv, x_send, x_recv, c_send, c_recv, r_send, r_recv, own_sem,
):
    mem = lax.axis_index("mem")
    tgt = lax.axis_index("tgt")
    inner = HEADS * HEAD

    def part(out, index):
        return lambda place: out.at[place, :, index * inner : (index + 1) * inner]

    def whole(out):
        return lambda place: out.at[place]

    groups = (
        ((self_q, part(qkv_out, 0)), (self_k, part(qkv_out, 1))),
        ((self_v, part(qkv_out, 2)), (cross_q, part(cq_out, 0))),
        ((cross_k, part(kv_out, 0)), (cross_v, part(kv_out, 1))),
        ((self_o, whole(so_out)), (cross_o, whole(co_out))),
    )
    greet_all(mem, tgt)
    near = jnp.bitwise_xor(mem, 1)
    far = jnp.bitwise_xor(mem, 2)

    def over_tgt(member, number, step, offset):
        src, dst = member
        if step < 4:
            return peer_copy(
                src, dst(tgt), t_send.at[step, number], t_recv.at[step, number],
                tgt=jnp.bitwise_xor(tgt, offset),
            )
        place = jnp.bitwise_xor(tgt, offset - 1)
        return peer_copy(
            dst(place), dst(place), t_send.at[step, number], t_recv.at[step, number],
            tgt=jnp.bitwise_xor(tgt, 1),
        )

    def over_far(member, number, step, offset):
        dst = member[1](jnp.bitwise_xor(tgt, offset))
        return peer_copy(dst, dst, x_send.at[step, number], x_recv.at[step, number], mem=far)

    def over_near(member, number, step, offset):
        dst = member[1](jnp.bitwise_xor(tgt, offset))
        return peer_copy(dst, dst, c_send.at[step, number], c_recv.at[step, number], mem=near)

    def relay(member, number, step, offset):
        dst = member[1](jnp.bitwise_xor(tgt, offset))
        return peer_copy(dst, dst, r_send.at[step, number], r_recv.at[step, number], mem=near)

    steps = list(enumerate(FIRST + PASSED))
    for index, group in enumerate(groups):

        @pl.when(mem == index)
        def _(index=index, group=group):
            members = list(enumerate(group))
            far_members = list(enumerate(groups[index ^ 2]))
            near_members = list(enumerate(groups[index ^ 1]))
            last_members = list(enumerate(groups[index ^ 3]))
            extra = [(2, far_members[0][1])] if index % 2 else []
            far_sent = members[1:] if index % 2 else members
            far_got = far_members[1:] if index % 2 else far_members
            for step, offset in steps[:4]:
                for number, member in members + extra:
                    over_tgt(member, number, step, offset).start()
            own = []
            for place, (src, dst) in enumerate(member for all_of in groups for member in all_of):
                own.append(pltpu.make_async_copy(src, dst(tgt), own_sem.at[place]))
                own[-1].start()
            for step, offset in steps:
                for number, member in members:
                    over_tgt(member, number, step, offset).wait_recv()
                    if 0 < step < 4:
                        over_tgt(member, number, step + 3, offset + 1).start()
                    if (number, member) in far_sent:
                        over_far(member, number, step, offset).start()
                    over_near(member, number, step, offset).start()
                for number, member in extra:
                    over_tgt(member, number, step, offset).wait_recv()
                    if 0 < step < 4:
                        over_tgt(member, number, step + 3, offset + 1).start()
                    relay(member, 0, step, offset).start()
            for step, offset in steps:
                for number, member in far_got:
                    over_far(member, number, step, offset).wait_recv()
                    relay(member, number, step, offset).start()
            for step, offset in steps:
                for number, member in near_members:
                    over_near(member, number, step, offset).wait_recv()
                for number, member in last_members:
                    relay(member, number, step, offset).wait_recv()
                for number, member in members + extra:
                    over_tgt(member, number, step, offset).wait_send()
                for number, member in far_sent:
                    over_far(member, number, step, offset).wait_send()
                for number, member in members:
                    over_near(member, number, step, offset).wait_send()
                for number, member in far_members:
                    relay(member, number, step, offset).wait_send()
            for copy in own:
                copy.wait()


def gather_weights(weights):
    tgts = lax.axis_size("tgt")
    rows, inner = weights[0].shape
    o_rows, model = weights[-1].shape

    def out(columns, height=rows):
        return jax.ShapeDtypeStruct((tgts, height, columns), BF)

    shapes = (out(3 * inner), out(2 * inner), out(inner), out(model, o_rows), out(model, o_rows))
    sems = [pltpu.SemaphoreType.DMA((7, 3))] * 2 + [pltpu.SemaphoreType.DMA((7, 2))] * 6
    return pl.pallas_call(
        gather_kernel,
        out_shape=shapes,
        in_specs=[ANY_SPEC] * 8,
        out_specs=(ANY_SPEC,) * 5,
        scratch_shapes=sems + [pltpu.SemaphoreType.DMA((8,))],
        compiler_params=pltpu.CompilerParams(collective_id=4, has_side_effects=True),
        cost_estimate=pl.CostEstimate(
            flops=0, bytes_accessed=150 * 1024 * 1024, transcendentals=0
        ),
        name="gather_weights",
    )(*weights)


TURNS = (7, 6, 5, 4, 3, 2, 1, 0)


def reduce_kernel(
    qkv_ref, kv_ref, cq_ref, so_ref, co_ref, small_ref, units_ref,
    q_out, k_out, v_out, cq_out, ck_out, cv_out, so_out, co_out, small_out, units_out,
    small_in, s_send, s_recv, u_send, u_recv, u_own,
    wide_in, tall_in, wide_x, tall_x, wide_y, tall_y, wide_z, tall_z, wide_e, tall_e,
    a_send, a_recv, b_send, b_recv, x_send, x_recv, y_send, y_recv, z_send, z_recv,
    e_send, e_recv,
):
    mem = lax.axis_index("mem")
    tgt = lax.axis_index("tgt")
    inner = HEADS * HEAD

    def part(ref, index):
        return lambda place: ref.at[place, :, index * inner : (index + 1) * inner]

    def whole(ref):
        return lambda place: ref.at[place]

    wide = (wide_in, wide_x, wide_y, wide_z, wide_e)
    tall = (tall_in, tall_x, tall_y, tall_z, tall_e)
    groups = (
        ((part(qkv_ref, 0), q_out, wide), (part(qkv_ref, 1), k_out, wide)),
        ((part(qkv_ref, 2), v_out, wide), (part(cq_ref, 0), cq_out, wide)),
        ((part(kv_ref, 0), ck_out, wide), (part(kv_ref, 1), cv_out, wide)),
        ((whole(so_ref), so_out, tall), (whole(co_ref), co_out, tall)),
    )
    greet_all(mem, tgt)
    near = jnp.bitwise_xor(mem, 1)
    far = jnp.bitwise_xor(mem, 2)

    def to_near(member, number, step, lane):
        place = jnp.bitwise_xor(tgt, TURNS[step])
        send_sems, recv_sems = ((a_send, a_recv), (b_send, b_recv))[lane]
        return peer_copy(
            member[0](place), member[2][0].at[lane, step, number],
            send_sems.at[step, number], recv_sems.at[step, number], mem=near,
        )

    def to_far(member, number, step):
        buffer = member[2][1]
        return peer_copy(
            buffer.at[0, step, number], buffer.at[1, step, number],
            x_send.at[step, number], x_recv.at[step, number], mem=far,
        )

    def to_side(member, number, turn):
        buffer = member[2][2]
        return peer_copy(
            buffer.at[0, turn, number], buffer.at[1, turn, number],
            y_send.at[turn, number], y_recv.at[turn, number], tgt=jnp.bitwise_xor(tgt, 1),
        )

    def to_owner(member, number, turn):
        buffer = member[2][3]
        return peer_copy(
            buffer.at[0, turn, number], buffer.at[1, turn, number],
            z_send.at[turn, number], z_recv.at[turn, number],
            tgt=jnp.bitwise_xor(tgt, TURNS[2 * turn + 1]),
        )

    def to_all(member, number, lane, peer):
        buffer = member[2][4]
        return peer_copy(
            buffer.at[2 if lane == 2 else 0, number],
            buffer.at[(1, 2, 3)[lane], number],
            e_send.at[lane, number], e_recv.at[lane, number], mem=peer,
        )

    z_place = tgt // 2
    y_place = tgt % 2
    small_mem = [
        peer_copy(small_in.at[mem], small_in.at[mem], s_send.at[offset], s_recv.at[offset],
                  mem=jnp.bitwise_xor(mem, offset))
        for offset in (1, 2, 3)
    ]
    small_y = peer_copy(small_in.at[4 + y_place], small_in.at[4 + y_place], s_send.at[0],
                        s_recv.at[0], tgt=jnp.bitwise_xor(tgt, 1))
    small_z = [
        peer_copy(small_in.at[6 + z_place], small_in.at[6 + z_place], s_send.at[3 + offset],
                  s_recv.at[3 + offset], tgt=jnp.bitwise_xor(tgt, 2 * offset))
        for offset in (1, 2, 3)
    ]
    small_in[mem] = small_ref[...]
    for move in small_mem:
        move.start()

    share_far = peer_copy(units_ref, units_out.at[mem], u_send.at[0], u_recv.at[0], mem=far)
    share_near = peer_copy(units_ref, units_out.at[mem], u_send.at[1], u_recv.at[1], mem=near)
    share_on = peer_copy(units_out.at[far], units_out.at[far], u_send.at[2], u_recv.at[2], mem=near)
    share_own = pltpu.make_async_copy(units_ref, units_out.at[mem], u_own)
    share_own.start()

    for index, group in enumerate(groups):

        @pl.when(mem == index)
        def _(index=index, group=group):
            mine = list(enumerate(group))
            near_group = list(enumerate(groups[index ^ 1]))
            far_group = list(enumerate(groups[index ^ 2]))
            last_group = list(enumerate(groups[index ^ 3]))
            steps = range(len(TURNS))
            for step in steps:
                for number, member in last_group:
                    to_near(member, number, step, 1).start()
                for number, member in near_group:
                    to_near(member, number, step, 0).start()
            for step in steps:
                place = jnp.bitwise_xor(tgt, TURNS[step])
                for number, member in far_group:
                    to_near(member, number, step, 1).wait_recv()
                    member[2][1][0, step, number] = (
                        member[0](place)[...].astype(F32)
                        + member[2][0][1, step, number].astype(F32)
                    ).astype(BF)
                    to_far(member, number, step).start()
            share_far.start()
            share_near.start()
            for move in small_mem:
                move.wait_recv()
            small_in[4 + y_place] = (small_in[0] + small_in[1]) + (small_in[2] + small_in[3])
            small_y.start()
            def mem_sum(member, number, step):
                to_near(member, number, step, 0).wait_recv()
                to_far(member, number, step).wait_recv()
                return (
                    member[0](jnp.bitwise_xor(tgt, TURNS[step]))[...].astype(F32)
                    + member[2][0][0, step, number].astype(F32)
                    + member[2][1][1, step, number].astype(F32)
                )

            def for_side(turn):
                for number, member in mine:
                    member[2][2][0, turn, number] = mem_sum(member, number, 2 * turn).astype(BF)
                    to_side(member, number, turn).start()

            for_side(0)
            small_y.wait_recv()
            small_in[6 + z_place] = small_in[4] + small_in[5]
            for move in small_z:
                move.start()
            for_side(1)
            for_side(2)
            for_side(3)
            for turn in range(4):
                for number, member in mine:
                    total = mem_sum(member, number, 2 * turn + 1)
                    to_side(member, number, turn).wait_recv()
                    total = total + member[2][2][1, turn, number].astype(F32)
                    if turn < 3:
                        member[2][3][0, turn, number] = total.astype(BF)
                        to_owner(member, number, turn).start()
                        continue
                    member[2][4][0, number] = total.astype(BF)
            for number, member in mine:
                total = member[2][4][0, number].astype(F32)
                for other in range(3):
                    to_owner(member, number, other).wait_recv()
                    total = total + member[2][3][1, other, number].astype(F32)
                member[2][4][0, number] = total.astype(BF)
                to_all(member, number, 1, far).start()
                to_all(member, number, 0, near).start()
                member[1][...] = member[2][4][0, number]
            for number, member in far_group:
                to_all(member, number, 1, far).wait_recv()
                to_all(member, number, 2, near).start()
                member[1][...] = member[2][4][2, number]
            for number, member in near_group:
                to_all(member, number, 0, near).wait_recv()
                member[1][...] = member[2][4][1, number]
            for number, member in last_group:
                to_all(member, number, 2, near).wait_recv()
                member[1][...] = member[2][4][3, number]
            for move in small_z:
                move.wait_recv()
            small_out[...] = (small_in[6] + small_in[7]) + (small_in[8] + small_in[9])
            share_far.wait_recv()
            share_on.start()
            share_near.wait_recv()
            share_on.wait_recv()
            share_own.wait()
            for move in (*small_mem, small_y, *small_z, share_far, share_near, share_on):
                move.wait_send()
            for step in steps:
                for number, member in last_group:
                    to_near(member, number, step, 1).wait_send()
                for number, member in near_group:
                    to_near(member, number, step, 0).wait_send()
                for number, member in far_group:
                    to_far(member, number, step).wait_send()
            for number, member in mine:
                for turn in range(4):
                    to_side(member, number, turn).wait_send()
                for turn in range(3):
                    to_owner(member, number, turn).wait_send()
                to_all(member, number, 0, near).wait_send()
                to_all(member, number, 1, far).wait_send()
            for number, member in far_group:
                to_all(member, number, 2, near).wait_send()


def reduce_weights(d_qkv, d_kv, d_cq, d_so, d_co, small, units):
    rows, inner = d_cq.shape[1:]
    o_rows, model = d_so.shape[1:]
    wide, tall = (rows, inner), (o_rows, model)
    scratch = []
    for lead in ((2, 8, 2), (2, 8, 2), (2, 4, 2), (2, 3, 2), (4, 2)):
        scratch += [pltpu.VMEM(lead + wide, BF), pltpu.VMEM(lead + tall, BF)]
    sems = []
    for count in (8, 8, 8, 4, 3, 3):
        sems += [pltpu.SemaphoreType.DMA((count, 2))] * 2
    return pl.pallas_call(
        reduce_kernel,
        out_shape=tuple(jax.ShapeDtypeStruct(wide, BF) for _ in range(6))
        + tuple(jax.ShapeDtypeStruct(tall, BF) for _ in range(2))
        + (
            jax.ShapeDtypeStruct(small.shape, F32),
            jax.ShapeDtypeStruct((4,) + units.shape, BF),
        ),
        in_specs=[VMEM_SPEC] * 6 + [ANY_SPEC],
        out_specs=(VMEM_SPEC,) * 9 + (ANY_SPEC,),
        scratch_shapes=[pltpu.VMEM((10,) + small.shape, F32)]
        + [pltpu.SemaphoreType.DMA((7,))] * 2
        + [pltpu.SemaphoreType.DMA((3,))] * 2
        + [pltpu.SemaphoreType.DMA]
        + scratch
        + sems,
        compiler_params=pltpu.CompilerParams(
            collective_id=5, has_side_effects=True, vmem_limit_bytes=VMEM_CAP
        ),
        cost_estimate=pl.CostEstimate(
            flops=0, bytes_accessed=150 * 1024 * 1024, transcendentals=0
        ),
        name="reduce_weights",
    )(d_qkv, d_kv, d_cq, d_so, d_co, small, units)


def pick_kernel(tgts, groups, gate_ref, up_ref, out_ref):
    mem = lax.axis_index("mem")
    shard = gate_ref.shape[1] // tgts
    piece = shard // groups

    for group in range(groups):

        @pl.when(mem == group)
        def _(group=group):
            for number, ref in enumerate((gate_ref, up_ref)):
                parts = []
                for place in range(tgts):
                    start = place * shard + group * piece
                    parts.append(ref[:, start : start + piece].astype(F32))
                quarter = jnp.concatenate(parts, axis=1).astype(BF)
                for block in range(quarter.shape[1] // 128):
                    start = block * 256 + number * 128
                    out_ref[:, start : start + 128] = quarter[:, block * 128 : block * 128 + 128]


def pick_units(gate, up):
    groups, tgts = lax.axis_size("mem"), lax.axis_size("tgt")
    rows, units = gate.shape
    return pl.pallas_call(
        functools.partial(pick_kernel, tgts, groups),
        out_shape=jax.ShapeDtypeStruct((rows, 2 * units // groups), BF),
        in_specs=[VMEM_SPEC] * 2,
        out_specs=VMEM_SPEC,
        compiler_params=pltpu.CompilerParams(vmem_limit_bytes=VMEM_CAP),
        name="pick_units",
    )(gate, up)


def place_kernel(tgts, groups, parts_ref, down_parts_ref, *refs):
    count = (len(refs) - 3) // 2
    gate_ref, up_ref, down_ref = refs[count : count + 3]
    for src, dst in zip(refs[:count], refs[count + 3 :]):
        dst[...] = src[...].astype(F32)
    height = down_parts_ref.shape[1]
    for group in range(groups):
        down_ref[group * height : (group + 1) * height, :] = down_parts_ref[group].astype(F32)
    units = gate_ref.shape[1]
    piece = units // tgts // groups
    for number, ref in enumerate((gate_ref, up_ref)):
        quarters = []
        for group in range(groups):
            blocks = [
                parts_ref[group, :, start : start + 128]
                for start in range(number * 128, 2 * units // groups, 256)
            ]
            quarters.append(jnp.concatenate(blocks, axis=1).astype(F32))
        ref[...] = jnp.concatenate(
            [
                quarters[group][:, place * piece : (place + 1) * piece]
                for place in range(tgts)
                for group in range(groups)
            ],
            axis=1,
        )


def place_units(parts, down_parts, sums):
    groups, tgts = lax.axis_size("mem"), lax.axis_size("tgt")
    rows, columns = parts.shape[1:]
    wide = jax.ShapeDtypeStruct((rows, groups * columns // 2), F32)
    down = jax.ShapeDtypeStruct((groups * down_parts.shape[1], down_parts.shape[2]), F32)
    shapes = (wide, wide, down) + tuple(jax.ShapeDtypeStruct(part.shape, F32) for part in sums)
    return pl.pallas_call(
        functools.partial(place_kernel, tgts, groups),
        out_shape=shapes,
        in_specs=[VMEM_SPEC] * (2 + len(sums)),
        out_specs=(VMEM_SPEC,) * len(shapes),
        compiler_params=pltpu.CompilerParams(vmem_limit_bytes=VMEM_CAP),
        name="place_units",
    )(parts, down_parts, *sums)


def share_kernel(src, out, sends, recvs, own_sem):
    mem = lax.axis_index("mem")
    greet("mem", (1, 2))
    near = jnp.bitwise_xor(mem, 1)
    far = jnp.bitwise_xor(mem, 2)
    to_far = peer_copy(src, out.at[mem], sends.at[0], recvs.at[0], mem=far)
    to_near = peer_copy(src, out.at[mem], sends.at[1], recvs.at[1], mem=near)
    pass_on = peer_copy(out.at[far], out.at[far], sends.at[2], recvs.at[2], mem=near)
    to_far.start()
    to_near.start()
    own = pltpu.make_async_copy(src, out.at[mem], own_sem)
    own.start()
    to_far.wait_recv()
    pass_on.start()
    to_near.wait_recv()
    pass_on.wait_recv()
    for copy in (to_far, to_near, pass_on):
        copy.wait_send()
    own.wait()


def share(value):
    groups = lax.axis_size("mem")
    return pl.pallas_call(
        share_kernel,
        out_shape=jax.ShapeDtypeStruct((groups,) + value.shape, BF),
        in_specs=[ANY_SPEC],
        out_specs=ANY_SPEC,
        scratch_shapes=[pltpu.SemaphoreType.DMA((3,))] * 2 + [pltpu.SemaphoreType.DMA],
        compiler_params=pltpu.CompilerParams(collective_id=6, has_side_effects=True),
        cost_estimate=pl.CostEstimate(
            flops=0, bytes_accessed=30 * 1024 * 1024, transcendentals=0
        ),
        name="share_sums",
    )(value)


def over_mem(value, offset):
    return lax.ppermute(value, "mem", [(i, i ^ offset) for i in range(4)])


def gather_mem(value):
    far = over_mem(value, 2)
    near = over_mem(value, 1)
    return value, near, far, over_mem(far, 1)


def gather_tgt(shard):
    return lax.all_gather(shard, "tgt", axis=0, tiled=True)


def scatter_tgt(partial):
    return lax.psum_scatter(partial, "tgt", scatter_dimension=0, tiled=True)


def in_tiles(value):
    rows, columns = value.shape
    value = jnp.pad(value, ((0, 0), (0, -columns % 128)))
    return value.reshape(rows // 8, 8, -1, 128).swapaxes(1, 2).reshape(-1, 8, 128)


def from_tiles(tiles, rows, columns):
    shards = tiles.shape[0]
    tiles = tiles.reshape(shards * rows // 8, -1, 8, 128).swapaxes(1, 2)
    return tiles.reshape(shards * rows, -1)[:, :columns]


def gather_units(gate_up, down):
    if gate_up.shape[0] % 8 or down.shape[0] % 8:
        return gather_tgt(gate_up), gather_tgt(down)
    tiles = in_tiles(gate_up)
    both = lax.all_gather(jnp.concatenate([tiles, in_tiles(down)]), "tgt", axis=0)
    return (
        from_tiles(both[:, : tiles.shape[0]], *gate_up.shape),
        from_tiles(both[:, tiles.shape[0] :], *down.shape),
    )


def attention_weights(weights):
    if lax.axis_size("tgt") == 8:
        return gather_weights(weights)
    parts = [lax.all_gather(weight, "tgt", axis=0) for weight in weights]
    return (
        jnp.concatenate(parts[:3], axis=-1),
        jnp.concatenate(parts[4:6], axis=-1),
        parts[3],
        parts[6],
        parts[7],
    )


def weight_sums(partials, small, units):
    if lax.axis_size("tgt") == 8:
        return reduce_weights(*partials, small, units)
    inner = HEADS * HEAD
    totals = [
        lax.psum_scatter(partial, "tgt", scatter_dimension=0, tiled=False) for partial in partials
    ]
    qkv, kv, cq, so, co = lax.psum(totals, "mem")
    return (
        qkv[:, :inner], qkv[:, inner : 2 * inner], qkv[:, 2 * inner :], cq,
        kv[:, :inner], kv[:, inner:], so, co, lax.psum(small, ("tgt", "mem")),
        lax.all_gather(units, "mem", axis=0),
    )


def on_device(
    target, memory, lengths, gate_bias, out_grad, gain_self, gain_cross, gain_ffn, rel_table,
    self_q, self_k, self_v, self_o, cross_q, cross_k, cross_v, cross_o, ffn_gate, ffn_up, ffn_down,
):
    groups = lax.axis_size("mem")
    tgts = lax.axis_size("tgt")
    mem_index = lax.axis_index("mem")
    items, seq, model = target.shape
    all_items, positions_dev, _ = memory.shape
    inner = HEADS * HEAD
    tokens = items * ROWS
    shard_in = ffn_gate.shape[0]
    hidden_shard = ffn_down.shape[0]
    piece = hidden_shard // groups
    quarter = tgts * piece

    def padded(value):
        return jnp.pad(value, ((0, 0), (0, ROWS - seq), (0, 0))).reshape(tokens, model)

    def trimmed(value):
        return value.reshape(items, ROWS, model)[:, :seq]

    norm_self = gain_self.astype(F32)
    norm_cross = gain_cross.astype(F32)
    norm_ffn = gain_ffn.astype(F32)
    onehot = jnp.asarray(distance_onehot())
    base = jnp.pad(
        lax.dot_general(rel_table, onehot, TN, precision=HIGH), ((0, 2), (0, 0))
    )
    positions = mem_index * positions_dev + jnp.arange(positions_dev)
    bias = jnp.where(positions[None, :] < lengths[:, None], gate_bias, NEG)[:, None, :]

    self_w, cross_kv_w, cross_q_w, self_o_w, cross_o_w = (
        weight.reshape(-1, weight.shape[-1])
        for weight in attention_weights(
            (self_q, self_k, self_v, cross_q, cross_k, cross_v, self_o, cross_o)
        )
    )
    gate_up = pick_units(ffn_gate, ffn_up)
    down = lax.dynamic_slice_in_dim(ffn_down, mem_index * piece, piece, axis=0)
    gate_up, down = gather_units(gate_up, down)

    inputs = padded(target).astype(F32)
    upstream_low = padded(out_grad)
    late, self_w = lax.optimization_barrier((upstream_low, self_w))
    upstreams = gather_mem(late)

    h1 = (inputs * rms_scale(inputs) * norm_self).astype(BF)
    qkv = dot(h1, self_w).astype(BF).reshape(items, ROWS, 3 * inner)
    att = self_fwd(qkv, base).reshape(tokens, inner)
    y1 = inputs + dot(att, self_o_w)
    h2 = (y1 * rms_scale(y1) * norm_cross).astype(BF)
    cq = dot(h2, cross_q_w).astype(BF).reshape(items, ROWS, inner)
    ckv = jnp.einsum(
        "npd,dc->npc", memory, cross_kv_w, preferred_element_type=F32
    ).astype(BF)
    all_queries, catt, lse = cross_fwd(cq, ckv, bias)
    catt = catt.reshape(tokens, inner)
    y2 = y1 + dot(catt, cross_o_w)
    h3 = (y2 * rms_scale(y2) * norm_ffn).astype(BF)

    h3_back, out_near, out_far, grad_gate_up, grad_down = ffn(h3, upstreams, gate_up, down, items)
    out_sum = over_mem(out_far, 2)
    grad_gate_up = scatter_tgt(grad_gate_up)
    dx, grad_norm_ffn = rms_back(y2, norm_ffn, h3_back)
    dy2 = upstream_low.astype(F32) + dx
    e2 = dy2.astype(BF)
    grad_cross_o = dot_tn(catt, e2)
    dcatt = dot_nt(e2, cross_o_w).astype(BF)
    delta = jnp.sum(
        (dcatt.astype(F32) * catt.astype(F32)).reshape(tokens, HEADS, HEAD), axis=-1
    ).reshape(items, ROWS, HEADS)
    stats = jnp.concatenate(
        [lse[:, :, :8], delta, jnp.zeros((items, ROWS, STATS - 8 - HEADS), F32)], axis=-1
    )
    dckv, dcq = cross_bwd(
        all_queries, dcatt.reshape(items, ROWS, inner), stats, ckv, bias
    )
    y2_late, grad_down, dcq = lax.optimization_barrier((y2, grad_down, dcq))
    grad_down = scatter_tgt(grad_down)
    layer_out = trimmed(
        (y2_late + out_near.astype(F32) + out_sum.astype(F32)).astype(BF)
    )
    dcq = dcq.reshape(tokens, inner)
    grad_cross_kv = jnp.einsum("npd,npc->dc", memory, dckv, preferred_element_type=F32)
    memory_grad = jnp.einsum(
        "npc,dc->npd", dckv, cross_kv_w, preferred_element_type=F32
    ).astype(BF)
    grad_cross_q = dot_tn(h2, dcq)
    dx, grad_norm_cross = rms_back(y1, norm_cross, dot_nt(dcq, cross_q_w))
    dy1 = dy2 + dx
    e1 = dy1.astype(BF)
    grad_self_o = dot_tn(att, e1)
    datt = dot_nt(e1, self_o_w).astype(BF).reshape(items, ROWS, inner)
    dqkv, diag = self_bwd(qkv, datt, base)
    dqkv = dqkv.reshape(tokens, 3 * inner)
    grad_self = dot_tn(h1, dqkv)
    dx, grad_norm_self = rms_back(inputs, norm_self, dot_nt(dqkv, self_w))
    target_grad = trimmed((dy1 + dx).astype(BF))
    table = lax.dot_general(
        onehot, diag[:HEADS], NT, precision=HIGH
    )

    small = jnp.concatenate(
        [grad_norm_self, grad_norm_cross, grad_norm_ffn, table.reshape(-1)]
    )
    *sums, small, grad_gate_up = weight_sums(
        tuple(
            partial.astype(BF).reshape(tgts, -1, partial.shape[-1])
            for partial in (grad_self, grad_cross_kv, grad_cross_q, grad_self_o, grad_cross_o)
        ),
        jnp.pad(small, (0, -small.size % 1024)).reshape(-1, 128),
        grad_gate_up,
    )
    grad_down, small = lax.optimization_barrier((grad_down, small))
    grad_down = share(grad_down)
    grad_gate, grad_up, grad_down, *columns = place_units(grad_gate_up, grad_down, sums)
    small = small.reshape(-1)
    norms = [small[start : start + model] for start in range(0, 3 * model, model)]
    table = small[3 * model : 3 * model + table.size].reshape(table.shape)
    return (
        layer_out,
        target_grad,
        memory_grad,
        *norms,
        table,
        columns[0],
        columns[1],
        columns[2],
        columns[6],
        columns[3],
        columns[4],
        columns[5],
        columns[7],
        grad_gate,
        grad_up,
        grad_down,
    )


def solution(mesh):
    owned = P(("tgt", "mem"), None, None)
    held = P("tgt", "mem", None)
    rows = P("tgt", None)
    return jax.shard_map(
        on_device,
        mesh=mesh,
        in_specs=(owned, held, P("tgt"), P("tgt", "mem"), owned, P(), P(), P(), P()) + (rows,) * 11,
        out_specs=(owned, owned, held, P(), P(), P(), P()) + (rows,) * 11,
        check_vma=False,
    )
```

```python
import functools

import jax
import jax.numpy as jnp
import numpy as np
from jax import lax
from jax.experimental import pallas as pl
from jax.experimental.pallas import tpu as pltpu
from jax.sharding import PartitionSpec as P

HEADS = 6
HEAD = 64
BUCKETS = 32
MAX_DIST = 128
ROWS = 192
SPAN = 256
STATS = 128

EPS = 1e-06
NEG = -1e30
HIGH = lax.Precision.HIGHEST
BF = jnp.bfloat16
F32 = jnp.float32
MESH = pl.DeviceIdType.MESH
NT = (((1,), (1,)), ((), ()))
TN = (((0,), (0,)), ((), ()))
VMEM_SPEC = pl.BlockSpec(memory_space=pltpu.VMEM)
ANY_SPEC = pl.BlockSpec(memory_space=pl.ANY)
VMEM_CAP = 56 * 1024 * 1024
FFN_CAP = 62 * 1024 * 1024


def distance_onehot():
    distance = (SPAN - np.arange(SPAN)) % SPAN
    exact_max = BUCKETS // 2
    scaled = (
        np.log(np.maximum(distance, 1) / exact_max)
        / np.log(MAX_DIST / exact_max)
        * (BUCKETS - exact_max)
    )
    far = np.minimum(
        exact_max + np.floor(np.maximum(scaled, 0.0)).astype(np.int64), BUCKETS - 1
    )
    bucket = np.where(distance < exact_max, distance, far)
    return (np.arange(BUCKETS)[:, None] == bucket[None, :]).astype(np.float32)


def dot(left, right):
    return jnp.dot(left, right, preferred_element_type=F32)


def dot_nt(left, right):
    return lax.dot_general(left, right, NT, preferred_element_type=F32)


def dot_tn(left, right):
    return lax.dot_general(left, right, TN, preferred_element_type=F32)


def rms_scale(inputs):
    return lax.rsqrt(jnp.mean(inputs * inputs, axis=-1, keepdims=True) + EPS)


def rms_back(inputs, gain, upstream):
    scale = rms_scale(inputs)
    gu = gain * upstream
    inner = jnp.mean(inputs * gu, axis=-1, keepdims=True)
    dx = scale * gu - inputs * (scale * scale * scale * inner)
    return dx, jnp.sum(upstream * inputs * scale, axis=0)


def half_masks():
    lane = lax.broadcasted_iota(jnp.int32, (1, 2 * HEAD), 1)
    low = (lane < HEAD).astype(BF)
    return low, 1 - low


def stacked(value, masks):
    return jnp.concatenate([value * masks[0], value * masks[1]], axis=0)


def joined_heads(value):
    rows = value.shape[0] // 2
    is_low = lax.broadcasted_iota(jnp.int32, (1, 2 * HEAD), 1) < HEAD
    return jnp.where(is_low, value[:rows], value[rows:])


def pair(index):
    return slice(index * 2 * HEAD, (index + 1) * 2 * HEAD)


def head_bias(base_ref, head):
    row = jnp.broadcast_to(base_ref[head : head + 1, :], (ROWS, SPAN))
    return pltpu.roll(row, 0, 1, stride=1, stride_axis=0)


def two_biases(base_ref, index, causal):
    return jnp.concatenate(
        [jnp.where(causal, head_bias(base_ref, 2 * index + half), NEG) for half in range(2)], axis=0
    )


def causal_mask():
    rows = lax.broadcasted_iota(jnp.int32, (ROWS, SPAN), 0)
    cols = lax.broadcasted_iota(jnp.int32, (ROWS, SPAN), 1)
    return cols <= rows


def self_fwd_kernel(items, qkv_ref, base_ref, att_ref, k_pad, v_pad):
    inner = HEADS * HEAD
    k_pad[...] = jnp.zeros_like(k_pad)
    v_pad[...] = jnp.zeros_like(v_pad)
    for item in range(items):
        k_pad[item, :ROWS, :] = qkv_ref[item, :, inner : 2 * inner]
        v_pad[item, :ROWS, :] = qkv_ref[item, :, 2 * inner :]
    causal = causal_mask()
    masks = half_masks()
    for index in range(HEADS // 2):
        bias = two_biases(base_ref, index, causal)
        for item in range(items):
            query = stacked(qkv_ref[item, :, pair(index)], masks)
            scores = dot_nt(query, k_pad[item, :, pair(index)]) + bias
            top = jnp.max(scores, axis=-1, keepdims=True)
            probs = jnp.exp(scores - top)
            probs = probs * (1.0 / jnp.sum(probs, axis=-1, keepdims=True))
            part = dot(probs.astype(BF), v_pad[item, :, pair(index)])
            att_ref[item, :, pair(index)] = joined_heads(part).astype(BF)


def self_fwd(qkv, base):
    items = qkv.shape[0]
    inner = HEADS * HEAD
    return pl.pallas_call(
        functools.partial(self_fwd_kernel, items),
        out_shape=jax.ShapeDtypeStruct((items, ROWS, inner), BF),
        in_specs=[VMEM_SPEC] * 2,
        out_specs=VMEM_SPEC,
        scratch_shapes=[pltpu.VMEM((items, SPAN, inner), BF)] * 2,
        compiler_params=pltpu.CompilerParams(vmem_limit_bytes=VMEM_CAP),
        cost_estimate=pl.CostEstimate(
            flops=items * HEADS * ROWS * SPAN * 128 * 4,
            bytes_accessed=items * ROWS * inner * 8,
            transcendentals=items * HEADS * ROWS * SPAN,
        ),
        name="self_fwd",
    )(qkv, base)


def diagonal_sums(values):
    total = values[:8]
    for start in range(8, ROWS, 8):
        total = total + pltpu.roll(values[start : start + 8], SPAN - start, 1)
    row = lax.broadcasted_iota(jnp.int32, (8, SPAN), 0)
    for bit in (1, 2, 4):
        total = jnp.where((row & bit) > 0, pltpu.roll(total, SPAN - bit, 1), total)
    return jnp.sum(total, axis=0, keepdims=True)


def self_bwd_kernel(items, qkv_ref, datt_ref, base_ref, dqkv_ref, diag_ref, k_pad, v_pad):
    inner = HEADS * HEAD
    k_pad[...] = jnp.zeros_like(k_pad)
    v_pad[...] = jnp.zeros_like(v_pad)
    diag_ref[...] = jnp.zeros_like(diag_ref)
    for item in range(items):
        k_pad[item, :ROWS, :] = qkv_ref[item, :, inner : 2 * inner]
        v_pad[item, :ROWS, :] = qkv_ref[item, :, 2 * inner :]
    causal = causal_mask()
    masks = half_masks()
    for index in range(HEADS // 2):
        bias = two_biases(base_ref, index, causal)
        ds_sum = None
        for item in range(items):
            query = stacked(qkv_ref[item, :, pair(index)], masks)
            upstream = stacked(datt_ref[item, :, pair(index)], masks)
            keys = k_pad[item, :, pair(index)]
            scores = dot_nt(query, keys) + bias
            top = jnp.max(scores, axis=-1, keepdims=True)
            probs = jnp.exp(scores - top)
            probs = probs * (1.0 / jnp.sum(probs, axis=-1, keepdims=True))
            dprobs = dot_nt(upstream, v_pad[item, :, pair(index)])
            delta = jnp.sum(probs * dprobs, axis=-1, keepdims=True)
            ds = probs * (dprobs - delta)
            ds_sum = ds if item == 0 else ds_sum + ds
            ds_low = ds.astype(BF)
            dqkv_ref[item, :, pair(index)] = joined_heads(dot(ds_low, keys)).astype(BF)
            dqkv_ref[item, :, pair(index + 3)] = dot_tn(ds_low, query)[:ROWS].astype(BF)
            dqkv_ref[item, :, pair(index + 6)] = dot_tn(probs.astype(BF), upstream)[
                :ROWS
            ].astype(BF)
        for half in range(2):
            head = 2 * index + half
            diag_ref[head : head + 1, :] = diagonal_sums(
                ds_sum[half * ROWS : (half + 1) * ROWS]
            )


def self_bwd(qkv, datt, base):
    items = qkv.shape[0]
    inner = HEADS * HEAD
    return pl.pallas_call(
        functools.partial(self_bwd_kernel, items),
        out_shape=(
            jax.ShapeDtypeStruct((items, ROWS, 3 * inner), BF),
            jax.ShapeDtypeStruct((8, SPAN), F32),
        ),
        in_specs=[VMEM_SPEC] * 3,
        out_specs=(VMEM_SPEC, VMEM_SPEC),
        scratch_shapes=[pltpu.VMEM((items, SPAN, inner), BF)] * 2,
        compiler_params=pltpu.CompilerParams(vmem_limit_bytes=VMEM_CAP),
        cost_estimate=pl.CostEstimate(
            flops=items * HEADS * ROWS * SPAN * 128 * 10,
            bytes_accessed=items * ROWS * inner * 14,
            transcendentals=items * HEADS * ROWS * SPAN,
        ),
        name="self_bwd",
    )(qkv, datt, base)


def greet(axis, offsets):
    me = lax.axis_index(axis)
    barrier = pltpu.get_barrier_semaphore()
    for offset in offsets:
        pl.semaphore_signal(
            barrier, inc=1, device_id={axis: jnp.bitwise_xor(me, offset)}, device_id_type=MESH
        )
    pl.semaphore_wait(barrier, len(offsets))


def send(src, dst, send_sem, recv_sem, offset):
    me = lax.axis_index("mem")
    return pltpu.make_async_remote_copy(
        src_ref=src,
        dst_ref=dst,
        send_sem=send_sem,
        recv_sem=recv_sem,
        device_id={"mem": jnp.bitwise_xor(me, offset)},
        device_id_type=MESH,
    )


def column(stats, index):
    return stats[:, index : index + 1]


def spread(stats, index, masks):
    return jnp.where(masks, column(stats, 2 * index), column(stats, 2 * index + 1))


def cross_fwd_kernel(
    items, q_ref, kv_ref, bias_ref, all_ref, att_ref, lse_ref,
    out_o, out_s, in_o, in_s, q_send, q_recv, o_send, o_recv, s_send, s_recv,
):
    me = lax.axis_index("mem")
    greet("mem", (1, 2, 3))
    q_to_core = send(q_ref, all_ref.at[1], q_send.at[0], q_recv.at[0], 1)
    q_to_far = send(q_ref, all_ref.at[2], q_send.at[1], q_recv.at[1], 2)
    q_relay = send(all_ref.at[2], all_ref.at[3], q_send.at[2], q_recv.at[2], 1)
    q_to_far.start()
    q_to_core.start()
    all_ref[0] = q_ref[...]
    low, high = half_masks()
    lane = lax.broadcasted_iota(jnp.int32, (1, STATS), 1)
    is_low = lax.broadcasted_iota(jnp.int32, (1, 2 * HEAD), 1) < HEAD
    copies = []
    for slot in (0, 2, 3, 1):
        if slot == 2:
            q_to_far.wait_recv()
            q_relay.start()
        if slot == 3:
            q_relay.wait_recv()
        if slot == 1:
            q_to_core.wait_recv()
        owner = jnp.bitwise_xor(me, slot)
        for item in range(items):
            place = owner * items + item
            bias = bias_ref[place]
            stats = jnp.zeros((ROWS, STATS), F32)
            for index in range(HEADS // 2):
                both = all_ref[slot, item, :, pair(index)]
                keys = kv_ref[place, :, pair(index)]
                values = kv_ref[place, :, pair(index + HEADS // 2)]
                scores = dot_nt(stacked(both, (low, high)), keys) + bias
                top = jnp.max(scores, axis=-1, keepdims=True)
                probs = jnp.exp(scores - top)
                amount = jnp.sum(probs, axis=-1, keepdims=True)
                total = joined_heads(dot(probs.astype(BF), values) * (1.0 / amount))
                level = top + jnp.log(amount)
                for half in range(2):
                    stats = jnp.where(
                        lane == 2 * index + half, level[half * ROWS : (half + 1) * ROWS], stats
                    )
                out_o[slot, item, :, pair(index)] = total.astype(BF)
            out_s[slot, item] = stats.T[:8]
        if slot:
            copies.append(send(out_o.at[slot], in_o.at[slot], o_send.at[slot], o_recv.at[slot], slot))
            copies.append(send(out_s.at[slot], in_s.at[slot], s_send.at[slot], s_recv.at[slot], slot))
            copies[-2].start()
            copies[-1].start()
    q_to_core.wait_send()
    q_to_far.wait_send()
    q_relay.wait_send()
    for copy in copies:
        copy.wait()
    for item in range(items):
        stats = [
            jnp.concatenate([part, jnp.zeros((STATS - 8, ROWS), F32)], axis=0).T
            for part in [out_s[0, item]] + [in_s[slot, item] for slot in (1, 2, 3)]
        ]
        top = jnp.maximum(jnp.maximum(stats[0], stats[1]), jnp.maximum(stats[2], stats[3]))
        shares = [jnp.exp(part - top) for part in stats]
        amount = shares[0] + shares[1] + shares[2] + shares[3]
        lse_ref[item] = top + jnp.log(amount)
        scale = 1.0 / amount
        shares = [part * scale for part in shares]
        for index in range(HEADS // 2):
            total = out_o[0, item, :, pair(index)].astype(F32) * spread(shares[0], index, is_low)
            for slot in (1, 2, 3):
                total += in_o[slot, item, :, pair(index)].astype(F32) * spread(
                    shares[slot], index, is_low
                )
            att_ref[item, :, pair(index)] = total.astype(BF)


def cross_fwd(queries, keys_values, bias):
    items = queries.shape[0]
    inner = HEADS * HEAD
    block = (4, items, ROWS, inner)
    stat_block = (4, items, 8, ROWS)
    flops = 4 * items * HEADS * ROWS * SPAN * 128 * 4
    return pl.pallas_call(
        functools.partial(cross_fwd_kernel, items),
        out_shape=(
            jax.ShapeDtypeStruct(block, BF),
            jax.ShapeDtypeStruct((items, ROWS, inner), BF),
            jax.ShapeDtypeStruct((items, ROWS, STATS), F32),
        ),
        in_specs=[VMEM_SPEC] * 3,
        out_specs=(VMEM_SPEC,) * 3,
        scratch_shapes=[
            pltpu.VMEM(block, BF),
            pltpu.VMEM(stat_block, F32),
            pltpu.VMEM(block, BF),
            pltpu.VMEM(stat_block, F32),
            pltpu.SemaphoreType.DMA((3,)),
            pltpu.SemaphoreType.DMA((3,)),
            pltpu.SemaphoreType.DMA((4,)),
            pltpu.SemaphoreType.DMA((4,)),
            pltpu.SemaphoreType.DMA((4,)),
            pltpu.SemaphoreType.DMA((4,)),
        ],
        compiler_params=pltpu.CompilerParams(
            collective_id=1, has_side_effects=True, vmem_limit_bytes=VMEM_CAP
        ),
        cost_estimate=pl.CostEstimate(
            flops=flops, bytes_accessed=8 * 1024 * 1024, transcendentals=flops // 512
        ),
        name="cross_fwd",
    )(queries, keys_values, bias)


def cross_bwd_kernel(
    items, all_ref, back_ref, stat_ref, kv_ref, bias_ref, dkv_ref, dq_ref,
    all_b, all_s, out_q, in_q, b_send, b_recv, s_send, s_recv, q_send, q_recv,
):
    me = lax.axis_index("mem")
    greet("mem", (1, 2, 3))
    moves = []
    for offset, slot, source in ((2, 2, None), (1, 1, None), (1, 3, 2)):
        number = len(moves)
        moves.append(
            (
                send(back_ref if source is None else all_b.at[source], all_b.at[slot],
                     b_send.at[number], b_recv.at[number], offset),
                send(stat_ref if source is None else all_s.at[source], all_s.at[slot],
                     s_send.at[number], s_recv.at[number], offset),
            )
        )
    for move in moves[:2]:
        for copy in move:
            copy.start()
    low, high = half_masks()
    copies = []
    for slot in (0, 2, 3, 1):
        if slot == 2:
            for copy in moves[0]:
                copy.wait_recv()
            for copy in moves[2]:
                copy.start()
        if slot == 3:
            for copy in moves[2]:
                copy.wait_recv()
        if slot == 1:
            for copy in moves[1]:
                copy.wait_recv()
        owner = jnp.bitwise_xor(me, slot)
        for item in range(items):
            place = owner * items + item
            bias = bias_ref[place]
            stats = stat_ref[item] if slot == 0 else all_s[slot, item]
            stats = jnp.concatenate([stats, jnp.zeros((STATS - 16, ROWS), F32)], axis=0).T
            for index in range(HEADS // 2):
                both = all_ref[slot, item, :, pair(index)]
                if slot == 0:
                    upstream = back_ref[item, :, pair(index)]
                else:
                    upstream = all_b[slot, item, :, pair(index)]
                keys = kv_ref[place, :, pair(index)]
                values = kv_ref[place, :, pair(index + HEADS // 2)]
                query = stacked(both, (low, high))
                back = stacked(upstream, (low, high))

                def both_columns(start, index=index, stats=stats):
                    return jnp.concatenate(
                        [column(stats, start + 2 * index + half) for half in range(2)], axis=0
                    )

                scores = dot_nt(query, keys) + bias
                probs = jnp.exp(scores - both_columns(0))
                dprobs = dot_nt(back, values)
                ds = (probs * (dprobs - both_columns(8))).astype(BF)
                dq = joined_heads(dot(ds, keys))
                dk = dot_tn(ds, query)
                dv = dot_tn(probs.astype(BF), back)
                out_q[slot, item, :, pair(index)] = dq.astype(BF)
                dkv_ref[place, :, pair(index)] = dk.astype(BF)
                dkv_ref[place, :, pair(index + HEADS // 2)] = dv.astype(BF)
        if slot:
            copies.append(send(out_q.at[slot], in_q.at[slot], q_send.at[slot], q_recv.at[slot], slot))
            copies[-1].start()
    for move in moves:
        for copy in move:
            copy.wait_send()
    for copy in copies:
        copy.wait()
    for item in range(items):
        for index in range(HEADS // 2):
            total = out_q[0, item, :, pair(index)].astype(F32)
            for slot in (1, 2, 3):
                total += in_q[slot, item, :, pair(index)].astype(F32)
            dq_ref[item, :, pair(index)] = total.astype(BF)


def cross_bwd(all_queries, back, stats, keys_values, bias):
    items = back.shape[0]
    inner = HEADS * HEAD
    block = (4, items, ROWS, inner)
    flops = 4 * items * HEADS * ROWS * SPAN * 128 * 10
    return pl.pallas_call(
        functools.partial(cross_bwd_kernel, items),
        out_shape=(
            jax.ShapeDtypeStruct(keys_values.shape, BF),
            jax.ShapeDtypeStruct((items, ROWS, inner), BF),
        ),
        in_specs=[VMEM_SPEC] * 5,
        out_specs=(VMEM_SPEC,) * 2,
        scratch_shapes=[
            pltpu.VMEM(block, BF),
            pltpu.VMEM((4, items, 16, ROWS), F32),
            pltpu.VMEM(block, BF),
            pltpu.VMEM(block, BF),
            pltpu.SemaphoreType.DMA((3,)),
            pltpu.SemaphoreType.DMA((3,)),
            pltpu.SemaphoreType.DMA((3,)),
            pltpu.SemaphoreType.DMA((3,)),
            pltpu.SemaphoreType.DMA((4,)),
            pltpu.SemaphoreType.DMA((4,)),
        ],
        compiler_params=pltpu.CompilerParams(
            collective_id=2, has_side_effects=True, vmem_limit_bytes=VMEM_CAP
        ),
        cost_estimate=pl.CostEstimate(
            flops=flops, bytes_accessed=12 * 1024 * 1024, transcendentals=flops // 1280
        ),
        name="cross_bwd",
    )(all_queries, back, stats, keys_values, bias)


CUBIC = 0.044715
ROOT = float(np.sqrt(2.0 / np.pi))


def strips(width, step):
    return [(start, min(step, width - start)) for start in range(0, width, step)]


def ffn_kernel(
    items, h_ref, up0_ref, up1_ref, up2_ref, up3_ref, gate_up_hbm, down_hbm,
    h_back_ref, near_ref, far_ref, grad_gu_hbm, grad_down_hbm,
    gate_up_ref, down_ref, h_all, u_all, hidden, two_back, h_part, y_part, h_in, y_in, gu_strip, down_strip,
    h_send, h_recv, d_send, d_recv, y_send, y_recv, load_sem, up_sem, store_sem,
):
    tokens, model = h_ref.shape
    last = 1 + items
    rows = tokens // items
    units = down_ref.shape[0]
    loads = [
        pltpu.make_async_copy(gate_up_hbm, gate_up_ref, load_sem.at[0]),
        pltpu.make_async_copy(down_hbm, down_ref, load_sem.at[1]),
        pltpu.make_async_copy(up0_ref, u_all.at[0], load_sem.at[2]),
        pltpu.make_async_copy(up1_ref, u_all.at[last], load_sem.at[3]),
    ]
    for copy in loads:
        copy.start()
    ups = []
    for item in range(items):
        mine = pl.ds(item * rows, rows)
        for place, ref in enumerate((up2_ref, up3_ref)):
            ups.append(
                pltpu.make_async_copy(
                    ref.at[mine], u_all.at[1 + item, pl.ds(place * rows, rows)],
                    up_sem.at[item, place],
                )
            )
            ups[-1].start()
    greet("mem", (1, 2))
    h_to_core = send(h_ref, h_all.at[last], h_send.at[0], h_recv.at[0], 1)
    h_to_far, h_relay, d_pass, d_far, y_pass = [], [], [], [], []
    first, second = pl.ds(0, rows), pl.ds(rows, rows)
    for item in range(items):
        block = at = 1 + item
        h_to_far.append(
            send(h_ref.at[pl.ds(item * rows, rows)], h_all.at[block, first],
                 h_send.at[at], h_recv.at[at], 2)
        )
        h_relay.append(
            send(h_all.at[block, first], h_all.at[block, second],
                 h_send.at[at + items], h_recv.at[at + items], 1)
        )
        d_pass.append(
            send(h_part.at[block, second], h_in.at[1, pl.ds(item * rows, rows)],
                 d_send.at[at], d_recv.at[at], 1)
        )
        y_pass.append(
            send(y_part.at[block, second], y_in.at[1, pl.ds(item * rows, rows)],
                 y_send.at[at], y_recv.at[at], 1)
        )
        d_far.append(
            send(h_part.at[block, first], h_in.at[2, pl.ds(item * rows, rows)],
                 d_send.at[at + items], d_recv.at[at + items], 2)
        )
    d_near = send(h_part.at[last], h_in.at[0], d_send.at[0], d_recv.at[0], 1)
    y_near = send(y_part.at[last], y_in.at[0], y_send.at[0], y_recv.at[0], 1)
    h_to_core.start()
    h_to_far[0].start()
    h_all[0] = h_ref[...]
    for copy in loads:
        copy.wait()
    for copy in ups:
        copy.wait()

    def give_back(item):
        mine = pl.ds(item * rows, rows)
        d_pass[item].wait_recv()
        h_part[1 + item, first, :] = (
            h_part[1 + item, first, :].astype(F32) + h_in[1, mine, :].astype(F32)
        ).astype(BF)
        d_far[item].start()

    def token_block(slot, carry):
        @pl.when(slot == last)
        def _():
            h_to_core.wait_recv()

        for item in range(items):

            @pl.when(slot == 1 + item)
            def _(item=item):
                h_relay[item].wait_recv()

            @pl.when(slot == 2 + item)
            def _(item=item):
                d_pass[item].start()
                y_pass[item].start()

        def units_block(block, inside):
            pairs = pl.ds(pl.multiple_of(block * 256, 256), 256)
            ones = pl.ds(pl.multiple_of(block * 128, 128), 128)
            both = dot(h_all[slot], gate_up_ref[:, pairs])
            back = dot_nt(u_all[slot], down_ref[ones, :]).astype(BF).astype(F32)
            gate, up = both[:, :128], both[:, 128:]
            square = gate * gate
            bend = jnp.tanh(ROOT * gate * (1.0 + CUBIC * square))
            share = 0.5 * (1.0 + bend)
            active = gate * share
            slope = share + 0.5 * gate * (1.0 - bend * bend) * (
                ROOT * (1.0 + 3.0 * CUBIC * square)
            )
            hidden[slot, :, ones] = (active * up).astype(BF)
            two_back[slot, :, pairs] = jnp.concatenate(
                [(back * up * slope).astype(BF), (back * active).astype(BF)], axis=1
            )
            return inside

        lax.fori_loop(0, units // 128, units_block, 0)
        for item in range(1, items):

            @pl.when(slot == item - 1)
            def _(item=item):
                h_to_far[item].start()

        for start, width in strips(model, 256):
            part = slice(start, start + width)
            h_part[slot, :, part] = dot_nt(two_back[slot], gate_up_ref[part, :]).astype(BF)
        for item in range(items):

            @pl.when(slot == item)
            def _(item=item):
                h_to_far[item].wait_recv()
                h_relay[item].start()

            @pl.when(slot == 2 + item)
            def _(item=item):
                give_back(item)

        for start, width in strips(model, 256):
            part = slice(start, start + width)
            y_part[slot, :, part] = dot(hidden[slot], down_ref[:, part]).astype(BF)
        return carry

    lax.fori_loop(0, 2 + items, token_block, 0)
    d_near.start()
    y_near.start()
    count = (2 + items) * tokens
    stores = []

    def store(value, strip, hbm, start, width):
        number = len(stores)
        if number >= 2:
            stores[number - 2].wait()
        strip[number % 2, :width, :] = value
        stores.append(
            pltpu.make_async_copy(
                strip.at[number % 2, pl.ds(0, width)],
                hbm.at[pl.ds(start, width)],
                store_sem.at[number],
            )
        )
        stores[-1].start()

    for start, width in strips(model, 256):
        part = slice(start, start + width)
        value = dot_tn(
            h_all[:, :, part].reshape(count, width), two_back[...].reshape(count, 2 * units)
        )
        store(value.astype(BF), gu_strip, grad_gu_hbm, start, width)
    for start, width in strips(units, 256):
        part = slice(start, start + width)
        value = dot_tn(
            hidden[:, :, part].reshape(count, width), u_all[...].reshape(count, model)
        )
        store(value.astype(BF), down_strip, grad_down_hbm, start, width)
    for item in range(items):
        mine = pl.ds(item * rows, rows)
        y_pass[item].wait_recv()
        far_ref[mine, :] = (
            y_part[1 + item, first, :].astype(F32) + y_in[1, mine, :].astype(F32)
        ).astype(BF)
    y_near.wait_recv()
    near_ref[...] = (y_part[0].astype(F32) + y_in[0].astype(F32)).astype(BF)
    d_near.wait_recv()
    for copy in d_far:
        copy.wait_recv()
    h_back_ref[...] = (
        h_part[0].astype(F32) + h_in[0].astype(F32) + h_in[2].astype(F32)
    )
    for copy in stores[-2:]:
        copy.wait()
    for copy in (h_to_core, d_near, y_near, *h_to_far, *h_relay, *d_pass, *y_pass, *d_far):
        copy.wait_send()


def ffn(h3, upstreams, gate_up, down, items):
    tokens, model = h3.shape
    units = down.shape[0]
    every = (2 + items, tokens, model)
    flops = (2 + items) * tokens * model * units * 18
    grads = len(strips(model, 256)) + len(strips(units, 256))
    return pl.pallas_call(
        functools.partial(ffn_kernel, items),
        out_shape=(
            jax.ShapeDtypeStruct((tokens, model), F32),
            jax.ShapeDtypeStruct((tokens, model), BF),
            jax.ShapeDtypeStruct((tokens, model), BF),
            jax.ShapeDtypeStruct((model, 2 * units), BF),
            jax.ShapeDtypeStruct((units, model), BF),
        ),
        in_specs=[VMEM_SPEC] + [ANY_SPEC] * 6,
        out_specs=(VMEM_SPEC,) * 3 + (ANY_SPEC,) * 2,
        scratch_shapes=[
            pltpu.VMEM((model, 2 * units), BF),
            pltpu.VMEM((units, model), BF),
            pltpu.VMEM(every, BF),
            pltpu.VMEM(every, BF),
            pltpu.VMEM((2 + items, tokens, units), BF),
            pltpu.VMEM((2 + items, tokens, 2 * units), BF),
            pltpu.VMEM(every, BF),
            pltpu.VMEM(every, BF),
            pltpu.VMEM((3, tokens, model), BF),
            pltpu.VMEM((2, tokens, model), BF),
            pltpu.VMEM((2, 256, 2 * units), BF),
            pltpu.VMEM((2, 256, model), BF),
        ]
        + [pltpu.SemaphoreType.DMA((1 + 2 * items,))] * 4
        + [pltpu.SemaphoreType.DMA((1 + items,))] * 2
        + [
            pltpu.SemaphoreType.DMA((4,)),
            pltpu.SemaphoreType.DMA((items, 2)),
            pltpu.SemaphoreType.DMA((grads,)),
        ],
        compiler_params=pltpu.CompilerParams(
            collective_id=3, has_side_effects=True, vmem_limit_bytes=FFN_CAP
        ),
        cost_estimate=pl.CostEstimate(
            flops=flops, bytes_accessed=32 * 1024 * 1024, transcendentals=4 * tokens * units
        ),
        name="feed_forward",
    )(h3, *upstreams, gate_up, down)


def peer_copy(src, dst, send_sem, recv_sem, tgt=None, mem=None):
    where = {}
    if tgt is not None:
        where["tgt"] = tgt
    if mem is not None:
        where["mem"] = mem
    return pltpu.make_async_remote_copy(
        src_ref=src, dst_ref=dst, send_sem=send_sem, recv_sem=recv_sem,
        device_id=where, device_id_type=MESH,
    )


def greet_all(mem, tgt):
    barrier = pltpu.get_barrier_semaphore()
    for offset in (1, 2, 3):
        pl.semaphore_signal(
            barrier, inc=1, device_id={"mem": jnp.bitwise_xor(mem, offset)}, device_id_type=MESH
        )
    for offset in (1, 2, 4, 6):
        pl.semaphore_signal(
            barrier, inc=1, device_id={"tgt": jnp.bitwise_xor(tgt, offset)}, device_id_type=MESH
        )
    pl.semaphore_wait(barrier, 7)


FIRST = (1, 2, 4, 6)
PASSED = (3, 5, 7)


def gather_kernel(
    self_q, self_k, self_v, cross_q, cross_k, cross_v, self_o, cross_o,
    qkv_out, kv_out, cq_out, so_out, co_out,
    t_send, t_recv, x_send, x_recv, c_send, c_recv, r_send, r_recv, own_sem,
):
    mem = lax.axis_index("mem")
    tgt = lax.axis_index("tgt")
    inner = HEADS * HEAD

    def part(out, index):
        return lambda place: out.at[place, :, index * inner : (index + 1) * inner]

    def whole(out):
        return lambda place: out.at[place]

    groups = (
        ((self_q, part(qkv_out, 0)), (self_k, part(qkv_out, 1))),
        ((self_v, part(qkv_out, 2)), (cross_q, part(cq_out, 0))),
        ((cross_k, part(kv_out, 0)), (cross_v, part(kv_out, 1))),
        ((self_o, whole(so_out)), (cross_o, whole(co_out))),
    )
    greet_all(mem, tgt)
    near = jnp.bitwise_xor(mem, 1)
    far = jnp.bitwise_xor(mem, 2)

    def over_tgt(member, number, step, offset):
        src, dst = member
        if step < 4:
            return peer_copy(
                src, dst(tgt), t_send.at[step, number], t_recv.at[step, number],
                tgt=jnp.bitwise_xor(tgt, offset),
            )
        place = jnp.bitwise_xor(tgt, offset - 1)
        return peer_copy(
            dst(place), dst(place), t_send.at[step, number], t_recv.at[step, number],
            tgt=jnp.bitwise_xor(tgt, 1),
        )

    def over_far(member, number, step, offset):
        dst = member[1](jnp.bitwise_xor(tgt, offset))
        return peer_copy(dst, dst, x_send.at[step, number], x_recv.at[step, number], mem=far)

    def over_near(member, number, step, offset):
        dst = member[1](jnp.bitwise_xor(tgt, offset))
        return peer_copy(dst, dst, c_send.at[step, number], c_recv.at[step, number], mem=near)

    def relay(member, number, step, offset):
        dst = member[1](jnp.bitwise_xor(tgt, offset))
        return peer_copy(dst, dst, r_send.at[step, number], r_recv.at[step, number], mem=near)

    steps = list(enumerate(FIRST + PASSED))
    for index, group in enumerate(groups):

        @pl.when(mem == index)
        def _(index=index, group=group):
            members = list(enumerate(group))
            far_members = list(enumerate(groups[index ^ 2]))
            near_members = list(enumerate(groups[index ^ 1]))
            last_members = list(enumerate(groups[index ^ 3]))
            extra = []
            far_sent = members
            far_got = far_members
            for step, offset in steps[:4]:
                for number, member in members + extra:
                    over_tgt(member, number, step, offset).start()
            own = []
            for place, (src, dst) in enumerate(member for all_of in groups for member in all_of):
                own.append(pltpu.make_async_copy(src, dst(tgt), own_sem.at[place]))
                own[-1].start()
            for step, offset in steps:
                for number, member in members:
                    over_tgt(member, number, step, offset).wait_recv()
                    if 0 < step < 4:
                        over_tgt(member, number, step + 3, offset + 1).start()
                    if (number, member) in far_sent:
                        over_far(member, number, step, offset).start()
                    over_near(member, number, step, offset).start()
                for number, member in extra:
                    over_tgt(member, number, step, offset).wait_recv()
                    if 0 < step < 4:
                        over_tgt(member, number, step + 3, offset + 1).start()
                    relay(member, 0, step, offset).start()
            for step, offset in steps:
                for number, member in far_got:
                    over_far(member, number, step, offset).wait_recv()
                    relay(member, number, step, offset).start()
            for step, offset in steps:
                for number, member in near_members:
                    over_near(member, number, step, offset).wait_recv()
                for number, member in last_members:
                    relay(member, number, step, offset).wait_recv()
                for number, member in members + extra:
                    over_tgt(member, number, step, offset).wait_send()
                for number, member in far_sent:
                    over_far(member, number, step, offset).wait_send()
                for number, member in members:
                    over_near(member, number, step, offset).wait_send()
                for number, member in far_members:
                    relay(member, number, step, offset).wait_send()
            for copy in own:
                copy.wait()


def gather_weights(weights):
    tgts = lax.axis_size("tgt")
    rows, inner = weights[0].shape
    o_rows, model = weights[-1].shape

    def out(columns, height=rows):
        return jax.ShapeDtypeStruct((tgts, height, columns), BF)

    shapes = (out(3 * inner), out(2 * inner), out(inner), out(model, o_rows), out(model, o_rows))
    sems = [pltpu.SemaphoreType.DMA((7, 3))] * 2 + [pltpu.SemaphoreType.DMA((7, 2))] * 6
    return pl.pallas_call(
        gather_kernel,
        out_shape=shapes,
        in_specs=[ANY_SPEC] * 8,
        out_specs=(ANY_SPEC,) * 5,
        scratch_shapes=sems + [pltpu.SemaphoreType.DMA((8,))],
        compiler_params=pltpu.CompilerParams(collective_id=4, has_side_effects=True),
        cost_estimate=pl.CostEstimate(
            flops=0, bytes_accessed=150 * 1024 * 1024, transcendentals=0
        ),
        name="gather_weights",
    )(*weights)


TURNS = (7, 6, 5, 4, 3, 2, 1, 0)


def reduce_kernel(
    qkv_ref, kv_ref, cq_ref, so_ref, co_ref, small_ref, units_ref,
    q_out, k_out, v_out, cq_out, ck_out, cv_out, so_out, co_out, small_out, units_out,
    small_in, s_send, s_recv, u_send, u_recv, u_own,
    wide_in, tall_in, wide_x, tall_x, wide_y, tall_y, wide_z, tall_z, wide_e, tall_e,
    a_send, a_recv, b_send, b_recv, x_send, x_recv, y_send, y_recv, z_send, z_recv,
    e_send, e_recv,
):
    mem = lax.axis_index("mem")
    tgt = lax.axis_index("tgt")
    inner = HEADS * HEAD

    def part(ref, index):
        return lambda place: ref.at[place, :, index * inner : (index + 1) * inner]

    def whole(ref):
        return lambda place: ref.at[place]

    wide = (wide_in, wide_x, wide_y, wide_z, wide_e)
    tall = (tall_in, tall_x, tall_y, tall_z, tall_e)
    groups = (
        ((part(qkv_ref, 0), q_out, wide), (part(qkv_ref, 1), k_out, wide)),
        ((part(qkv_ref, 2), v_out, wide), (part(cq_ref, 0), cq_out, wide)),
        ((part(kv_ref, 0), ck_out, wide), (part(kv_ref, 1), cv_out, wide)),
        ((whole(so_ref), so_out, tall), (whole(co_ref), co_out, tall)),
    )
    greet_all(mem, tgt)
    near = jnp.bitwise_xor(mem, 1)
    far = jnp.bitwise_xor(mem, 2)

    def to_near(member, number, step, lane):
        place = jnp.bitwise_xor(tgt, TURNS[step])
        send_sems, recv_sems = ((a_send, a_recv), (b_send, b_recv))[lane]
        return peer_copy(
            member[0](place), member[2][0].at[lane, step, number],
            send_sems.at[step, number], recv_sems.at[step, number], mem=near,
        )

    def to_far(member, number, step):
        buffer = member[2][1]
        return peer_copy(
            buffer.at[0, step, number], buffer.at[1, step, number],
            x_send.at[step, number], x_recv.at[step, number], mem=far,
        )

    def to_side(member, number, turn):
        buffer = member[2][2]
        return peer_copy(
            buffer.at[0, turn, number], buffer.at[1, turn, number],
            y_send.at[turn, number], y_recv.at[turn, number], tgt=jnp.bitwise_xor(tgt, 1),
        )

    def to_owner(member, number, turn):
        buffer = member[2][3]
        return peer_copy(
            buffer.at[0, turn, number], buffer.at[1, turn, number],
            z_send.at[turn, number], z_recv.at[turn, number],
            tgt=jnp.bitwise_xor(tgt, TURNS[2 * turn + 1]),
        )

    def to_all(member, number, lane, peer):
        buffer = member[2][4]
        return peer_copy(
            buffer.at[2 if lane == 2 else 0, number],
            buffer.at[(1, 2, 3)[lane], number],
            e_send.at[lane, number], e_recv.at[lane, number], mem=peer,
        )

    z_place = tgt // 2
    y_place = tgt % 2
    small_mem = [
        peer_copy(small_in.at[mem], small_in.at[mem], s_send.at[offset], s_recv.at[offset],
                  mem=jnp.bitwise_xor(mem, offset))
        for offset in (1, 2, 3)
    ]
    small_y = peer_copy(small_in.at[4 + y_place], small_in.at[4 + y_place], s_send.at[0],
                        s_recv.at[0], tgt=jnp.bitwise_xor(tgt, 1))
    small_z = [
        peer_copy(small_in.at[6 + z_place], small_in.at[6 + z_place], s_send.at[3 + offset],
                  s_recv.at[3 + offset], tgt=jnp.bitwise_xor(tgt, 2 * offset))
        for offset in (1, 2, 3)
    ]
    small_in[mem] = small_ref[...]
    for move in small_mem:
        move.start()

    share_far = peer_copy(units_ref, units_out.at[mem], u_send.at[0], u_recv.at[0], mem=far)
    share_near = peer_copy(units_ref, units_out.at[mem], u_send.at[1], u_recv.at[1], mem=near)
    share_on = peer_copy(units_out.at[far], units_out.at[far], u_send.at[2], u_recv.at[2], mem=near)
    share_own = pltpu.make_async_copy(units_ref, units_out.at[mem], u_own)
    share_own.start()

    for index, group in enumerate(groups):

        @pl.when(mem == index)
        def _(index=index, group=group):
            mine = list(enumerate(group))
            near_group = list(enumerate(groups[index ^ 1]))
            far_group = list(enumerate(groups[index ^ 2]))
            last_group = list(enumerate(groups[index ^ 3]))
            steps = range(len(TURNS))
            for step in steps:
                for number, member in last_group:
                    to_near(member, number, step, 1).start()
                for number, member in near_group:
                    to_near(member, number, step, 0).start()
            for step in steps:
                place = jnp.bitwise_xor(tgt, TURNS[step])
                for number, member in far_group:
                    to_near(member, number, step, 1).wait_recv()
                    member[2][1][0, step, number] = (
                        member[0](place)[...].astype(F32)
                        + member[2][0][1, step, number].astype(F32)
                    ).astype(BF)
                    to_far(member, number, step).start()
            share_far.start()
            share_near.start()
            for move in small_mem:
                move.wait_recv()
            small_in[4 + y_place] = (small_in[0] + small_in[1]) + (small_in[2] + small_in[3])
            small_y.start()
            def mem_sum(member, number, step):
                to_near(member, number, step, 0).wait_recv()
                to_far(member, number, step).wait_recv()
                return (
                    member[0](jnp.bitwise_xor(tgt, TURNS[step]))[...].astype(F32)
                    + member[2][0][0, step, number].astype(F32)
                    + member[2][1][1, step, number].astype(F32)
                )

            def for_side(turn):
                for number, member in mine:
                    member[2][2][0, turn, number] = mem_sum(member, number, 2 * turn).astype(BF)
                    to_side(member, number, turn).start()

            for_side(0)
            small_y.wait_recv()
            small_in[6 + z_place] = small_in[4] + small_in[5]
            for move in small_z:
                move.start()
            for_side(1)
            for_side(2)
            for_side(3)
            for turn in range(4):
                for number, member in mine:
                    total = mem_sum(member, number, 2 * turn + 1)
                    to_side(member, number, turn).wait_recv()
                    total = total + member[2][2][1, turn, number].astype(F32)
                    if turn < 3:
                        member[2][3][0, turn, number] = total.astype(BF)
                        to_owner(member, number, turn).start()
                        continue
                    member[2][4][0, number] = total.astype(BF)
            for number, member in mine:
                total = member[2][4][0, number].astype(F32)
                for other in range(3):
                    to_owner(member, number, other).wait_recv()
                    total = total + member[2][3][1, other, number].astype(F32)
                member[2][4][0, number] = total.astype(BF)
                to_all(member, number, 1, far).start()
                to_all(member, number, 0, near).start()
                member[1][...] = member[2][4][0, number]
            for number, member in far_group:
                to_all(member, number, 1, far).wait_recv()
                to_all(member, number, 2, near).start()
                member[1][...] = member[2][4][2, number]
            for number, member in near_group:
                to_all(member, number, 0, near).wait_recv()
                member[1][...] = member[2][4][1, number]
            for number, member in last_group:
                to_all(member, number, 2, near).wait_recv()
                member[1][...] = member[2][4][3, number]
            for move in small_z:
                move.wait_recv()
            small_out[...] = (small_in[6] + small_in[7]) + (small_in[8] + small_in[9])
            share_far.wait_recv()
            share_on.start()
            share_near.wait_recv()
            share_on.wait_recv()
            share_own.wait()
            for move in (*small_mem, small_y, *small_z, share_far, share_near, share_on):
                move.wait_send()
            for step in steps:
                for number, member in last_group:
                    to_near(member, number, step, 1).wait_send()
                for number, member in near_group:
                    to_near(member, number, step, 0).wait_send()
                for number, member in far_group:
                    to_far(member, number, step).wait_send()
            for number, member in mine:
                for turn in range(4):
                    to_side(member, number, turn).wait_send()
                for turn in range(3):
                    to_owner(member, number, turn).wait_send()
                to_all(member, number, 0, near).wait_send()
                to_all(member, number, 1, far).wait_send()
            for number, member in far_group:
                to_all(member, number, 2, near).wait_send()


def reduce_weights(d_qkv, d_kv, d_cq, d_so, d_co, small, units):
    rows, inner = d_cq.shape[1:]
    o_rows, model = d_so.shape[1:]
    wide, tall = (rows, inner), (o_rows, model)
    scratch = []
    for lead in ((2, 8, 2), (2, 8, 2), (2, 4, 2), (2, 3, 2), (4, 2)):
        scratch += [pltpu.VMEM(lead + wide, BF), pltpu.VMEM(lead + tall, BF)]
    sems = []
    for count in (8, 8, 8, 4, 3, 3):
        sems += [pltpu.SemaphoreType.DMA((count, 2))] * 2
    return pl.pallas_call(
        reduce_kernel,
        out_shape=tuple(jax.ShapeDtypeStruct(wide, BF) for _ in range(6))
        + tuple(jax.ShapeDtypeStruct(tall, BF) for _ in range(2))
        + (
            jax.ShapeDtypeStruct(small.shape, F32),
            jax.ShapeDtypeStruct((4,) + units.shape, BF),
        ),
        in_specs=[VMEM_SPEC] * 6 + [ANY_SPEC],
        out_specs=(VMEM_SPEC,) * 9 + (ANY_SPEC,),
        scratch_shapes=[pltpu.VMEM((10,) + small.shape, F32)]
        + [pltpu.SemaphoreType.DMA((7,))] * 2
        + [pltpu.SemaphoreType.DMA((3,))] * 2
        + [pltpu.SemaphoreType.DMA]
        + scratch
        + sems,
        compiler_params=pltpu.CompilerParams(
            collective_id=5, has_side_effects=True, vmem_limit_bytes=VMEM_CAP
        ),
        cost_estimate=pl.CostEstimate(
            flops=0, bytes_accessed=150 * 1024 * 1024, transcendentals=0
        ),
        name="reduce_weights",
    )(d_qkv, d_kv, d_cq, d_so, d_co, small, units)


def pick_kernel(tgts, groups, gate_ref, up_ref, out_ref):
    mem = lax.axis_index("mem")
    shard = gate_ref.shape[1] // tgts
    piece = shard // groups

    for group in range(groups):

        @pl.when(mem == group)
        def _(group=group):
            for number, ref in enumerate((gate_ref, up_ref)):
                parts = []
                for place in range(tgts):
                    start = place * shard + group * piece
                    parts.append(ref[:, start : start + piece].astype(F32))
                quarter = jnp.concatenate(parts, axis=1).astype(BF)
                for block in range(quarter.shape[1] // 128):
                    start = block * 256 + number * 128
                    out_ref[:, start : start + 128] = quarter[:, block * 128 : block * 128 + 128]


def pick_units(gate, up):
    groups, tgts = lax.axis_size("mem"), lax.axis_size("tgt")
    rows, units = gate.shape
    return pl.pallas_call(
        functools.partial(pick_kernel, tgts, groups),
        out_shape=jax.ShapeDtypeStruct((rows, 2 * units // groups), BF),
        in_specs=[VMEM_SPEC] * 2,
        out_specs=VMEM_SPEC,
        compiler_params=pltpu.CompilerParams(vmem_limit_bytes=VMEM_CAP),
        name="pick_units",
    )(gate, up)


def place_kernel(tgts, groups, parts_ref, down_parts_ref, *refs):
    count = (len(refs) - 3) // 2
    gate_ref, up_ref, down_ref = refs[count : count + 3]
    for src, dst in zip(refs[:count], refs[count + 3 :]):
        dst[...] = src[...].astype(F32)
    height = down_parts_ref.shape[1]
    for group in range(groups):
        down_ref[group * height : (group + 1) * height, :] = down_parts_ref[group].astype(F32)
    units = gate_ref.shape[1]
    piece = units // tgts // groups
    for number, ref in enumerate((gate_ref, up_ref)):
        quarters = []
        for group in range(groups):
            blocks = [
                parts_ref[group, :, start : start + 128]
                for start in range(number * 128, 2 * units // groups, 256)
            ]
            quarters.append(jnp.concatenate(blocks, axis=1).astype(F32))
        ref[...] = jnp.concatenate(
            [
                quarters[group][:, place * piece : (place + 1) * piece]
                for place in range(tgts)
                for group in range(groups)
            ],
            axis=1,
        )


def place_units(parts, down_parts, sums):
    groups, tgts = lax.axis_size("mem"), lax.axis_size("tgt")
    rows, columns = parts.shape[1:]
    wide = jax.ShapeDtypeStruct((rows, groups * columns // 2), F32)
    down = jax.ShapeDtypeStruct((groups * down_parts.shape[1], down_parts.shape[2]), F32)
    shapes = (wide, wide, down) + tuple(jax.ShapeDtypeStruct(part.shape, F32) for part in sums)
    return pl.pallas_call(
        functools.partial(place_kernel, tgts, groups),
        out_shape=shapes,
        in_specs=[VMEM_SPEC] * (2 + len(sums)),
        out_specs=(VMEM_SPEC,) * len(shapes),
        compiler_params=pltpu.CompilerParams(vmem_limit_bytes=VMEM_CAP),
        name="place_units",
    )(parts, down_parts, *sums)


def share_kernel(src, out, sends, recvs, own_sem):
    mem = lax.axis_index("mem")
    greet("mem", (1, 2))
    near = jnp.bitwise_xor(mem, 1)
    far = jnp.bitwise_xor(mem, 2)
    to_far = peer_copy(src, out.at[mem], sends.at[0], recvs.at[0], mem=far)
    to_near = peer_copy(src, out.at[mem], sends.at[1], recvs.at[1], mem=near)
    pass_on = peer_copy(out.at[far], out.at[far], sends.at[2], recvs.at[2], mem=near)
    to_far.start()
    to_near.start()
    own = pltpu.make_async_copy(src, out.at[mem], own_sem)
    own.start()
    to_far.wait_recv()
    pass_on.start()
    to_near.wait_recv()
    pass_on.wait_recv()
    for copy in (to_far, to_near, pass_on):
        copy.wait_send()
    own.wait()


def share(value):
    groups = lax.axis_size("mem")
    return pl.pallas_call(
        share_kernel,
        out_shape=jax.ShapeDtypeStruct((groups,) + value.shape, BF),
        in_specs=[ANY_SPEC],
        out_specs=ANY_SPEC,
        scratch_shapes=[pltpu.SemaphoreType.DMA((3,))] * 2 + [pltpu.SemaphoreType.DMA],
        compiler_params=pltpu.CompilerParams(collective_id=6, has_side_effects=True),
        cost_estimate=pl.CostEstimate(
            flops=0, bytes_accessed=30 * 1024 * 1024, transcendentals=0
        ),
        name="share_sums",
    )(value)


def over_mem(value, offset):
    return lax.ppermute(value, "mem", [(i, i ^ offset) for i in range(4)])


def gather_mem(value):
    far = over_mem(value, 2)
    near = over_mem(value, 1)
    return value, near, far, over_mem(far, 1)


def gather_tgt(shard):
    return lax.all_gather(shard, "tgt", axis=0, tiled=True)


def scatter_tgt(partial):
    return lax.psum_scatter(partial, "tgt", scatter_dimension=0, tiled=True)


def in_tiles(value):
    rows, columns = value.shape
    value = jnp.pad(value, ((0, 0), (0, -columns % 128)))
    return value.reshape(rows // 8, 8, -1, 128).swapaxes(1, 2).reshape(-1, 8, 128)


def from_tiles(tiles, rows, columns):
    shards = tiles.shape[0]
    tiles = tiles.reshape(shards * rows // 8, -1, 8, 128).swapaxes(1, 2)
    return tiles.reshape(shards * rows, -1)[:, :columns]


def gather_units(gate_up, down):
    if gate_up.shape[0] % 8 or down.shape[0] % 8:
        return gather_tgt(gate_up), gather_tgt(down)
    tiles = in_tiles(gate_up)
    both = lax.all_gather(jnp.concatenate([tiles, in_tiles(down)]), "tgt", axis=0)
    return (
        from_tiles(both[:, : tiles.shape[0]], *gate_up.shape),
        from_tiles(both[:, tiles.shape[0] :], *down.shape),
    )


def attention_weights(weights):
    if lax.axis_size("tgt") == 8:
        return gather_weights(weights)
    parts = [lax.all_gather(weight, "tgt", axis=0) for weight in weights]
    return (
        jnp.concatenate(parts[:3], axis=-1),
        jnp.concatenate(parts[4:6], axis=-1),
        parts[3],
        parts[6],
        parts[7],
    )


def weight_sums(partials, small, units):
    if lax.axis_size("tgt") == 8:
        return reduce_weights(*partials, small, units)
    inner = HEADS * HEAD
    totals = [
        lax.psum_scatter(partial, "tgt", scatter_dimension=0, tiled=False) for partial in partials
    ]
    qkv, kv, cq, so, co = lax.psum(totals, "mem")
    return (
        qkv[:, :inner], qkv[:, inner : 2 * inner], qkv[:, 2 * inner :], cq,
        kv[:, :inner], kv[:, inner:], so, co, lax.psum(small, ("tgt", "mem")),
        lax.all_gather(units, "mem", axis=0),
    )


def on_device(
    target, memory, lengths, gate_bias, out_grad, gain_self, gain_cross, gain_ffn, rel_table,
    self_q, self_k, self_v, self_o, cross_q, cross_k, cross_v, cross_o, ffn_gate, ffn_up, ffn_down,
):
    groups = lax.axis_size("mem")
    tgts = lax.axis_size("tgt")
    mem_index = lax.axis_index("mem")
    items, seq, model = target.shape
    all_items, positions_dev, _ = memory.shape
    inner = HEADS * HEAD
    tokens = items * ROWS
    shard_in = ffn_gate.shape[0]
    hidden_shard = ffn_down.shape[0]
    piece = hidden_shard // groups
    quarter = tgts * piece

    def padded(value):
        return jnp.pad(value, ((0, 0), (0, ROWS - seq), (0, 0))).reshape(tokens, model)

    def trimmed(value):
        return value.reshape(items, ROWS, model)[:, :seq]

    norm_self = gain_self.astype(F32)
    norm_cross = gain_cross.astype(F32)
    norm_ffn = gain_ffn.astype(F32)
    onehot = jnp.asarray(distance_onehot())
    base = jnp.pad(
        lax.dot_general(rel_table, onehot, TN, precision=HIGH), ((0, 2), (0, 0))
    )
    positions = mem_index * positions_dev + jnp.arange(positions_dev)
    bias = jnp.where(positions[None, :] < lengths[:, None], gate_bias, NEG)[:, None, :]

    self_w, cross_kv_w, cross_q_w, self_o_w, cross_o_w = (
        weight.reshape(-1, weight.shape[-1])
        for weight in attention_weights(
            (self_q, self_k, self_v, cross_q, cross_k, cross_v, self_o, cross_o)
        )
    )
    gate_up = pick_units(ffn_gate, ffn_up)
    down = lax.dynamic_slice_in_dim(ffn_down, mem_index * piece, piece, axis=0)
    gate_up, down = gather_units(gate_up, down)

    inputs = padded(target).astype(F32)
    upstream_low = padded(out_grad)
    late, self_w = lax.optimization_barrier((upstream_low, self_w))
    upstreams = gather_mem(late)

    h1 = (inputs * rms_scale(inputs) * norm_self).astype(BF)
    qkv = dot(h1, self_w).astype(BF).reshape(items, ROWS, 3 * inner)
    att = self_fwd(qkv, base).reshape(tokens, inner)
    y1 = inputs + dot(att, self_o_w)
    h2 = (y1 * rms_scale(y1) * norm_cross).astype(BF)
    cq = dot(h2, cross_q_w).astype(BF).reshape(items, ROWS, inner)
    ckv = jnp.einsum(
        "npd,dc->npc", memory, cross_kv_w, preferred_element_type=F32
    ).astype(BF)
    all_queries, catt, lse = cross_fwd(cq, ckv, bias)
    catt = catt.reshape(tokens, inner)
    y2 = y1 + dot(catt, cross_o_w)
    h3 = (y2 * rms_scale(y2) * norm_ffn).astype(BF)

    h3_back, out_near, out_far, grad_gate_up, grad_down = ffn(h3, upstreams, gate_up, down, items)
    out_sum = over_mem(out_far, 2)
    grad_gate_up = scatter_tgt(grad_gate_up)
    dx, grad_norm_ffn = rms_back(y2, norm_ffn, h3_back)
    dy2 = upstream_low.astype(F32) + dx
    e2 = dy2.astype(BF)
    grad_cross_o = dot_tn(catt, e2).astype(BF)
    dcatt = dot_nt(e2, cross_o_w).astype(BF)
    delta = jnp.sum(
        (dcatt.astype(F32) * catt.astype(F32)).reshape(tokens, HEADS, HEAD), axis=-1
    ).reshape(items, ROWS, HEADS)
    stats = jnp.concatenate(
        [lse[:, :, :8], delta, jnp.zeros((items, ROWS, 8 - HEADS), F32)], axis=-1
    ).swapaxes(1, 2)
    dckv, dcq = cross_bwd(
        all_queries, dcatt.reshape(items, ROWS, inner), stats, ckv, bias
    )
    y2_late, grad_down, dcq = lax.optimization_barrier((y2, grad_down, dcq))
    grad_down = scatter_tgt(grad_down)
    layer_out = trimmed(
        (y2_late + out_near.astype(F32) + out_sum.astype(F32)).astype(BF)
    )
    dcq = dcq.reshape(tokens, inner)
    grad_cross_kv = jnp.einsum("npd,npc->dc", memory, dckv, preferred_element_type=F32)
    memory_grad = jnp.einsum(
        "npc,dc->npd", dckv, cross_kv_w, preferred_element_type=F32
    ).astype(BF)
    grad_cross_q = dot_tn(h2, dcq)
    dx, grad_norm_cross = rms_back(y1, norm_cross, dot_nt(dcq, cross_q_w))
    dy1 = dy2 + dx
    e1 = dy1.astype(BF)
    grad_self_o = dot_tn(att, e1).astype(BF)
    datt = dot_nt(e1, self_o_w).astype(BF).reshape(items, ROWS, inner)
    dqkv, diag = self_bwd(qkv, datt, base)
    dqkv = dqkv.reshape(tokens, 3 * inner)
    grad_self = dot_tn(h1, dqkv)
    dx, grad_norm_self = rms_back(inputs, norm_self, dot_nt(dqkv, self_w))
    target_grad = trimmed((dy1 + dx).astype(BF))
    table = lax.dot_general(
        onehot, diag[:HEADS], NT, precision=HIGH
    )

    small = jnp.concatenate(
        [grad_norm_self, grad_norm_cross, grad_norm_ffn, table.reshape(-1)]
    )
    *sums, small, grad_gate_up = weight_sums(
        tuple(
            partial.astype(BF).reshape(tgts, -1, partial.shape[-1])
            for partial in (grad_self, grad_cross_kv, grad_cross_q, grad_self_o, grad_cross_o)
        ),
        jnp.pad(small, (0, -small.size % 1024)).reshape(-1, 128),
        grad_gate_up,
    )
    grad_down, small = lax.optimization_barrier((grad_down, small))
    grad_down = share(grad_down)
    grad_gate, grad_up, grad_down, *columns = place_units(grad_gate_up, grad_down, sums)
    small = small.reshape(-1)
    norms = [small[start : start + model] for start in range(0, 3 * model, model)]
    table = small[3 * model : 3 * model + table.size].reshape(table.shape)
    return (
        layer_out,
        target_grad,
        memory_grad,
        *norms,
        table,
        columns[0],
        columns[1],
        columns[2],
        columns[6],
        columns[3],
        columns[4],
        columns[5],
        columns[7],
        grad_gate,
        grad_up,
        grad_down,
    )


def solution(mesh):
    owned = P(("tgt", "mem"), None, None)
    held = P("tgt", "mem", None)
    rows = P("tgt", None)
    return jax.shard_map(
        on_device,
        mesh=mesh,
        in_specs=(owned, held, P("tgt"), P("tgt", "mem"), owned, P(), P(), P(), P()) + (rows,) * 11,
        out_specs=(owned, owned, held, P(), P(), P(), P()) + (rows,) * 11,
        check_vma=False,
    )
```

```python
import functools

import jax
import jax.numpy as jnp
import numpy as np
from jax import lax
from jax.experimental import pallas as pl
from jax.experimental.pallas import tpu as pltpu
from jax.sharding import PartitionSpec as P

HEADS = 6
HEAD = 64
BUCKETS = 32
MAX_DIST = 128
ROWS = 192
SPAN = 256
STATS = 128

EPS = 1e-06
NEG = -1e30
HIGH = lax.Precision.HIGHEST
BF = jnp.bfloat16
F32 = jnp.float32
MESH = pl.DeviceIdType.MESH
NT = (((1,), (1,)), ((), ()))
TN = (((0,), (0,)), ((), ()))
VMEM_SPEC = pl.BlockSpec(memory_space=pltpu.VMEM)
ANY_SPEC = pl.BlockSpec(memory_space=pl.ANY)
VMEM_CAP = 56 * 1024 * 1024
FFN_CAP = 62 * 1024 * 1024


def distance_onehot():
    distance = (SPAN - np.arange(SPAN)) % SPAN
    exact_max = BUCKETS // 2
    scaled = (
        np.log(np.maximum(distance, 1) / exact_max)
        / np.log(MAX_DIST / exact_max)
        * (BUCKETS - exact_max)
    )
    far = np.minimum(
        exact_max + np.floor(np.maximum(scaled, 0.0)).astype(np.int64), BUCKETS - 1
    )
    bucket = np.where(distance < exact_max, distance, far)
    return (np.arange(BUCKETS)[:, None] == bucket[None, :]).astype(np.float32)


def dot(left, right):
    return jnp.dot(left, right, preferred_element_type=F32)


def dot_nt(left, right):
    return lax.dot_general(left, right, NT, preferred_element_type=F32)


def dot_tn(left, right):
    return lax.dot_general(left, right, TN, preferred_element_type=F32)


def rms_scale(inputs):
    return lax.rsqrt(jnp.mean(inputs * inputs, axis=-1, keepdims=True) + EPS)


def rms_back(inputs, gain, upstream):
    scale = rms_scale(inputs)
    gu = gain * upstream
    inner = jnp.mean(inputs * gu, axis=-1, keepdims=True)
    dx = scale * gu - inputs * (scale * scale * scale * inner)
    return dx, jnp.sum(upstream * inputs * scale, axis=0)


def half_masks():
    lane = lax.broadcasted_iota(jnp.int32, (1, 2 * HEAD), 1)
    low = (lane < HEAD).astype(BF)
    return low, 1 - low


def stacked(value, masks):
    return jnp.concatenate([value * masks[0], value * masks[1]], axis=0)


def joined_heads(value):
    rows = value.shape[0] // 2
    is_low = lax.broadcasted_iota(jnp.int32, (1, 2 * HEAD), 1) < HEAD
    return jnp.where(is_low, value[:rows], value[rows:])


def pair(index):
    return slice(index * 2 * HEAD, (index + 1) * 2 * HEAD)


def head_bias(base_ref, head):
    row = jnp.broadcast_to(base_ref[head : head + 1, :], (ROWS, SPAN))
    return pltpu.roll(row, 0, 1, stride=1, stride_axis=0)


def two_biases(base_ref, index, causal):
    return jnp.concatenate(
        [jnp.where(causal, head_bias(base_ref, 2 * index + half), NEG) for half in range(2)], axis=0
    )


def causal_mask():
    rows = lax.broadcasted_iota(jnp.int32, (ROWS, SPAN), 0)
    cols = lax.broadcasted_iota(jnp.int32, (ROWS, SPAN), 1)
    return cols <= rows


def self_fwd_kernel(items, qkv_ref, base_ref, att_ref, k_pad, v_pad):
    inner = HEADS * HEAD
    k_pad[...] = jnp.zeros_like(k_pad)
    v_pad[...] = jnp.zeros_like(v_pad)
    for item in range(items):
        k_pad[item, :ROWS, :] = qkv_ref[item, :, inner : 2 * inner]
        v_pad[item, :ROWS, :] = qkv_ref[item, :, 2 * inner :]
    causal = causal_mask()
    masks = half_masks()
    for index in range(HEADS // 2):
        bias = two_biases(base_ref, index, causal)
        for item in range(items):
            query = stacked(qkv_ref[item, :, pair(index)], masks)
            scores = dot_nt(query, k_pad[item, :, pair(index)]) + bias
            top = jnp.max(scores, axis=-1, keepdims=True)
            probs = jnp.exp(scores - top)
            probs = probs * (1.0 / jnp.sum(probs, axis=-1, keepdims=True))
            part = dot(probs.astype(BF), v_pad[item, :, pair(index)])
            att_ref[item, :, pair(index)] = joined_heads(part).astype(BF)


def self_fwd(qkv, base):
    items = qkv.shape[0]
    inner = HEADS * HEAD
    return pl.pallas_call(
        functools.partial(self_fwd_kernel, items),
        out_shape=jax.ShapeDtypeStruct((items, ROWS, inner), BF),
        in_specs=[VMEM_SPEC] * 2,
        out_specs=VMEM_SPEC,
        scratch_shapes=[pltpu.VMEM((items, SPAN, inner), BF)] * 2,
        compiler_params=pltpu.CompilerParams(vmem_limit_bytes=VMEM_CAP),
        cost_estimate=pl.CostEstimate(
            flops=items * HEADS * ROWS * SPAN * 128 * 4,
            bytes_accessed=items * ROWS * inner * 8,
            transcendentals=items * HEADS * ROWS * SPAN,
        ),
        name="self_fwd",
    )(qkv, base)


def diagonal_sums(values):
    total = values[:8]
    for start in range(8, ROWS, 8):
        total = total + pltpu.roll(values[start : start + 8], SPAN - start, 1)
    row = lax.broadcasted_iota(jnp.int32, (8, SPAN), 0)
    for bit in (1, 2, 4):
        total = jnp.where((row & bit) > 0, pltpu.roll(total, SPAN - bit, 1), total)
    return jnp.sum(total, axis=0, keepdims=True)


def self_bwd_kernel(items, qkv_ref, datt_ref, base_ref, dqkv_ref, diag_ref, k_pad, v_pad):
    inner = HEADS * HEAD
    k_pad[...] = jnp.zeros_like(k_pad)
    v_pad[...] = jnp.zeros_like(v_pad)
    diag_ref[...] = jnp.zeros_like(diag_ref)
    for item in range(items):
        k_pad[item, :ROWS, :] = qkv_ref[item, :, inner : 2 * inner]
        v_pad[item, :ROWS, :] = qkv_ref[item, :, 2 * inner :]
    causal = causal_mask()
    masks = half_masks()
    for index in range(HEADS // 2):
        bias = two_biases(base_ref, index, causal)
        ds_sum = None
        for item in range(items):
            query = stacked(qkv_ref[item, :, pair(index)], masks)
            upstream = stacked(datt_ref[item, :, pair(index)], masks)
            keys = k_pad[item, :, pair(index)]
            scores = dot_nt(query, keys) + bias
            top = jnp.max(scores, axis=-1, keepdims=True)
            probs = jnp.exp(scores - top)
            probs = probs * (1.0 / jnp.sum(probs, axis=-1, keepdims=True))
            dprobs = dot_nt(upstream, v_pad[item, :, pair(index)])
            delta = jnp.sum(probs * dprobs, axis=-1, keepdims=True)
            ds = probs * (dprobs - delta)
            ds_sum = ds if item == 0 else ds_sum + ds
            ds_low = ds.astype(BF)
            dqkv_ref[item, :, pair(index)] = joined_heads(dot(ds_low, keys)).astype(BF)
            dqkv_ref[item, :, pair(index + 3)] = dot_tn(ds_low, query)[:ROWS].astype(BF)
            dqkv_ref[item, :, pair(index + 6)] = dot_tn(probs.astype(BF), upstream)[
                :ROWS
            ].astype(BF)
        for half in range(2):
            head = 2 * index + half
            diag_ref[head : head + 1, :] = diagonal_sums(
                ds_sum[half * ROWS : (half + 1) * ROWS]
            )


def self_bwd(qkv, datt, base):
    items = qkv.shape[0]
    inner = HEADS * HEAD
    return pl.pallas_call(
        functools.partial(self_bwd_kernel, items),
        out_shape=(
            jax.ShapeDtypeStruct((items, ROWS, 3 * inner), BF),
            jax.ShapeDtypeStruct((8, SPAN), F32),
        ),
        in_specs=[VMEM_SPEC] * 3,
        out_specs=(VMEM_SPEC, VMEM_SPEC),
        scratch_shapes=[pltpu.VMEM((items, SPAN, inner), BF)] * 2,
        compiler_params=pltpu.CompilerParams(vmem_limit_bytes=VMEM_CAP),
        cost_estimate=pl.CostEstimate(
            flops=items * HEADS * ROWS * SPAN * 128 * 10,
            bytes_accessed=items * ROWS * inner * 14,
            transcendentals=items * HEADS * ROWS * SPAN,
        ),
        name="self_bwd",
    )(qkv, datt, base)


def greet(axis, offsets):
    me = lax.axis_index(axis)
    barrier = pltpu.get_barrier_semaphore()
    for offset in offsets:
        pl.semaphore_signal(
            barrier, inc=1, device_id={axis: jnp.bitwise_xor(me, offset)}, device_id_type=MESH
        )
    pl.semaphore_wait(barrier, len(offsets))


def send(src, dst, send_sem, recv_sem, offset):
    me = lax.axis_index("mem")
    return pltpu.make_async_remote_copy(
        src_ref=src,
        dst_ref=dst,
        send_sem=send_sem,
        recv_sem=recv_sem,
        device_id={"mem": jnp.bitwise_xor(me, offset)},
        device_id_type=MESH,
    )


def column(stats, index):
    return stats[:, index : index + 1]


def spread(stats, index, masks):
    return jnp.where(masks, column(stats, 2 * index), column(stats, 2 * index + 1))


def cross_fwd_kernel(
    items, q_ref, kv_ref, bias_ref, all_ref, att_ref, lse_ref,
    out_o, out_s, in_o, in_s, q_send, q_recv, o_send, o_recv, s_send, s_recv,
):
    me = lax.axis_index("mem")
    greet("mem", (1, 2, 3))
    q_to_core = send(q_ref, all_ref.at[1], q_send.at[0], q_recv.at[0], 1)
    q_to_far = send(q_ref, all_ref.at[2], q_send.at[1], q_recv.at[1], 2)
    q_relay = send(all_ref.at[2], all_ref.at[3], q_send.at[2], q_recv.at[2], 1)
    q_to_far.start()
    q_to_core.start()
    all_ref[0] = q_ref[...]
    low, high = half_masks()
    lane = lax.broadcasted_iota(jnp.int32, (1, STATS), 1)
    is_low = lax.broadcasted_iota(jnp.int32, (1, 2 * HEAD), 1) < HEAD
    copies = []
    for slot in (0, 2, 3, 1):
        if slot == 2:
            q_to_far.wait_recv()
            q_relay.start()
        if slot == 3:
            q_relay.wait_recv()
        if slot == 1:
            q_to_core.wait_recv()
        owner = jnp.bitwise_xor(me, slot)
        for item in range(items):
            place = owner * items + item
            bias = bias_ref[place]
            stats = jnp.zeros((ROWS, STATS), F32)
            for index in range(HEADS // 2):
                both = all_ref[slot, item, :, pair(index)]
                keys = kv_ref[place, :, pair(index)]
                values = kv_ref[place, :, pair(index + HEADS // 2)]
                scores = dot_nt(stacked(both, (low, high)), keys) + bias
                top = jnp.max(scores, axis=-1, keepdims=True)
                probs = jnp.exp(scores - top)
                amount = jnp.sum(probs, axis=-1, keepdims=True)
                total = joined_heads(dot(probs.astype(BF), values) * (1.0 / amount))
                level = top + jnp.log(amount)
                for half in range(2):
                    stats = jnp.where(
                        lane == 2 * index + half, level[half * ROWS : (half + 1) * ROWS], stats
                    )
                out_o[slot, item, :, pair(index)] = total.astype(BF)
            out_s[slot, item] = stats.T[:8]
        if slot:
            copies.append(send(out_o.at[slot], in_o.at[slot], o_send.at[slot], o_recv.at[slot], slot))
            copies.append(send(out_s.at[slot], in_s.at[slot], s_send.at[slot], s_recv.at[slot], slot))
            copies[-2].start()
            copies[-1].start()
    q_to_core.wait_send()
    q_to_far.wait_send()
    q_relay.wait_send()
    for copy in copies:
        copy.wait()
    for item in range(items):
        stats = [
            jnp.concatenate([part, jnp.zeros((STATS - 8, ROWS), F32)], axis=0).T
            for part in [out_s[0, item]] + [in_s[slot, item] for slot in (1, 2, 3)]
        ]
        top = jnp.maximum(jnp.maximum(stats[0], stats[1]), jnp.maximum(stats[2], stats[3]))
        shares = [jnp.exp(part - top) for part in stats]
        amount = shares[0] + shares[1] + shares[2] + shares[3]
        lse_ref[item] = top + jnp.log(amount)
        scale = 1.0 / amount
        shares = [part * scale for part in shares]
        for index in range(HEADS // 2):
            total = out_o[0, item, :, pair(index)].astype(F32) * spread(shares[0], index, is_low)
            for slot in (1, 2, 3):
                total += in_o[slot, item, :, pair(index)].astype(F32) * spread(
                    shares[slot], index, is_low
                )
            att_ref[item, :, pair(index)] = total.astype(BF)


def cross_fwd(queries, keys_values, bias):
    items = queries.shape[0]
    inner = HEADS * HEAD
    block = (4, items, ROWS, inner)
    stat_block = (4, items, 8, ROWS)
    flops = 4 * items * HEADS * ROWS * SPAN * 128 * 4
    return pl.pallas_call(
        functools.partial(cross_fwd_kernel, items),
        out_shape=(
            jax.ShapeDtypeStruct(block, BF),
            jax.ShapeDtypeStruct((items, ROWS, inner), BF),
            jax.ShapeDtypeStruct((items, ROWS, STATS), F32),
        ),
        in_specs=[VMEM_SPEC] * 3,
        out_specs=(VMEM_SPEC,) * 3,
        scratch_shapes=[
            pltpu.VMEM(block, BF),
            pltpu.VMEM(stat_block, F32),
            pltpu.VMEM(block, BF),
            pltpu.VMEM(stat_block, F32),
            pltpu.SemaphoreType.DMA((3,)),
            pltpu.SemaphoreType.DMA((3,)),
            pltpu.SemaphoreType.DMA((4,)),
            pltpu.SemaphoreType.DMA((4,)),
            pltpu.SemaphoreType.DMA((4,)),
            pltpu.SemaphoreType.DMA((4,)),
        ],
        compiler_params=pltpu.CompilerParams(
            collective_id=1, has_side_effects=True, vmem_limit_bytes=VMEM_CAP
        ),
        cost_estimate=pl.CostEstimate(
            flops=flops, bytes_accessed=8 * 1024 * 1024, transcendentals=flops // 512
        ),
        name="cross_fwd",
    )(queries, keys_values, bias)


def cross_bwd_kernel(
    items, all_ref, back_ref, stat_ref, kv_ref, bias_ref, dkv_ref, dq_ref,
    all_b, all_s, out_q, in_q, b_send, b_recv, s_send, s_recv, q_send, q_recv,
):
    me = lax.axis_index("mem")
    greet("mem", (1, 2, 3))
    moves = []
    for offset, slot, source in ((2, 2, None), (1, 1, None), (1, 3, 2)):
        number = len(moves)
        moves.append(
            (
                send(back_ref if source is None else all_b.at[source], all_b.at[slot],
                     b_send.at[number], b_recv.at[number], offset),
                send(stat_ref if source is None else all_s.at[source], all_s.at[slot],
                     s_send.at[number], s_recv.at[number], offset),
            )
        )
    for move in moves[:2]:
        for copy in move:
            copy.start()
    low, high = half_masks()
    copies = []
    for slot in (0, 2, 3, 1):
        if slot == 2:
            for copy in moves[0]:
                copy.wait_recv()
            for copy in moves[2]:
                copy.start()
        if slot == 3:
            for copy in moves[2]:
                copy.wait_recv()
        if slot == 1:
            for copy in moves[1]:
                copy.wait_recv()
        owner = jnp.bitwise_xor(me, slot)
        for item in range(items):
            place = owner * items + item
            bias = bias_ref[place]
            stats = stat_ref[item] if slot == 0 else all_s[slot, item]
            stats = jnp.concatenate([stats, jnp.zeros((STATS - 16, ROWS), F32)], axis=0).T
            for index in range(HEADS // 2):
                both = all_ref[slot, item, :, pair(index)]
                if slot == 0:
                    upstream = back_ref[item, :, pair(index)]
                else:
                    upstream = all_b[slot, item, :, pair(index)]
                keys = kv_ref[place, :, pair(index)]
                values = kv_ref[place, :, pair(index + HEADS // 2)]
                query = stacked(both, (low, high))
                back = stacked(upstream, (low, high))

                def both_columns(start, index=index, stats=stats):
                    return jnp.concatenate(
                        [column(stats, start + 2 * index + half) for half in range(2)], axis=0
                    )

                scores = dot_nt(query, keys) + bias
                probs = jnp.exp(scores - both_columns(0))
                dprobs = dot_nt(back, values)
                ds = (probs * (dprobs - both_columns(8))).astype(BF)
                dq = joined_heads(dot(ds, keys))
                dk = dot_tn(ds, query)
                dv = dot_tn(probs.astype(BF), back)
                out_q[slot, item, :, pair(index)] = dq.astype(BF)
                dkv_ref[place, :, pair(index)] = dk.astype(BF)
                dkv_ref[place, :, pair(index + HEADS // 2)] = dv.astype(BF)
        if slot:
            copies.append(send(out_q.at[slot], in_q.at[slot], q_send.at[slot], q_recv.at[slot], slot))
            copies[-1].start()
    for move in moves:
        for copy in move:
            copy.wait_send()
    for copy in copies:
        copy.wait()
    for item in range(items):
        for index in range(HEADS // 2):
            total = out_q[0, item, :, pair(index)].astype(F32)
            for slot in (1, 2, 3):
                total += in_q[slot, item, :, pair(index)].astype(F32)
            dq_ref[item, :, pair(index)] = total.astype(BF)


def cross_bwd(all_queries, back, stats, keys_values, bias):
    items = back.shape[0]
    inner = HEADS * HEAD
    block = (4, items, ROWS, inner)
    flops = 4 * items * HEADS * ROWS * SPAN * 128 * 10
    return pl.pallas_call(
        functools.partial(cross_bwd_kernel, items),
        out_shape=(
            jax.ShapeDtypeStruct(keys_values.shape, BF),
            jax.ShapeDtypeStruct((items, ROWS, inner), BF),
        ),
        in_specs=[VMEM_SPEC] * 5,
        out_specs=(VMEM_SPEC,) * 2,
        scratch_shapes=[
            pltpu.VMEM(block, BF),
            pltpu.VMEM((4, items, 16, ROWS), F32),
            pltpu.VMEM(block, BF),
            pltpu.VMEM(block, BF),
            pltpu.SemaphoreType.DMA((3,)),
            pltpu.SemaphoreType.DMA((3,)),
            pltpu.SemaphoreType.DMA((3,)),
            pltpu.SemaphoreType.DMA((3,)),
            pltpu.SemaphoreType.DMA((4,)),
            pltpu.SemaphoreType.DMA((4,)),
        ],
        compiler_params=pltpu.CompilerParams(
            collective_id=2, has_side_effects=True, vmem_limit_bytes=VMEM_CAP
        ),
        cost_estimate=pl.CostEstimate(
            flops=flops, bytes_accessed=12 * 1024 * 1024, transcendentals=flops // 1280
        ),
        name="cross_bwd",
    )(all_queries, back, stats, keys_values, bias)


CUBIC = 0.044715
ROOT = float(np.sqrt(2.0 / np.pi))


def strips(width, step):
    return [(start, min(step, width - start)) for start in range(0, width, step)]


def ffn_kernel(
    items, h_ref, up0_ref, up1_ref, up2_ref, up3_ref, gate_up_hbm, down_hbm,
    h_back_ref, near_ref, far_ref, grad_gu_hbm, grad_down_hbm,
    gate_up_ref, down_ref, h_all, u_all, hidden, two_back, h_part, y_part, h_in, y_in, gu_strip, down_strip,
    h_send, h_recv, d_send, d_recv, y_send, y_recv, load_sem, up_sem, store_sem,
):
    tokens, model = h_ref.shape
    last = 1 + items
    rows = tokens // items
    units = down_ref.shape[0]
    loads = [
        pltpu.make_async_copy(gate_up_hbm, gate_up_ref, load_sem.at[0]),
        pltpu.make_async_copy(down_hbm, down_ref, load_sem.at[1]),
        pltpu.make_async_copy(up0_ref, u_all.at[0], load_sem.at[2]),
        pltpu.make_async_copy(up1_ref, u_all.at[last], load_sem.at[3]),
    ]
    for copy in loads:
        copy.start()
    ups = []
    for item in range(items):
        mine = pl.ds(item * rows, rows)
        for place, ref in enumerate((up2_ref, up3_ref)):
            ups.append(
                pltpu.make_async_copy(
                    ref.at[mine], u_all.at[1 + item, pl.ds(place * rows, rows)],
                    up_sem.at[item, place],
                )
            )
            ups[-1].start()
    greet("mem", (1, 2))
    h_to_core = send(h_ref, h_all.at[last], h_send.at[0], h_recv.at[0], 1)
    h_to_far, h_relay, d_pass, d_far, y_pass = [], [], [], [], []
    first, second = pl.ds(0, rows), pl.ds(rows, rows)
    for item in range(items):
        block = at = 1 + item
        h_to_far.append(
            send(h_ref.at[pl.ds(item * rows, rows)], h_all.at[block, first],
                 h_send.at[at], h_recv.at[at], 2)
        )
        h_relay.append(
            send(h_all.at[block, first], h_all.at[block, second],
                 h_send.at[at + items], h_recv.at[at + items], 1)
        )
        d_pass.append(
            send(h_part.at[block, second], h_in.at[1, pl.ds(item * rows, rows)],
                 d_send.at[at], d_recv.at[at], 1)
        )
        y_pass.append(
            send(y_part.at[block, second], y_in.at[1, pl.ds(item * rows, rows)],
                 y_send.at[at], y_recv.at[at], 1)
        )
        d_far.append(
            send(h_part.at[block, first], h_in.at[2, pl.ds(item * rows, rows)],
                 d_send.at[at + items], d_recv.at[at + items], 2)
        )
    d_near = send(h_part.at[last], h_in.at[0], d_send.at[0], d_recv.at[0], 1)
    y_near = send(y_part.at[last], y_in.at[0], y_send.at[0], y_recv.at[0], 1)
    h_to_core.start()
    h_to_far[0].start()
    h_all[0] = h_ref[...]
    for copy in loads:
        copy.wait()
    for copy in ups:
        copy.wait()

    def give_back(item):
        mine = pl.ds(item * rows, rows)
        d_pass[item].wait_recv()
        h_part[1 + item, first, :] = (
            h_part[1 + item, first, :].astype(F32) + h_in[1, mine, :].astype(F32)
        ).astype(BF)
        d_far[item].start()

    def token_block(slot, carry):
        @pl.when(slot == last)
        def _():
            h_to_core.wait_recv()

        for item in range(items):

            @pl.when(slot == 1 + item)
            def _(item=item):
                h_relay[item].wait_recv()

            @pl.when(slot == 2 + item)
            def _(item=item):
                d_pass[item].start()
                y_pass[item].start()

        def units_block(block, inside):
            pairs = pl.ds(pl.multiple_of(block * 256, 256), 256)
            ones = pl.ds(pl.multiple_of(block * 128, 128), 128)
            both = dot(h_all[slot], gate_up_ref[:, pairs])
            back = dot_nt(u_all[slot], down_ref[ones, :]).astype(BF).astype(F32)
            gate, up = both[:, :128], both[:, 128:]
            square = gate * gate
            bend = jnp.tanh(ROOT * gate * (1.0 + CUBIC * square))
            share = 0.5 * (1.0 + bend)
            active = gate * share
            slope = share + 0.5 * gate * (1.0 - bend * bend) * (
                ROOT * (1.0 + 3.0 * CUBIC * square)
            )
            hidden[slot, :, ones] = (active * up).astype(BF)
            two_back[slot, :, pairs] = jnp.concatenate(
                [(back * up * slope).astype(BF), (back * active).astype(BF)], axis=1
            )
            return inside

        lax.fori_loop(0, units // 128, units_block, 0)
        for item in range(1, items):

            @pl.when(slot == item - 1)
            def _(item=item):
                h_to_far[item].start()

        for start, width in strips(model, 256):
            part = slice(start, start + width)
            h_part[slot, :, part] = dot_nt(two_back[slot], gate_up_ref[part, :]).astype(BF)
        for item in range(items):

            @pl.when(slot == item)
            def _(item=item):
                h_to_far[item].wait_recv()
                h_relay[item].start()

            @pl.when(slot == 2 + item)
            def _(item=item):
                give_back(item)

        for start, width in strips(model, 256):
            part = slice(start, start + width)
            y_part[slot, :, part] = dot(hidden[slot], down_ref[:, part]).astype(BF)
        return carry

    lax.fori_loop(0, 2 + items, token_block, 0)
    d_near.start()
    y_near.start()
    count = (2 + items) * tokens
    stores = []

    def store(value, strip, hbm, start, width):
        number = len(stores)
        if number >= 2:
            stores[number - 2].wait()
        strip[number % 2, :width, :] = value
        stores.append(
            pltpu.make_async_copy(
                strip.at[number % 2, pl.ds(0, width)],
                hbm.at[pl.ds(start, width)],
                store_sem.at[number],
            )
        )
        stores[-1].start()

    for start, width in strips(model, 256):
        part = slice(start, start + width)
        value = dot_tn(
            h_all[:, :, part].reshape(count, width), two_back[...].reshape(count, 2 * units)
        )
        store(value.astype(BF), gu_strip, grad_gu_hbm, start, width)
    for start, width in strips(units, 256):
        part = slice(start, start + width)
        value = dot_tn(
            hidden[:, :, part].reshape(count, width), u_all[...].reshape(count, model)
        )
        store(value.astype(BF), down_strip, grad_down_hbm, start, width)
    for item in range(items):
        mine = pl.ds(item * rows, rows)
        y_pass[item].wait_recv()
        far_ref[mine, :] = (
            y_part[1 + item, first, :].astype(F32) + y_in[1, mine, :].astype(F32)
        ).astype(BF)
    y_near.wait_recv()
    near_ref[...] = (y_part[0].astype(F32) + y_in[0].astype(F32)).astype(BF)
    d_near.wait_recv()
    for copy in d_far:
        copy.wait_recv()
    h_back_ref[...] = (
        h_part[0].astype(F32) + h_in[0].astype(F32) + h_in[2].astype(F32)
    )
    for copy in stores[-2:]:
        copy.wait()
    for copy in (h_to_core, d_near, y_near, *h_to_far, *h_relay, *d_pass, *y_pass, *d_far):
        copy.wait_send()


def ffn(h3, upstreams, gate_up, down, items):
    tokens, model = h3.shape
    units = down.shape[0]
    every = (2 + items, tokens, model)
    flops = (2 + items) * tokens * model * units * 18
    grads = len(strips(model, 256)) + len(strips(units, 256))
    return pl.pallas_call(
        functools.partial(ffn_kernel, items),
        out_shape=(
            jax.ShapeDtypeStruct((tokens, model), F32),
            jax.ShapeDtypeStruct((tokens, model), BF),
            jax.ShapeDtypeStruct((tokens, model), BF),
            jax.ShapeDtypeStruct((model, 2 * units), BF),
            jax.ShapeDtypeStruct((units, model), BF),
        ),
        in_specs=[VMEM_SPEC] + [ANY_SPEC] * 6,
        out_specs=(VMEM_SPEC,) * 3 + (ANY_SPEC,) * 2,
        scratch_shapes=[
            pltpu.VMEM((model, 2 * units), BF),
            pltpu.VMEM((units, model), BF),
            pltpu.VMEM(every, BF),
            pltpu.VMEM(every, BF),
            pltpu.VMEM((2 + items, tokens, units), BF),
            pltpu.VMEM((2 + items, tokens, 2 * units), BF),
            pltpu.VMEM(every, BF),
            pltpu.VMEM(every, BF),
            pltpu.VMEM((3, tokens, model), BF),
            pltpu.VMEM((2, tokens, model), BF),
            pltpu.VMEM((2, 256, 2 * units), BF),
            pltpu.VMEM((2, 256, model), BF),
        ]
        + [pltpu.SemaphoreType.DMA((1 + 2 * items,))] * 4
        + [pltpu.SemaphoreType.DMA((1 + items,))] * 2
        + [
            pltpu.SemaphoreType.DMA((4,)),
            pltpu.SemaphoreType.DMA((items, 2)),
            pltpu.SemaphoreType.DMA((grads,)),
        ],
        compiler_params=pltpu.CompilerParams(
            collective_id=3, has_side_effects=True, vmem_limit_bytes=FFN_CAP
        ),
        cost_estimate=pl.CostEstimate(
            flops=flops, bytes_accessed=32 * 1024 * 1024, transcendentals=4 * tokens * units
        ),
        name="feed_forward",
    )(h3, *upstreams, gate_up, down)


def peer_copy(src, dst, send_sem, recv_sem, tgt=None, mem=None):
    where = {}
    if tgt is not None:
        where["tgt"] = tgt
    if mem is not None:
        where["mem"] = mem
    return pltpu.make_async_remote_copy(
        src_ref=src, dst_ref=dst, send_sem=send_sem, recv_sem=recv_sem,
        device_id=where, device_id_type=MESH,
    )


def greet_all(mem, tgt):
    barrier = pltpu.get_barrier_semaphore()
    for offset in (1, 2, 3):
        pl.semaphore_signal(
            barrier, inc=1, device_id={"mem": jnp.bitwise_xor(mem, offset)}, device_id_type=MESH
        )
    for offset in (1, 2, 4, 6):
        pl.semaphore_signal(
            barrier, inc=1, device_id={"tgt": jnp.bitwise_xor(tgt, offset)}, device_id_type=MESH
        )
    pl.semaphore_wait(barrier, 7)


FIRST = (1, 2, 4, 6)
PASSED = (3, 5, 7)


def gather_kernel(
    self_q, self_k, self_v, cross_q, cross_k, cross_v, self_o, cross_o,
    qkv_out, kv_out, cq_out, so_out, co_out,
    t_send, t_recv, x_send, x_recv, c_send, c_recv, r_send, r_recv, own_sem,
):
    mem = lax.axis_index("mem")
    tgt = lax.axis_index("tgt")
    inner = HEADS * HEAD

    def part(out, index):
        return lambda place: out.at[place, :, index * inner : (index + 1) * inner]

    def whole(out):
        return lambda place: out.at[place]

    groups = (
        ((self_q, part(qkv_out, 0)), (self_k, part(qkv_out, 1))),
        ((self_v, part(qkv_out, 2)), (cross_q, part(cq_out, 0))),
        ((cross_k, part(kv_out, 0)), (cross_v, part(kv_out, 1))),
        ((self_o, whole(so_out)), (cross_o, whole(co_out))),
    )
    greet_all(mem, tgt)
    near = jnp.bitwise_xor(mem, 1)
    far = jnp.bitwise_xor(mem, 2)

    def over_tgt(member, number, step, offset):
        src, dst = member
        if step < 4:
            return peer_copy(
                src, dst(tgt), t_send.at[step, number], t_recv.at[step, number],
                tgt=jnp.bitwise_xor(tgt, offset),
            )
        place = jnp.bitwise_xor(tgt, offset - 1)
        return peer_copy(
            dst(place), dst(place), t_send.at[step, number], t_recv.at[step, number],
            tgt=jnp.bitwise_xor(tgt, 1),
        )

    def over_far(member, number, step, offset):
        dst = member[1](jnp.bitwise_xor(tgt, offset))
        return peer_copy(dst, dst, x_send.at[step, number], x_recv.at[step, number], mem=far)

    def over_near(member, number, step, offset):
        dst = member[1](jnp.bitwise_xor(tgt, offset))
        return peer_copy(dst, dst, c_send.at[step, number], c_recv.at[step, number], mem=near)

    def relay(member, number, step, offset):
        dst = member[1](jnp.bitwise_xor(tgt, offset))
        return peer_copy(dst, dst, r_send.at[step, number], r_recv.at[step, number], mem=near)

    steps = list(enumerate(FIRST + PASSED))
    for index, group in enumerate(groups):

        @pl.when(mem == index)
        def _(index=index, group=group):
            members = list(enumerate(group))
            far_members = list(enumerate(groups[index ^ 2]))
            near_members = list(enumerate(groups[index ^ 1]))
            last_members = list(enumerate(groups[index ^ 3]))
            extra = []
            far_sent = members
            far_got = far_members
            for step, offset in steps[:4]:
                for number, member in members + extra:
                    over_tgt(member, number, step, offset).start()
            own = []
            for place, (src, dst) in enumerate(member for all_of in groups for member in all_of):
                own.append(pltpu.make_async_copy(src, dst(tgt), own_sem.at[place]))
                own[-1].start()
            for step, offset in steps:
                for number, member in members:
                    over_tgt(member, number, step, offset).wait_recv()
                    if 0 < step < 4:
                        over_tgt(member, number, step + 3, offset + 1).start()
                    if (number, member) in far_sent:
                        over_far(member, number, step, offset).start()
                    over_near(member, number, step, offset).start()
                for number, member in extra:
                    over_tgt(member, number, step, offset).wait_recv()
                    if 0 < step < 4:
                        over_tgt(member, number, step + 3, offset + 1).start()
                    relay(member, 0, step, offset).start()
            for step, offset in steps:
                for number, member in far_got:
                    over_far(member, number, step, offset).wait_recv()
                    relay(member, number, step, offset).start()
            for step, offset in steps:
                for number, member in near_members:
                    over_near(member, number, step, offset).wait_recv()
                for number, member in last_members:
                    relay(member, number, step, offset).wait_recv()
                for number, member in members + extra:
                    over_tgt(member, number, step, offset).wait_send()
                for number, member in far_sent:
                    over_far(member, number, step, offset).wait_send()
                for number, member in members:
                    over_near(member, number, step, offset).wait_send()
                for number, member in far_members:
                    relay(member, number, step, offset).wait_send()
            for copy in own:
                copy.wait()


def gather_weights(weights):
    tgts = lax.axis_size("tgt")
    rows, inner = weights[0].shape
    o_rows, model = weights[-1].shape

    def out(columns, height=rows):
        return jax.ShapeDtypeStruct((tgts, height, columns), BF)

    shapes = (out(3 * inner), out(2 * inner), out(inner), out(model, o_rows), out(model, o_rows))
    sems = [pltpu.SemaphoreType.DMA((7, 3))] * 2 + [pltpu.SemaphoreType.DMA((7, 2))] * 6
    return pl.pallas_call(
        gather_kernel,
        out_shape=shapes,
        in_specs=[ANY_SPEC] * 8,
        out_specs=(ANY_SPEC,) * 5,
        scratch_shapes=sems + [pltpu.SemaphoreType.DMA((8,))],
        compiler_params=pltpu.CompilerParams(collective_id=4, has_side_effects=True),
        cost_estimate=pl.CostEstimate(
            flops=0, bytes_accessed=150 * 1024 * 1024, transcendentals=0
        ),
        name="gather_weights",
    )(*weights)


TURNS = (7, 6, 5, 4, 3, 2, 1, 0)


def reduce_kernel(
    qkv_ref, kv_ref, cq_ref, so_ref, co_ref, small_ref, units_ref,
    q_out, k_out, v_out, cq_out, ck_out, cv_out, so_out, co_out, small_out, units_out,
    small_in, s_send, s_recv, u_send, u_recv, u_own,
    wide_in, tall_in, wide_x, tall_x, wide_y, tall_y, wide_z, tall_z, wide_e, tall_e,
    a_send, a_recv, b_send, b_recv, x_send, x_recv, y_send, y_recv, z_send, z_recv,
    e_send, e_recv,
):
    mem = lax.axis_index("mem")
    tgt = lax.axis_index("tgt")
    inner = HEADS * HEAD

    def part(ref, index):
        return lambda place: ref.at[place, :, index * inner : (index + 1) * inner]

    def whole(ref):
        return lambda place: ref.at[place]

    wide = (wide_in, wide_x, wide_y, wide_z, wide_e)
    tall = (tall_in, tall_x, tall_y, tall_z, tall_e)
    groups = (
        ((part(qkv_ref, 0), q_out, wide), (part(qkv_ref, 1), k_out, wide)),
        ((part(qkv_ref, 2), v_out, wide), (part(cq_ref, 0), cq_out, wide)),
        ((part(kv_ref, 0), ck_out, wide), (part(kv_ref, 1), cv_out, wide)),
        ((whole(so_ref), so_out, tall), (whole(co_ref), co_out, tall)),
    )
    greet_all(mem, tgt)
    near = jnp.bitwise_xor(mem, 1)
    far = jnp.bitwise_xor(mem, 2)

    def to_near(member, number, step, lane):
        place = jnp.bitwise_xor(tgt, TURNS[step])
        send_sems, recv_sems = ((a_send, a_recv), (b_send, b_recv))[lane]
        return peer_copy(
            member[0](place), member[2][0].at[lane, step, number],
            send_sems.at[step, number], recv_sems.at[step, number], mem=near,
        )

    def to_far(member, number, step):
        buffer = member[2][1]
        return peer_copy(
            buffer.at[0, step, number], buffer.at[1, step, number],
            x_send.at[step, number], x_recv.at[step, number], mem=far,
        )

    def to_side(member, number, turn):
        buffer = member[2][2]
        return peer_copy(
            buffer.at[0, turn, number], buffer.at[1, turn, number],
            y_send.at[turn, number], y_recv.at[turn, number], tgt=jnp.bitwise_xor(tgt, 1),
        )

    def to_owner(member, number, turn):
        buffer = member[2][3]
        return peer_copy(
            buffer.at[0, turn, number], buffer.at[1, turn, number],
            z_send.at[turn, number], z_recv.at[turn, number],
            tgt=jnp.bitwise_xor(tgt, TURNS[2 * turn + 1]),
        )

    def to_all(member, number, lane, peer):
        buffer = member[2][4]
        return peer_copy(
            buffer.at[2 if lane == 2 else 0, number],
            buffer.at[(1, 2, 3)[lane], number],
            e_send.at[lane, number], e_recv.at[lane, number], mem=peer,
        )

    z_place = tgt // 2
    y_place = tgt % 2
    small_mem = [
        peer_copy(small_in.at[mem], small_in.at[mem], s_send.at[offset], s_recv.at[offset],
                  mem=jnp.bitwise_xor(mem, offset))
        for offset in (1, 2, 3)
    ]
    small_y = peer_copy(small_in.at[4 + y_place], small_in.at[4 + y_place], s_send.at[0],
                        s_recv.at[0], tgt=jnp.bitwise_xor(tgt, 1))
    small_z = [
        peer_copy(small_in.at[6 + z_place], small_in.at[6 + z_place], s_send.at[3 + offset],
                  s_recv.at[3 + offset], tgt=jnp.bitwise_xor(tgt, 2 * offset))
        for offset in (1, 2, 3)
    ]
    small_in[mem] = small_ref[...]
    for move in small_mem:
        move.start()

    share_far = peer_copy(units_ref, units_out.at[mem], u_send.at[0], u_recv.at[0], mem=far)
    share_near = peer_copy(units_ref, units_out.at[mem], u_send.at[1], u_recv.at[1], mem=near)
    share_on = peer_copy(units_out.at[far], units_out.at[far], u_send.at[2], u_recv.at[2], mem=near)
    share_own = pltpu.make_async_copy(units_ref, units_out.at[mem], u_own)
    share_own.start()

    for index, group in enumerate(groups):

        @pl.when(mem == index)
        def _(index=index, group=group):
            mine = list(enumerate(group))
            near_group = list(enumerate(groups[index ^ 1]))
            far_group = list(enumerate(groups[index ^ 2]))
            last_group = list(enumerate(groups[index ^ 3]))
            steps = range(len(TURNS))
            for step in steps:
                for number, member in last_group:
                    to_near(member, number, step, 1).start()
                for number, member in near_group:
                    to_near(member, number, step, 0).start()
            for step in steps:
                place = jnp.bitwise_xor(tgt, TURNS[step])
                for number, member in far_group:
                    to_near(member, number, step, 1).wait_recv()
                    member[2][1][0, step, number] = (
                        member[0](place)[...].astype(F32)
                        + member[2][0][1, step, number].astype(F32)
                    ).astype(BF)
                    to_far(member, number, step).start()
            for move in small_mem:
                move.wait_recv()
            small_in[4 + y_place] = (small_in[0] + small_in[1]) + (small_in[2] + small_in[3])
            small_y.start()
            def mem_sum(member, number, step):
                to_near(member, number, step, 0).wait_recv()
                to_far(member, number, step).wait_recv()
                return (
                    member[0](jnp.bitwise_xor(tgt, TURNS[step]))[...].astype(F32)
                    + member[2][0][0, step, number].astype(F32)
                    + member[2][1][1, step, number].astype(F32)
                )

            def for_side(turn):
                for number, member in mine:
                    member[2][2][0, turn, number] = mem_sum(member, number, 2 * turn).astype(BF)
                    to_side(member, number, turn).start()

            for_side(0)
            small_y.wait_recv()
            small_in[6 + z_place] = small_in[4] + small_in[5]
            for move in small_z:
                move.start()
            for_side(1)
            for_side(2)
            for_side(3)
            share_far.start()
            share_near.start()
            for turn in range(4):
                for number, member in mine:
                    total = mem_sum(member, number, 2 * turn + 1)
                    to_side(member, number, turn).wait_recv()
                    total = total + member[2][2][1, turn, number].astype(F32)
                    if turn < 3:
                        member[2][3][0, turn, number] = total.astype(BF)
                        to_owner(member, number, turn).start()
                        continue
                    member[2][4][0, number] = total.astype(BF)
            for number, member in mine:
                total = member[2][4][0, number].astype(F32)
                for other in range(3):
                    to_owner(member, number, other).wait_recv()
                    total = total + member[2][3][1, other, number].astype(F32)
                member[2][4][0, number] = total.astype(BF)
                to_all(member, number, 1, far).start()
                to_all(member, number, 0, near).start()
                member[1][...] = member[2][4][0, number]
            for number, member in far_group:
                to_all(member, number, 1, far).wait_recv()
                to_all(member, number, 2, near).start()
                member[1][...] = member[2][4][2, number]
            for number, member in near_group:
                to_all(member, number, 0, near).wait_recv()
                member[1][...] = member[2][4][1, number]
            for number, member in last_group:
                to_all(member, number, 2, near).wait_recv()
                member[1][...] = member[2][4][3, number]
            for move in small_z:
                move.wait_recv()
            small_out[...] = (small_in[6] + small_in[7]) + (small_in[8] + small_in[9])
            share_far.wait_recv()
            share_on.start()
            share_near.wait_recv()
            share_on.wait_recv()
            share_own.wait()
            for move in (*small_mem, small_y, *small_z, share_far, share_near, share_on):
                move.wait_send()
            for step in steps:
                for number, member in last_group:
                    to_near(member, number, step, 1).wait_send()
                for number, member in near_group:
                    to_near(member, number, step, 0).wait_send()
                for number, member in far_group:
                    to_far(member, number, step).wait_send()
            for number, member in mine:
                for turn in range(4):
                    to_side(member, number, turn).wait_send()
                for turn in range(3):
                    to_owner(member, number, turn).wait_send()
                to_all(member, number, 0, near).wait_send()
                to_all(member, number, 1, far).wait_send()
            for number, member in far_group:
                to_all(member, number, 2, near).wait_send()


def reduce_weights(d_qkv, d_kv, d_cq, d_so, d_co, small, units):
    rows, inner = d_cq.shape[1:]
    o_rows, model = d_so.shape[1:]
    wide, tall = (rows, inner), (o_rows, model)
    scratch = []
    for lead in ((2, 8, 2), (2, 8, 2), (2, 4, 2), (2, 3, 2), (4, 2)):
        scratch += [pltpu.VMEM(lead + wide, BF), pltpu.VMEM(lead + tall, BF)]
    sems = []
    for count in (8, 8, 8, 4, 3, 3):
        sems += [pltpu.SemaphoreType.DMA((count, 2))] * 2
    return pl.pallas_call(
        reduce_kernel,
        out_shape=tuple(jax.ShapeDtypeStruct(wide, BF) for _ in range(6))
        + tuple(jax.ShapeDtypeStruct(tall, BF) for _ in range(2))
        + (
            jax.ShapeDtypeStruct(small.shape, F32),
            jax.ShapeDtypeStruct((4,) + units.shape, BF),
        ),
        in_specs=[VMEM_SPEC] * 6 + [ANY_SPEC],
        out_specs=(VMEM_SPEC,) * 9 + (ANY_SPEC,),
        scratch_shapes=[pltpu.VMEM((10,) + small.shape, F32)]
        + [pltpu.SemaphoreType.DMA((7,))] * 2
        + [pltpu.SemaphoreType.DMA((3,))] * 2
        + [pltpu.SemaphoreType.DMA]
        + scratch
        + sems,
        compiler_params=pltpu.CompilerParams(
            collective_id=5, has_side_effects=True, vmem_limit_bytes=VMEM_CAP
        ),
        cost_estimate=pl.CostEstimate(
            flops=0, bytes_accessed=150 * 1024 * 1024, transcendentals=0
        ),
        name="reduce_weights",
    )(d_qkv, d_kv, d_cq, d_so, d_co, small, units)


def pick_kernel(tgts, groups, gate_ref, up_ref, out_ref):
    mem = lax.axis_index("mem")
    shard = gate_ref.shape[1] // tgts
    piece = shard // groups

    for group in range(groups):

        @pl.when(mem == group)
        def _(group=group):
            for number, ref in enumerate((gate_ref, up_ref)):
                parts = []
                for place in range(tgts):
                    start = place * shard + group * piece
                    parts.append(ref[:, start : start + piece].astype(F32))
                quarter = jnp.concatenate(parts, axis=1).astype(BF)
                for block in range(quarter.shape[1] // 128):
                    start = block * 256 + number * 128
                    out_ref[:, start : start + 128] = quarter[:, block * 128 : block * 128 + 128]


def pick_units(gate, up):
    groups, tgts = lax.axis_size("mem"), lax.axis_size("tgt")
    rows, units = gate.shape
    return pl.pallas_call(
        functools.partial(pick_kernel, tgts, groups),
        out_shape=jax.ShapeDtypeStruct((rows, 2 * units // groups), BF),
        in_specs=[VMEM_SPEC] * 2,
        out_specs=VMEM_SPEC,
        compiler_params=pltpu.CompilerParams(vmem_limit_bytes=VMEM_CAP),
        name="pick_units",
    )(gate, up)


def place_kernel(tgts, groups, parts_ref, down_parts_ref, *refs):
    count = (len(refs) - 3) // 2
    gate_ref, up_ref, down_ref = refs[count : count + 3]
    for src, dst in zip(refs[:count], refs[count + 3 :]):
        dst[...] = src[...].astype(F32)
    height = down_parts_ref.shape[1]
    for group in range(groups):
        down_ref[group * height : (group + 1) * height, :] = down_parts_ref[group].astype(F32)
    units = gate_ref.shape[1]
    piece = units // tgts // groups
    for number, ref in enumerate((gate_ref, up_ref)):
        quarters = []
        for group in range(groups):
            blocks = [
                parts_ref[group, :, start : start + 128]
                for start in range(number * 128, 2 * units // groups, 256)
            ]
            quarters.append(jnp.concatenate(blocks, axis=1).astype(F32))
        ref[...] = jnp.concatenate(
            [
                quarters[group][:, place * piece : (place + 1) * piece]
                for place in range(tgts)
                for group in range(groups)
            ],
            axis=1,
        )


def place_units(parts, down_parts, sums):
    groups, tgts = lax.axis_size("mem"), lax.axis_size("tgt")
    rows, columns = parts.shape[1:]
    wide = jax.ShapeDtypeStruct((rows, groups * columns // 2), F32)
    down = jax.ShapeDtypeStruct((groups * down_parts.shape[1], down_parts.shape[2]), F32)
    shapes = (wide, wide, down) + tuple(jax.ShapeDtypeStruct(part.shape, F32) for part in sums)
    return pl.pallas_call(
        functools.partial(place_kernel, tgts, groups),
        out_shape=shapes,
        in_specs=[VMEM_SPEC] * (2 + len(sums)),
        out_specs=(VMEM_SPEC,) * len(shapes),
        compiler_params=pltpu.CompilerParams(vmem_limit_bytes=VMEM_CAP),
        name="place_units",
    )(parts, down_parts, *sums)


def share_kernel(src, out, sends, recvs, own_sem):
    mem = lax.axis_index("mem")
    greet("mem", (1, 2))
    near = jnp.bitwise_xor(mem, 1)
    far = jnp.bitwise_xor(mem, 2)
    to_far = peer_copy(src, out.at[mem], sends.at[0], recvs.at[0], mem=far)
    to_near = peer_copy(src, out.at[mem], sends.at[1], recvs.at[1], mem=near)
    pass_on = peer_copy(out.at[far], out.at[far], sends.at[2], recvs.at[2], mem=near)
    to_far.start()
    to_near.start()
    own = pltpu.make_async_copy(src, out.at[mem], own_sem)
    own.start()
    to_far.wait_recv()
    pass_on.start()
    to_near.wait_recv()
    pass_on.wait_recv()
    for copy in (to_far, to_near, pass_on):
        copy.wait_send()
    own.wait()


def share(value):
    groups = lax.axis_size("mem")
    return pl.pallas_call(
        share_kernel,
        out_shape=jax.ShapeDtypeStruct((groups,) + value.shape, BF),
        in_specs=[ANY_SPEC],
        out_specs=ANY_SPEC,
        scratch_shapes=[pltpu.SemaphoreType.DMA((3,))] * 2 + [pltpu.SemaphoreType.DMA],
        compiler_params=pltpu.CompilerParams(collective_id=6, has_side_effects=True),
        cost_estimate=pl.CostEstimate(
            flops=0, bytes_accessed=30 * 1024 * 1024, transcendentals=0
        ),
        name="share_sums",
    )(value)


def over_mem(value, offset):
    return lax.ppermute(value, "mem", [(i, i ^ offset) for i in range(4)])


def gather_mem(value):
    far = over_mem(value, 2)
    near = over_mem(value, 1)
    return value, near, far, over_mem(far, 1)


def gather_tgt(shard):
    return lax.all_gather(shard, "tgt", axis=0, tiled=True)


def scatter_tgt(partial):
    return lax.psum_scatter(partial, "tgt", scatter_dimension=0, tiled=True)


def in_tiles(value):
    rows, columns = value.shape
    value = jnp.pad(value, ((0, 0), (0, -columns % 128)))
    return value.reshape(rows // 8, 8, -1, 128).swapaxes(1, 2).reshape(-1, 8, 128)


def from_tiles(tiles, rows, columns):
    shards = tiles.shape[0]
    tiles = tiles.reshape(shards * rows // 8, -1, 8, 128).swapaxes(1, 2)
    return tiles.reshape(shards * rows, -1)[:, :columns]


def gather_units(gate_up, down):
    if gate_up.shape[0] % 8 or down.shape[0] % 8:
        return gather_tgt(gate_up), gather_tgt(down)
    tiles = in_tiles(gate_up)
    both = lax.all_gather(jnp.concatenate([tiles, in_tiles(down)]), "tgt", axis=0)
    return (
        from_tiles(both[:, : tiles.shape[0]], *gate_up.shape),
        from_tiles(both[:, tiles.shape[0] :], *down.shape),
    )


def attention_weights(weights):
    if lax.axis_size("tgt") == 8:
        return gather_weights(weights)
    parts = [lax.all_gather(weight, "tgt", axis=0) for weight in weights]
    return (
        jnp.concatenate(parts[:3], axis=-1),
        jnp.concatenate(parts[4:6], axis=-1),
        parts[3],
        parts[6],
        parts[7],
    )


def weight_sums(partials, small, units):
    if lax.axis_size("tgt") == 8:
        return reduce_weights(*partials, small, units)
    inner = HEADS * HEAD
    totals = [
        lax.psum_scatter(partial, "tgt", scatter_dimension=0, tiled=False) for partial in partials
    ]
    qkv, kv, cq, so, co = lax.psum(totals, "mem")
    return (
        qkv[:, :inner], qkv[:, inner : 2 * inner], qkv[:, 2 * inner :], cq,
        kv[:, :inner], kv[:, inner:], so, co, lax.psum(small, ("tgt", "mem")),
        lax.all_gather(units, "mem", axis=0),
    )


def on_device(
    target, memory, lengths, gate_bias, out_grad, gain_self, gain_cross, gain_ffn, rel_table,
    self_q, self_k, self_v, self_o, cross_q, cross_k, cross_v, cross_o, ffn_gate, ffn_up, ffn_down,
):
    groups = lax.axis_size("mem")
    tgts = lax.axis_size("tgt")
    mem_index = lax.axis_index("mem")
    items, seq, model = target.shape
    all_items, positions_dev, _ = memory.shape
    inner = HEADS * HEAD
    tokens = items * ROWS
    shard_in = ffn_gate.shape[0]
    hidden_shard = ffn_down.shape[0]
    piece = hidden_shard // groups
    quarter = tgts * piece

    def padded(value):
        return jnp.pad(value, ((0, 0), (0, ROWS - seq), (0, 0))).reshape(tokens, model)

    def trimmed(value):
        return value.reshape(items, ROWS, model)[:, :seq]

    norm_self = gain_self.astype(F32)
    norm_cross = gain_cross.astype(F32)
    norm_ffn = gain_ffn.astype(F32)
    onehot = jnp.asarray(distance_onehot())
    base = jnp.pad(
        lax.dot_general(rel_table, onehot, TN, precision=HIGH), ((0, 2), (0, 0))
    )
    positions = mem_index * positions_dev + jnp.arange(positions_dev)
    bias = jnp.where(positions[None, :] < lengths[:, None], gate_bias, NEG)[:, None, :]

    self_w, cross_kv_w, cross_q_w, self_o_w, cross_o_w = (
        weight.reshape(-1, weight.shape[-1])
        for weight in attention_weights(
            (self_q, self_k, self_v, cross_q, cross_k, cross_v, self_o, cross_o)
        )
    )
    gate_up = pick_units(ffn_gate, ffn_up)
    down = lax.dynamic_slice_in_dim(ffn_down, mem_index * piece, piece, axis=0)
    gate_up, down = gather_units(gate_up, down)

    inputs = padded(target).astype(F32)
    upstream_low = padded(out_grad)
    late, self_w = lax.optimization_barrier((upstream_low, self_w))
    upstreams = gather_mem(late)

    h1 = (inputs * rms_scale(inputs) * norm_self).astype(BF)
    qkv = dot(h1, self_w).astype(BF).reshape(items, ROWS, 3 * inner)
    att = self_fwd(qkv, base).reshape(tokens, inner)
    y1 = inputs + dot(att, self_o_w)
    h2 = (y1 * rms_scale(y1) * norm_cross).astype(BF)
    cq = dot(h2, cross_q_w).astype(BF).reshape(items, ROWS, inner)
    ckv = jnp.einsum(
        "npd,dc->npc", memory, cross_kv_w, preferred_element_type=F32
    ).astype(BF)
    all_queries, catt, lse = cross_fwd(cq, ckv, bias)
    catt = catt.reshape(tokens, inner)
    y2 = y1 + dot(catt, cross_o_w)
    h3 = (y2 * rms_scale(y2) * norm_ffn).astype(BF)

    h3_back, out_near, out_far, grad_gate_up, grad_down = ffn(h3, upstreams, gate_up, down, items)
    out_sum = over_mem(out_far, 2)
    grad_gate_up = scatter_tgt(grad_gate_up)
    dx, grad_norm_ffn = rms_back(y2, norm_ffn, h3_back)
    dy2 = upstream_low.astype(F32) + dx
    e2 = dy2.astype(BF)
    grad_cross_o = dot_tn(catt, e2).astype(BF)
    dcatt = dot_nt(e2, cross_o_w).astype(BF)
    delta = jnp.sum(
        (dcatt.astype(F32) * catt.astype(F32)).reshape(tokens, HEADS, HEAD), axis=-1
    ).reshape(items, ROWS, HEADS)
    stats = jnp.concatenate(
        [lse[:, :, :8], delta, jnp.zeros((items, ROWS, 8 - HEADS), F32)], axis=-1
    ).swapaxes(1, 2)
    dckv, dcq = cross_bwd(
        all_queries, dcatt.reshape(items, ROWS, inner), stats, ckv, bias
    )
    y2_late, grad_down, dcq = lax.optimization_barrier((y2, grad_down, dcq))
    grad_down = scatter_tgt(grad_down)
    layer_out = trimmed(
        (y2_late + out_near.astype(F32) + out_sum.astype(F32)).astype(BF)
    )
    dcq = dcq.reshape(tokens, inner)
    grad_cross_kv = jnp.einsum("npd,npc->dc", memory, dckv, preferred_element_type=F32)
    memory_grad = jnp.einsum(
        "npc,dc->npd", dckv, cross_kv_w, preferred_element_type=F32
    ).astype(BF)
    grad_cross_q = dot_tn(h2, dcq)
    dx, grad_norm_cross = rms_back(y1, norm_cross, dot_nt(dcq, cross_q_w))
    dy1 = dy2 + dx
    e1 = dy1.astype(BF)
    grad_self_o = dot_tn(att, e1).astype(BF)
    datt = dot_nt(e1, self_o_w).astype(BF).reshape(items, ROWS, inner)
    dqkv, diag = self_bwd(qkv, datt, base)
    dqkv = dqkv.reshape(tokens, 3 * inner)
    grad_self = dot_tn(h1, dqkv)
    dx, grad_norm_self = rms_back(inputs, norm_self, dot_nt(dqkv, self_w))
    target_grad = trimmed((dy1 + dx).astype(BF))
    table = lax.dot_general(
        onehot, diag[:HEADS], NT, precision=HIGH
    )

    small = jnp.concatenate(
        [grad_norm_self, grad_norm_cross, grad_norm_ffn, table.reshape(-1)]
    )
    *sums, small, grad_gate_up = weight_sums(
        tuple(
            partial.astype(BF).reshape(tgts, -1, partial.shape[-1])
            for partial in (grad_self, grad_cross_kv, grad_cross_q, grad_self_o, grad_cross_o)
        ),
        jnp.pad(small, (0, -small.size % 1024)).reshape(-1, 128),
        grad_gate_up,
    )
    grad_down, small = lax.optimization_barrier((grad_down, small))
    grad_down = share(grad_down)
    grad_gate, grad_up, grad_down, *columns = place_units(grad_gate_up, grad_down, sums)
    small = small.reshape(-1)
    norms = [small[start : start + model] for start in range(0, 3 * model, model)]
    table = small[3 * model : 3 * model + table.size].reshape(table.shape)
    return (
        layer_out,
        target_grad,
        memory_grad,
        *norms,
        table,
        columns[0],
        columns[1],
        columns[2],
        columns[6],
        columns[3],
        columns[4],
        columns[5],
        columns[7],
        grad_gate,
        grad_up,
        grad_down,
    )


def solution(mesh):
    owned = P(("tgt", "mem"), None, None)
    held = P("tgt", "mem", None)
    rows = P("tgt", None)
    return jax.shard_map(
        on_device,
        mesh=mesh,
        in_specs=(owned, held, P("tgt"), P("tgt", "mem"), owned, P(), P(), P(), P()) + (rows,) * 11,
        out_specs=(owned, owned, held, P(), P(), P(), P()) + (rows,) * 11,
        check_vma=False,
    )
```
